32 devices in a mesh: seq: 16 (over z, x, core), head: 2 (over y).
Axes of the slice: x: 2, y: 2, z: 4, core: 2. Of those that a mesh axis runs over, the one named last changes fastest.
Arguments:
- queries: bfloat16 [2048, 8, 1024], P(('seq', 'head')), may hold values from -256 to 256
- branch_key_value: bfloat16 [2048, 8, 256], P(('seq', 'head')), may hold values from -4 to 4
- branch_ids: int32 [2048], replicated, may hold values from 0 to 3, never falling along the last dimension, each value on 1 to 1024 neighbouring positions
- pool: bfloat16 [16, 16, 8, 256], P('seq', None, 'head'), may hold values from -4 to 4
- page_table: int32 [8, 8], P('head'), may hold values from 0 to 15, as said below
Outputs:
- attended: bfloat16 [2048, 8, 1024], P(('seq', 'head'))
The draws below stay inside these ranges and needn't reach their ends.
Inputs may be any that keep to these rules, and one draw needn't show every extreme that they name: `branch_ids`: never falls along the rows; each branch covers 1 to 1024 rows and one covers exactly 1024. `page_table`: row h holds 8 distinct page numbers.
All inputs are finite; a program needn't handle non-finite values.
Results may differ from the reference program's by a relative error of at most 0.0085.
Values may be sent and summed in bfloat16 or wider, within the bound.
A program may use at most 64 MiB of HBM per device.

```python
import math
import jax
import jax.numpy as jnp
import numpy as np
from jax import lax

KEY_VALUE_HEADS = 8
QUERY_GROUP = 8
HEAD_DIM = 128
PAGE_TOKENS = 16
BRANCH_TOKENS = 2048
BRANCH_MOST = 1024
BRANCHES = 4
POOL_PAGES = 16
LPAGES = 8


def shared_keys(key):
    return jnp.clip(jax.random.normal(key, (BRANCH_TOKENS, KEY_VALUE_HEADS, HEAD_DIM), jnp.float32), -4.0, 4.0)


def draw_branch_key_value(key, part):
    keys_part = shared_keys(key)
    key = jax.random.fold_in(key, 11)
    value_rows = jnp.clip(jax.random.normal(key, (BRANCH_TOKENS, KEY_VALUE_HEADS, HEAD_DIM), jnp.float32), -4.0, 4.0)
    return jnp.concatenate([keys_part, value_rows], axis=2).astype(jnp.bfloat16)


def draw_queries(key, part):
    key = jax.random.fold_in(key, 12)
    base_offset = jnp.clip(jax.random.normal(key, (BRANCH_TOKENS, KEY_VALUE_HEADS, QUERY_GROUP * HEAD_DIM), jnp.float32), -4.0, 4.0)
    return base_offset.astype(jnp.bfloat16)


def draw_page_table(key, part):
    key = jax.random.fold_in(key, 13)

    def single_head(head_index):
        sub_key = jax.random.fold_in(key, head_index)
        chosen = jax.random.permutation(sub_key, POOL_PAGES)[:LPAGES].astype(jnp.int32)
        inner = (jax.random.permutation(sub_key, POOL_PAGES - 2)[:LPAGES - 2] + 1).astype(jnp.int32)
        pinned = jnp.concatenate([jnp.array([0, POOL_PAGES - 1], jnp.int32), inner])
        return jnp.where(head_index == 0, pinned, chosen)
    return jax.vmap(single_head)(jnp.arange(KEY_VALUE_HEADS, dtype=jnp.int32))


def block_levels(own_key, shape, shards, low, top_value):
    gain = 1.0
    for dim, parts in shards:
        heights = jax.random.uniform(jax.random.fold_in(jax.random.fold_in(own_key, 6), dim), (parts,), jnp.float32, low / len(shards), top_value / len(shards))
        gain = gain * jnp.repeat(jnp.exp(heights), shape[dim] // parts).reshape((-1,) + (1,) * (len(shape) - 1 - dim))
    return gain


def split_up(amount, total, most, lean):
    weights = [(1 << 20) // math.isqrt(standing ** lean) + 1 for standing in range(2, amount + 1)]
    spare, holding = total - most - (amount - 1), [1] * (amount - 1)
    while spare > 0:
        free = [i for i in range(amount - 1) if holding[i] < most]
        whole, remaining = sum([weights[i] for i in free]), spare
        for i in free:
            addition = min(most - holding[i], max(1, remaining * weights[i] // whole), spare)
            holding[i] = holding[i] + addition
            spare = spare - addition
    return np.array([most] + holding)


def ragged(own_key, amount, total, limit, skew):
    if amount == 2:
        one = jax.random.randint(own_key, (), max(1, total - limit), min(limit, total - 1) + 1)
        return jnp.stack([one, total - one])
    tallies = jnp.asarray(split_up(amount, total, limit, skew), jnp.int32)
    pairs = (amount - 1) // 2
    source_of, taker = tallies[1:1 + 2 * pairs:2], tallies[2:2 + 2 * pairs:2]
    room = jnp.minimum(source_of - 1, limit - taker)
    passed = jax.random.randint(jax.random.fold_in(own_key, 1), (pairs,), 0, 1 << 20) % (room + 1)
    tallies = tallies.at[1:1 + 2 * pairs:2].set(source_of - passed).at[2:2 + 2 * pairs:2].set(taker + passed)
    return tallies[jax.random.permutation(jax.random.fold_in(own_key, 2), amount)]


def bell_draw(key, shape, spread, most, cuts=(), kind=jnp.bfloat16):
    result = jax.random.normal(key, shape, jnp.float32) * spread
    if len(cuts) > 0:
        result = block_levels(key, shape, cuts, -0.22, 0.18) * result
    return jnp.clip(result, min=-most, max=most).astype(kind)


def setup_inputs(seed: int = 0) -> dict:
    key_of = jax.random.split(jax.random.key(seed), 6)
    return {
        "queries": draw_queries(jax.random.fold_in(key_of[5], 71), 0),
        "branch_key_value": draw_branch_key_value(jax.random.fold_in(key_of[5], 71), 0),
        "branch_ids": jnp.searchsorted(jnp.cumsum(ragged(key_of[2], BRANCHES, BRANCH_TOKENS, BRANCH_MOST, 2)), jnp.arange(BRANCH_TOKENS), side="right").astype(jnp.int32),
        "pool": bell_draw(key_of[3], (POOL_PAGES, PAGE_TOKENS, KEY_VALUE_HEADS, 2 * HEAD_DIM), 1.0, 4.0, ((0, 16), (2, 2))),
        "page_table": draw_page_table(jax.random.fold_in(key_of[5], 71), 0),
    }


def reference(queries, branch_key_value, branch_ids, pool, page_table):
    scale = HEAD_DIM ** -0.5
    block_rows = math.gcd(BRANCH_TOKENS, 512)
    block_count = BRANCH_TOKENS // block_rows
    reach_limit = BRANCH_MOST
    padded_key_value = jnp.concatenate([jnp.zeros((reach_limit, KEY_VALUE_HEADS, 2 * HEAD_DIM), branch_key_value.dtype), branch_key_value], axis=0)
    padded_ids = jnp.concatenate([jnp.full((reach_limit,), -1, jnp.int32), branch_ids.astype(jnp.int32)], axis=0)
    row_offsets = jnp.arange(block_rows, dtype=jnp.int32)
    window_offsets = jnp.arange(reach_limit + block_rows, dtype=jnp.int32)

    def single_head(head_index):
        table = lax.dynamic_index_in_dim(page_table, head_index, 0, keepdims=False)
        pool_head = lax.dynamic_index_in_dim(pool, head_index, 2, keepdims=False)
        prefix_pairs = jnp.take(pool_head, table, axis=0).reshape(LPAGES * PAGE_TOKENS, 2 * HEAD_DIM)
        head_queries = lax.dynamic_index_in_dim(queries, head_index, 1, keepdims=False)
        head_kv = lax.dynamic_index_in_dim(padded_key_value, head_index, 1, keepdims=False)

        def one_block(block_index):
            start = (block_index * block_rows).astype(jnp.int32)
            query = lax.dynamic_slice_in_dim(head_queries, start, block_rows, 0)
            query = query.astype(jnp.float32).reshape(block_rows, QUERY_GROUP, HEAD_DIM)
            window = lax.dynamic_slice_in_dim(head_kv, start, reach_limit + block_rows, 0)
            window_ids = lax.dynamic_slice_in_dim(padded_ids, start, reach_limit + block_rows, 0)
            own_ids = lax.dynamic_slice_in_dim(branch_ids.astype(jnp.int32), start, block_rows, 0)
            query_rows = start + row_offsets
            key_rows = start - reach_limit + window_offsets
            allowed = (window_ids[None, :] == own_ids[:, None]) & (key_rows[None, :] <= query_rows[:, None])
            keys = jnp.concatenate([prefix_pairs[:, :HEAD_DIM], window[:, :HEAD_DIM]], axis=0).astype(jnp.float32)
            value_rows = jnp.concatenate([prefix_pairs[:, HEAD_DIM:], window[:, HEAD_DIM:]], axis=0).astype(jnp.float32)
            mask = jnp.concatenate([jnp.ones((block_rows, LPAGES * PAGE_TOKENS), bool), allowed], axis=1)
            scores = jnp.einsum("rgd,kd->rgk", query, keys) * scale
            scores = jnp.where(mask[:, None, :], scores, -jnp.inf)
            top = jnp.max(scores, axis=-1, keepdims=True)
            weights = jnp.exp(scores - top)
            total = jnp.sum(weights, axis=-1, keepdims=True)
            rounded = lax.optimization_barrier(weights.astype(jnp.bfloat16)).astype(jnp.float32)
            mixed = jnp.einsum("rgk,kd->rgd", rounded, value_rows) / total
            return mixed.astype(jnp.bfloat16).reshape(block_rows, QUERY_GROUP * HEAD_DIM)

        blocks = lax.map(one_block, jnp.arange(block_count, dtype=jnp.int32))
        return blocks.reshape(BRANCH_TOKENS, QUERY_GROUP * HEAD_DIM)

    attention_output = lax.map(single_head, jnp.arange(KEY_VALUE_HEADS, dtype=jnp.int32))
    return jnp.transpose(attention_output, (1, 0, 2))
```

```python
import functools

import jax
import jax.numpy as jnp
from jax import lax
from jax.experimental import pallas as pl
from jax.experimental.pallas import tpu as pltpu
from jax.sharding import PartitionSpec as P

HEAD_DIM = 128
MESH = pl.DeviceIdType.MESH

def passed_along(value, axis, by):
    count = lax.axis_size(axis)
    pairs = [(i, i + by) for i in range(count) if 0 <= i + by < count]
    return lax.ppermute(value, axis, pairs)


def blend_keys(state, query, pairs, allowed, scale):
    top, total, summed = state
    width = query.shape[-1]
    keys = pairs[..., :width]
    value_rows = pairs[..., width:]
    scores = jnp.einsum("rhgd,khd->rhgk", query, keys, preferred_element_type=jnp.float32) * scale
    scores = jnp.where(allowed, scores, -jnp.inf)
    new_top = jnp.maximum(top, jnp.max(scores, axis=-1))
    factor = jnp.exp(top - new_top)
    weights = jnp.exp(scores - new_top[..., None])
    total = total * factor + jnp.sum(weights, axis=-1)
    rounded = weights.astype(jnp.bfloat16)
    summed = summed * factor[..., None] + jnp.einsum(
        "rhgk,khd->rhgd", rounded, value_rows, preferred_element_type=jnp.float32
    )
    return (new_top, total, summed)


def per_device(queries, branch_key_value, branch_ids, pool, page_table):
    reach_count = min(32, lax.axis_size("seq") // 2)
    query, pairs = (
        lax.all_to_all(queries, "head", split_axis=1, concat_axis=0, tiled=True),
        lax.all_to_all(branch_key_value, "head", split_axis=1, concat_axis=0, tiled=True),
    )
    rows = query.shape[0]
    local_heads = query.shape[1]
    group = query.shape[2] // HEAD_DIM
    query = query.reshape(rows, local_heads, group, HEAD_DIM)
    scale = HEAD_DIM ** (-0.5)
    row_start = lax.axis_index("seq") * rows
    row_ids = jnp.arange(rows, dtype=jnp.int32)
    own_ids = lax.dynamic_slice_in_dim(branch_ids, row_start, rows, 0)
    own_rows = row_start + row_ids
    state = (
        jnp.full((rows, local_heads, group), -1e30, jnp.float32),
        jnp.zeros((rows, local_heads, group), jnp.float32),
        jnp.zeros((rows, local_heads, group, HEAD_DIM), jnp.float32),
    )
    page_rows = pool.shape[1]
    pair_width = pool.shape[3]
    piece = lax.all_gather(pool, "seq", axis=0, tiled=True)
    count = piece.shape[0]
    page_ids = jnp.arange(count, dtype=jnp.int32)
    chosen = jnp.any(page_table[:, :, None] == page_ids[None, None, :], axis=1)
    allowed = jnp.broadcast_to(chosen[:, :, None], (local_heads, count, page_rows))
    allowed = allowed.reshape(local_heads, count * page_rows)
    flat = piece.reshape(count * page_rows, local_heads, pair_width)

    def fold_in_piece(inner):
        return blend_keys(inner, query, flat, allowed[None, :, None, :], scale)

    def keep_state(inner):
        return inner

    state = lax.cond(jnp.any(chosen), fold_in_piece, keep_state, state)

    def causal_step(carry, block, back):
        key_start = row_start - back * rows
        key_ids = lax.dynamic_slice_in_dim(branch_ids, jnp.maximum(key_start, 0), rows, 0)
        key_rows = key_start + row_ids
        allowed = (
            (key_ids[None, :] == own_ids[:, None])
            & (key_rows[None, :] <= own_rows[:, None])
            & (key_start >= 0)
        )
        return blend_keys(carry, query, block, allowed[:, None, None, :], scale)

    state = causal_step(state, pairs, 0)
    for back in range(1, reach_count + 1):
        earlier = passed_along(pairs, "seq", back)
        state = causal_step(state, earlier, back)
    top, total, summed = state
    mixed = (
        (summed / total[..., None])
        .astype(jnp.bfloat16)
        .reshape(rows, local_heads, group * HEAD_DIM)
    )
    return lax.all_to_all(mixed, "head", split_axis=0, concat_axis=1, tiled=True)


PLANES = 4
PLANE_BLOCKS = 8
PIECES = 4
KZ, KX, KY, KD, KSZ, KSX, KSY, KSD = range(8)


def relay_kernel(
    listed,
    query_ref, pairs_ref, start_ref, pool_ref, table_ref, out_ref,
    window, prefix, tables, bias, pool_bias,
    send_sem, recv_sem, pool_send, pool_recv,
):
    heads, rows, width = pairs_ref.shape
    page_rows = pool_ref.shape[1]
    piece = heads // PIECES
    seq = lax.axis_index("seq")
    y = lax.axis_index("head")
    z, x, c = seq // 4, (seq // 2) % 2, seq % 2
    place = x * 4 + c * 2 + y

    def device(dz=0, dx=0, dc=0, dy=0):
        nx = 1 - x if dx else x
        nc = 1 - c if dc else c
        ny = 1 - y if dy else y
        return (((z + dz) * 2 + nx) * 2 + nc, ny)

    up, down = device(dz=1), device(dz=-1)
    xn, yn, sib = device(dx=1), device(dy=1), device(dc=1)

    barrier = pltpu.get_barrier_semaphore()
    for other in (xn, yn, sib):
        pl.semaphore_signal(barrier, inc=1, device_id=other, device_id_type=MESH)

    @pl.when(z < PLANES - 1)
    def _():
        pl.semaphore_signal(barrier, inc=1, device_id=up, device_id_type=MESH)

    @pl.when(z > 0)
    def _():
        pl.semaphore_signal(barrier, inc=1, device_id=down, device_id_type=MESH)

    def block_at(k, bx, bc, by):
        return (2 - k) * PLANE_BLOCKS + bx * 4 + bc * 2 + by

    window[:, pl.ds(block_at(0, x, c, y), 1)] = pairs_ref[...][:, None]
    half = heads // 2
    own_page = pl.ds(pl.multiple_of(((c * PLANES + z) * 2 + x) * page_rows, page_rows), page_rows)
    prefix[pl.ds(y * half, half), own_page, :] = pool_ref[...]
    tables[pl.ds(y, 1)] = table_ref[...][None]

    pl.semaphore_wait(
        barrier, 3 + jnp.where(z < PLANES - 1, 1, 0) + jnp.where(z > 0, 1, 0)
    )

    def message(kind, k, j, k_from, bx, bc, by, target):
        part = pl.ds(j * piece, piece)
        return pltpu.make_async_remote_copy(
            src_ref=window.at[part, block_at(k_from, bx, bc, by)],
            dst_ref=window.at[part, block_at(k, bx, bc, by)],
            send_sem=send_sem.at[kind, k, j],
            recv_sem=recv_sem.at[kind, k, j],
            device_id=target,
            device_id_type=MESH,
        )

    source = {
        KZ: (x, c, y), KX: (x, c, y), KY: (x, c, y),
        KSZ: (x, c, y), KSX: (1 - x, c, y), KSY: (x, c, 1 - y), KSD: (1 - x, c, 1 - y),
    }
    landing = {
        KZ: (x, c, y), KX: (1 - x, c, y), KY: (x, c, 1 - y), KD: (1 - x, c, 1 - y),
        KSZ: (x, 1 - c, y), KSX: (1 - x, 1 - c, y),
        KSY: (x, 1 - c, 1 - y), KSD: (1 - x, 1 - c, 1 - y),
    }
    targets = {KZ: up, KX: xn, KY: yn, KSZ: sib, KSX: sib, KSY: sib, KSD: sib}

    def x_first(j):
        return j < PIECES // 2

    def outgoing(kind, k, j):
        return message(kind, k, j, k - 1 if kind == KZ else k, *source[kind], targets[kind])

    def corner_out(k, j, by_y):
        where, target = ((1 - x, c, y), yn) if by_y else ((x, c, 1 - y), xn)
        return message(KD, k, j, k, *where, target)

    def present(k):
        return z >= k

    def takes_x(k):
        if k == 0:
            return x == 1
        return present(k) if k == 1 else present(k) & (x == 0)

    def gives_x(k):
        if k == 0:
            return x == 0
        return present(k) if k == 1 else present(k) & (x == 1)

    def sends(kind, k):
        if kind == KZ:
            return (z < PLANES - 1) & (z >= k - 1)
        if kind == KX:
            return gives_x(k)
        if kind in (KY, KSZ, KSY):
            return present(k)
        return takes_x(k)

    def receives(kind, k):
        if kind in (KX, KD, KSX, KSD):
            return takes_x(k)
        return present(k)

    def corner_sends(k, j, by_y):
        return takes_x(k) & x_first(j) if by_y else gives_x(k) & jnp.logical_not(x_first(j))

    started = []

    def start(kind, k, j):
        started.append((kind, k))

        @pl.when(sends(kind, k))
        def _():
            outgoing(kind, k, j).start()

    def corner_start(k, j, by_y):
        @pl.when(corner_sends(k, j, by_y))
        def _():
            corner_out(k, j, by_y).start()

    def for_pieces(body):
        lax.fori_loop(0, PIECES, lambda j, carry: (body(j), carry)[1], 0)

    def arrived(kind, k, j):
        @pl.when(receives(kind, k))
        def _():
            message(kind, k, j, k, *landing[kind], sib).wait_recv()

    def pool_message(index, src, target):
        return pltpu.make_async_remote_copy(
            src_ref=src, dst_ref=src,
            send_sem=pool_send.at[index], recv_sem=pool_recv.at[index],
            device_id=target, device_id_type=MESH,
        )

    def layer_at(plane, layer):
        return prefix.at[
            :, pl.ds(pl.multiple_of((layer * PLANES + plane) * 2 * page_rows, 2 * page_rows), 2 * page_rows), :
        ]

    table_out = pool_message(0, tables.at[pl.ds(y, 1)], yn)
    table_in = pool_message(0, tables.at[pl.ds(1 - y, 1)], yn)
    py_out = pool_message(1, prefix.at[pl.ds(y * half, half), own_page, :], yn)
    py_in = pool_message(1, prefix.at[pl.ds((1 - y) * half, half), own_page, :], yn)
    x_page = pl.ds(pl.multiple_of(((c * PLANES + z) * 2 + 1 - x) * page_rows, page_rows), page_rows)
    px_out = pool_message(2, prefix.at[:, own_page, :], xn)
    px_in = pool_message(2, prefix.at[:, x_page, :], xn)
    UP, DOWN, SIB_UP, SIB_DOWN, SIB_OWN = 3, 6, 9, 12, 15

    def from_below(d):
        return z >= d

    def from_above(d):
        return z + d < PLANES

    def up_out(d):
        return pool_message(UP + d - 1, layer_at(z - d + 1, c), up)

    def down_out(d):
        return pool_message(DOWN + d - 1, layer_at(z + d - 1, c), down)

    def up_sends(d):
        return (z < PLANES - 1) & (z >= d - 1)

    def down_sends(d):
        return (z > 0) & (z + d - 1 < PLANES)

    def pool_start(d):
        @pl.when(up_sends(d))
        def _():
            up_out(d).start()

        @pl.when(down_sends(d))
        def _():
            down_out(d).start()

    def pool_arrived(d):
        @pl.when(from_below(d))
        def _():
            pool_message(UP + d - 1, layer_at(z - d, c), up).wait_recv()
            pool_message(SIB_UP + d - 1, layer_at(z - d, c), sib).start()

        @pl.when(from_above(d))
        def _():
            pool_message(DOWN + d - 1, layer_at(z + d, c), up).wait_recv()
            pool_message(SIB_DOWN + d - 1, layer_at(z + d, c), sib).start()

        if d < PLANES - 1:
            pool_start(d + 1)

    py_out.start()
    table_out.start()

    @for_pieces
    def _(j):
        for kind, k in ((KZ, 1), (KX, 0), (KY, 0), (KSZ, 0)):
            start(kind, k, j)

    plane_rows = PLANE_BLOCKS * rows

    @pl.when(z < 2)
    def _():
        window[:, :PLANE_BLOCKS] = jnp.zeros((heads, PLANE_BLOCKS, rows, width), window.dtype)

    @pl.when(z < 1)
    def _():
        window[:, PLANE_BLOCKS:2 * PLANE_BLOCKS] = jnp.zeros((heads, PLANE_BLOCKS, rows, width), window.dtype)

    span = bias.shape[1]
    column = lax.broadcasted_iota(jnp.int32, (rows, span), 1)
    row = lax.broadcasted_iota(jnp.int32, (rows, span), 0)
    base = (z * PLANE_BLOCKS + place) * rows - 2 * plane_rows
    seen = (column >= start_ref[...] - base) & (column <= row + 2 * plane_rows)
    bias[...] = jnp.where(seen, 0.0, -1e30)

    py_in.wait_recv()
    px_out.start()

    @for_pieces
    def _(j):
        arrived(KZ, 1, j)
        for kind, k in ((KZ, 2), (KX, 1), (KY, 1), (KSZ, 1)):
            start(kind, k, j)

    px_in.wait_recv()
    pool_start(1)
    pool_message(SIB_OWN, layer_at(z, c), sib).start()

    def cross(k, j):
        arrived(KX, k, j)
        corner_start(k, j, True)
        start(KSX, k, j)
        arrived(KY, k, j)
        corner_start(k, j, False)
        start(KSY, k, j)

    def corner(k, j):
        arrived(KD, k, j)
        start(KSD, k, j)

    @for_pieces
    def _(j):
        cross(0, j)

    @for_pieces
    def _(j):
        arrived(KZ, 2, j)
        for kind, k in ((KX, 2), (KY, 2), (KSZ, 2)):
            start(kind, k, j)

    pool_arrived(1)

    @for_pieces
    def _(j):
        cross(1, j)
        corner(0, j)

    pool_arrived(2)

    @for_pieces
    def _(j):
        cross(2, j)
        corner(1, j)

    pool_arrived(3)

    @for_pieces
    def _(j):
        corner(2, j)

    table_in.wait_recv()
    pages = PLANES * 4
    keys = pages * page_rows
    slot = lax.broadcasted_iota(jnp.int32, (8, keys), 1) // page_rows
    page = (slot % (pages // 2)) * 2 + slot // (pages // 2)
    for side in range(2):
        table = tables[side]
        chosen = table[:, 0:1] == page
        for i in range(1, listed):
            chosen = chosen | (table[:, i:i + 1] == page)
        mask = jnp.where(chosen, 0.0, -1e30)
        for i in range(half):
            pool_bias[side * half + i] = mask[i:i + 1]

    for d in range(1, PLANES):
        @pl.when(from_below(d))
        def _():
            pool_message(SIB_UP + d - 1, layer_at(z - d, 1 - c), sib).wait_recv()

        @pl.when(from_above(d))
        def _():
            pool_message(SIB_DOWN + d - 1, layer_at(z + d, 1 - c), sib).wait_recv()
    pool_message(SIB_OWN, layer_at(z, 1 - c), sib).wait_recv()

    @for_pieces
    def _(j):
        for k in range(3):
            for kind in (KSZ, KSX, KSY, KSD):
                arrived(kind, k, j)

    factor = HEAD_DIM ** (-0.5) * 1.4426950408889634
    group = query_ref.shape[2] // HEAD_DIM
    ones = jnp.ones((span, HEAD_DIM), jnp.bfloat16)
    pool_ones = jnp.ones((keys, HEAD_DIM), jnp.bfloat16)
    contract = (((1,), (1,)), ((), ()))

    def one_head(h, carry):
        queries = query_ref[h]
        query = jnp.concatenate(
            [queries[:, g * HEAD_DIM:(g + 1) * HEAD_DIM] for g in range(group)], axis=0
        )
        near = window[h, pl.ds(place, 2 * PLANE_BLOCKS + 1)].reshape(span, width)
        far = prefix[h]
        near_scores = lax.dot_general(
            query, near[:, :HEAD_DIM], contract, preferred_element_type=jnp.float32
        )
        near_scores = (near_scores.reshape(group, rows, span) + bias[...][None]).reshape(group * rows, span)
        far_scores = lax.dot_general(
            query, far[:, :HEAD_DIM], contract, preferred_element_type=jnp.float32
        )
        far_scores = far_scores + pool_bias[h]
        top = jnp.maximum(
            jnp.max(near_scores, axis=1, keepdims=True), jnp.max(far_scores, axis=1, keepdims=True)
        )
        near_weights = jnp.exp2((near_scores - top) * factor).astype(jnp.bfloat16)
        far_weights = jnp.exp2((far_scores - top) * factor).astype(jnp.bfloat16)
        mixed = jnp.dot(
            near_weights,
            jnp.concatenate([near[:, HEAD_DIM:], ones], axis=1),
            preferred_element_type=jnp.float32,
        ) + jnp.dot(
            far_weights,
            jnp.concatenate([far[:, HEAD_DIM:], pool_ones], axis=1),
            preferred_element_type=jnp.float32,
        )
        result = (mixed[:, :HEAD_DIM] / mixed[:, HEAD_DIM:]).astype(out_ref.dtype)
        for g in range(group):
            out_ref[h, :, g * HEAD_DIM:(g + 1) * HEAD_DIM] = result[g * rows:(g + 1) * rows]
        return carry

    lax.fori_loop(0, heads, one_head, 0)

    @for_pieces
    def _(j):
        for kind, k in started:
            @pl.when(sends(kind, k))
            def _():
                outgoing(kind, k, j).wait_send()

        for k in range(3):
            for by_y in (True, False):
                @pl.when(corner_sends(k, j, by_y))
                def _():
                    corner_out(k, j, by_y).wait_send()

    table_out.wait_send()
    py_out.wait_send()
    px_out.wait_send()
    pool_message(SIB_OWN, layer_at(z, c), sib).wait_send()
    for d in range(1, PLANES):
        @pl.when(up_sends(d))
        def _():
            up_out(d).wait_send()

        @pl.when(down_sends(d))
        def _():
            down_out(d).wait_send()

        @pl.when(from_below(d))
        def _():
            pool_message(SIB_UP + d - 1, layer_at(z - d, c), sib).wait_send()

        @pl.when(from_above(d))
        def _():
            pool_message(SIB_DOWN + d - 1, layer_at(z + d, c), sib).wait_send()


def relayed(queries, branch_key_value, branch_ids, pool, page_table):
    rows, heads, width = branch_key_value.shape
    wide = queries.shape[2]
    page_rows = pool.shape[1]
    block = lax.axis_index("seq") * 2 + lax.axis_index("head")
    own_ids = lax.dynamic_slice_in_dim(branch_ids, block * rows, rows, 0)
    starts = jnp.sum((branch_ids[None, :] < own_ids[:, None]).astype(jnp.int32), axis=1, keepdims=True)
    table = jnp.pad(page_table, ((0, 8 - page_table.shape[0]), (0, 128 - page_table.shape[1])))
    span = 2 * PLANE_BLOCKS * rows + rows
    pool_keys = PLANES * 4 * page_rows
    vmem = pl.BlockSpec(memory_space=pltpu.VMEM)
    attended = pl.pallas_call(
        functools.partial(relay_kernel, page_table.shape[1]),
        out_shape=jax.ShapeDtypeStruct((heads, rows, wide), jnp.bfloat16),
        in_specs=[vmem] * 5,
        out_specs=vmem,
        scratch_shapes=[
            pltpu.VMEM((heads, 3 * PLANE_BLOCKS, rows, width), jnp.bfloat16),
            pltpu.VMEM((heads, pool_keys, width), jnp.bfloat16),
            pltpu.VMEM((2, 8, 128), jnp.int32),
            pltpu.VMEM((rows, span), jnp.float32),
            pltpu.VMEM((heads, 1, pool_keys), jnp.float32),
            pltpu.SemaphoreType.DMA((8, 3, PIECES)),
            pltpu.SemaphoreType.DMA((8, 3, PIECES)),
            pltpu.SemaphoreType.DMA((16,)),
            pltpu.SemaphoreType.DMA((16,)),
        ],
        compiler_params=pltpu.CompilerParams(
            collective_id=0, has_side_effects=True, vmem_limit_bytes=48 * 2**20
        ),
        cost_estimate=pl.CostEstimate(
            flops=4 * rows * wide * (span + pool_keys) * heads,
            bytes_accessed=2 * 2 * heads * rows * wide,
            transcendentals=rows * heads * (wide // HEAD_DIM) * (span + pool_keys),
        ),
    )(
        jnp.swapaxes(queries, 0, 1),
        jnp.swapaxes(branch_key_value, 0, 1),
        starts,
        jnp.swapaxes(pool[0], 0, 1),
        table,
    )
    return jnp.swapaxes(attended, 0, 1)


def solution(mesh):
    small = mesh.shape["seq"] == PLANES * 4 and mesh.shape["head"] == 2
    return jax.shard_map(
        relayed if small else per_device,
        mesh=mesh,
        in_specs=(
            P(("seq", "head"), None, None),
            P(("seq", "head"), None, None),
            P(),
            P("seq", None, "head", None),
            P("head", None),
        ),
        out_specs=P(("seq", "head"), None, None),
        check_vma=False,
    )
```

```python
import functools

import jax
import jax.numpy as jnp
from jax import lax
from jax.experimental import pallas as pl
from jax.experimental.pallas import tpu as pltpu
from jax.sharding import PartitionSpec as P

HEAD_DIM = 128
MESH = pl.DeviceIdType.MESH

def passed_along(value, axis, by):
    count = lax.axis_size(axis)
    pairs = [(i, i + by) for i in range(count) if 0 <= i + by < count]
    return lax.ppermute(value, axis, pairs)


def blend_keys(state, query, pairs, allowed, scale):
    top, total, summed = state
    width = query.shape[-1]
    keys = pairs[..., :width]
    value_rows = pairs[..., width:]
    scores = jnp.einsum("rhgd,khd->rhgk", query, keys, preferred_element_type=jnp.float32) * scale
    scores = jnp.where(allowed, scores, -jnp.inf)
    new_top = jnp.maximum(top, jnp.max(scores, axis=-1))
    factor = jnp.exp(top - new_top)
    weights = jnp.exp(scores - new_top[..., None])
    total = total * factor + jnp.sum(weights, axis=-1)
    rounded = weights.astype(jnp.bfloat16)
    summed = summed * factor[..., None] + jnp.einsum(
        "rhgk,khd->rhgd", rounded, value_rows, preferred_element_type=jnp.float32
    )
    return (new_top, total, summed)


def per_device(queries, branch_key_value, branch_ids, pool, page_table):
    reach_count = min(32, lax.axis_size("seq") // 2)
    query, pairs = (
        lax.all_to_all(queries, "head", split_axis=1, concat_axis=0, tiled=True),
        lax.all_to_all(branch_key_value, "head", split_axis=1, concat_axis=0, tiled=True),
    )
    rows = query.shape[0]
    local_heads = query.shape[1]
    group = query.shape[2] // HEAD_DIM
    query = query.reshape(rows, local_heads, group, HEAD_DIM)
    scale = HEAD_DIM ** (-0.5)
    row_start = lax.axis_index("seq") * rows
    row_ids = jnp.arange(rows, dtype=jnp.int32)
    own_ids = lax.dynamic_slice_in_dim(branch_ids, row_start, rows, 0)
    own_rows = row_start + row_ids
    state = (
        jnp.full((rows, local_heads, group), -1e30, jnp.float32),
        jnp.zeros((rows, local_heads, group), jnp.float32),
        jnp.zeros((rows, local_heads, group, HEAD_DIM), jnp.float32),
    )
    page_rows = pool.shape[1]
    pair_width = pool.shape[3]
    piece = lax.all_gather(pool, "seq", axis=0, tiled=True)
    count = piece.shape[0]
    page_ids = jnp.arange(count, dtype=jnp.int32)
    chosen = jnp.any(page_table[:, :, None] == page_ids[None, None, :], axis=1)
    allowed = jnp.broadcast_to(chosen[:, :, None], (local_heads, count, page_rows))
    allowed = allowed.reshape(local_heads, count * page_rows)
    flat = piece.reshape(count * page_rows, local_heads, pair_width)

    def fold_in_piece(inner):
        return blend_keys(inner, query, flat, allowed[None, :, None, :], scale)

    def keep_state(inner):
        return inner

    state = lax.cond(jnp.any(chosen), fold_in_piece, keep_state, state)

    def causal_step(carry, block, back):
        key_start = row_start - back * rows
        key_ids = lax.dynamic_slice_in_dim(branch_ids, jnp.maximum(key_start, 0), rows, 0)
        key_rows = key_start + row_ids
        allowed = (
            (key_ids[None, :] == own_ids[:, None])
            & (key_rows[None, :] <= own_rows[:, None])
            & (key_start >= 0)
        )
        return blend_keys(carry, query, block, allowed[:, None, None, :], scale)

    state = causal_step(state, pairs, 0)
    for back in range(1, reach_count + 1):
        earlier = passed_along(pairs, "seq", back)
        state = causal_step(state, earlier, back)
    top, total, summed = state
    mixed = (
        (summed / total[..., None])
        .astype(jnp.bfloat16)
        .reshape(rows, local_heads, group * HEAD_DIM)
    )
    return lax.all_to_all(mixed, "head", split_axis=0, concat_axis=1, tiled=True)


PLANES = 4
PLANE_BLOCKS = 8
PIECES = 4
KZ, KX, KY, KD, KSZ, KSX, KSY, KSD = range(8)


def relay_kernel(
    listed,
    query_ref, pairs_ref, start_ref, pool_ref, table_ref, out_ref,
    window, prefix, tables, bias, pool_bias, mixed, tops,
    send_sem, recv_sem, pool_send, pool_recv,
):
    heads, rows, width = pairs_ref.shape
    page_rows = pool_ref.shape[1]
    piece = heads // PIECES
    seq = lax.axis_index("seq")
    y = lax.axis_index("head")
    z, x, c = seq // 4, (seq // 2) % 2, seq % 2
    place = x * 4 + c * 2 + y

    def device(dz=0, dx=0, dc=0, dy=0):
        nx = 1 - x if dx else x
        nc = 1 - c if dc else c
        ny = 1 - y if dy else y
        return (((z + dz) * 2 + nx) * 2 + nc, ny)

    up, down = device(dz=1), device(dz=-1)
    xn, yn, sib = device(dx=1), device(dy=1), device(dc=1)

    barrier = pltpu.get_barrier_semaphore()
    for other in (xn, yn, sib):
        pl.semaphore_signal(barrier, inc=1, device_id=other, device_id_type=MESH)

    @pl.when(z < PLANES - 1)
    def _():
        pl.semaphore_signal(barrier, inc=1, device_id=up, device_id_type=MESH)

    @pl.when(z > 0)
    def _():
        pl.semaphore_signal(barrier, inc=1, device_id=down, device_id_type=MESH)

    def block_at(k, bx, bc, by):
        return (2 - k) * PLANE_BLOCKS + bx * 4 + bc * 2 + by

    window[:, pl.ds(block_at(0, x, c, y), 1)] = pairs_ref[...][:, None]
    half = heads // 2
    own_page = pl.ds(pl.multiple_of(((c * PLANES + z) * 2 + x) * page_rows, page_rows), page_rows)
    prefix[pl.ds(y * half, half), own_page, :] = pool_ref[...]
    tables[pl.ds(y, 1)] = table_ref[...][None]

    pl.semaphore_wait(
        barrier, 3 + jnp.where(z < PLANES - 1, 1, 0) + jnp.where(z > 0, 1, 0)
    )

    def message(kind, k, j, k_from, bx, bc, by, target):
        part = pl.ds(j * piece, piece)
        return pltpu.make_async_remote_copy(
            src_ref=window.at[part, block_at(k_from, bx, bc, by)],
            dst_ref=window.at[part, block_at(k, bx, bc, by)],
            send_sem=send_sem.at[kind, k, j],
            recv_sem=recv_sem.at[kind, k, j],
            device_id=target,
            device_id_type=MESH,
        )

    source = {
        KZ: (x, c, y), KX: (x, c, y), KY: (x, c, y),
        KSZ: (x, c, y), KSX: (1 - x, c, y), KSY: (x, c, 1 - y), KSD: (1 - x, c, 1 - y),
    }
    landing = {
        KZ: (x, c, y), KX: (1 - x, c, y), KY: (x, c, 1 - y), KD: (1 - x, c, 1 - y),
        KSZ: (x, 1 - c, y), KSX: (1 - x, 1 - c, y),
        KSY: (x, 1 - c, 1 - y), KSD: (1 - x, 1 - c, 1 - y),
    }
    targets = {KZ: up, KX: xn, KY: yn, KSZ: sib, KSX: sib, KSY: sib, KSD: sib}

    def x_first(j):
        return j < PIECES // 2

    def outgoing(kind, k, j):
        return message(kind, k, j, k - 1 if kind == KZ else k, *source[kind], targets[kind])

    def corner_out(k, j, by_y):
        where, target = ((1 - x, c, y), yn) if by_y else ((x, c, 1 - y), xn)
        return message(KD, k, j, k, *where, target)

    def present(k):
        return z >= k

    def takes_x(k):
        if k == 0:
            return x == 1
        return present(k) if k == 1 else present(k) & (x == 0)

    def gives_x(k):
        if k == 0:
            return x == 0
        return present(k) if k == 1 else present(k) & (x == 1)

    def sends(kind, k):
        if kind == KZ:
            return (z < PLANES - 1) & (z >= k - 1)
        if kind == KX:
            return gives_x(k)
        if kind in (KY, KSZ, KSY):
            return present(k)
        return takes_x(k)

    def receives(kind, k):
        if kind in (KX, KD, KSX, KSD):
            return takes_x(k)
        return present(k)

    def corner_sends(k, j, by_y):
        return takes_x(k) & x_first(j) if by_y else gives_x(k) & jnp.logical_not(x_first(j))

    started = []

    def start(kind, k, j):
        started.append((kind, k))

        @pl.when(sends(kind, k))
        def _():
            outgoing(kind, k, j).start()

    def corner_start(k, j, by_y):
        @pl.when(corner_sends(k, j, by_y))
        def _():
            corner_out(k, j, by_y).start()

    def for_pieces(body):
        lax.fori_loop(0, PIECES, lambda j, carry: (body(j), carry)[1], 0)

    def arrived(kind, k, j):
        @pl.when(receives(kind, k))
        def _():
            message(kind, k, j, k, *landing[kind], sib).wait_recv()

    def pool_message(index, src, target):
        return pltpu.make_async_remote_copy(
            src_ref=src, dst_ref=src,
            send_sem=pool_send.at[index], recv_sem=pool_recv.at[index],
            device_id=target, device_id_type=MESH,
        )

    def layer_at(plane, layer):
        return prefix.at[
            :, pl.ds(pl.multiple_of((layer * PLANES + plane) * 2 * page_rows, 2 * page_rows), 2 * page_rows), :
        ]

    table_out = pool_message(0, tables.at[pl.ds(y, 1)], yn)
    table_in = pool_message(0, tables.at[pl.ds(1 - y, 1)], yn)
    py_out = pool_message(1, prefix.at[pl.ds(y * half, half), own_page, :], yn)
    py_in = pool_message(1, prefix.at[pl.ds((1 - y) * half, half), own_page, :], yn)
    x_page = pl.ds(pl.multiple_of(((c * PLANES + z) * 2 + 1 - x) * page_rows, page_rows), page_rows)
    px_out = pool_message(2, prefix.at[:, own_page, :], xn)
    px_in = pool_message(2, prefix.at[:, x_page, :], xn)
    UP, DOWN, SIB_UP, SIB_DOWN, SIB_OWN = 3, 6, 9, 12, 15

    def from_below(d):
        return z >= d

    def from_above(d):
        return z + d < PLANES

    def up_out(d):
        return pool_message(UP + d - 1, layer_at(z - d + 1, c), up)

    def down_out(d):
        return pool_message(DOWN + d - 1, layer_at(z + d - 1, c), down)

    def up_sends(d):
        return (z < PLANES - 1) & (z >= d - 1)

    def down_sends(d):
        return (z > 0) & (z + d - 1 < PLANES)

    def pool_start(d):
        @pl.when(up_sends(d))
        def _():
            up_out(d).start()

        @pl.when(down_sends(d))
        def _():
            down_out(d).start()

    def pool_arrived(d):
        @pl.when(from_below(d))
        def _():
            pool_message(UP + d - 1, layer_at(z - d, c), up).wait_recv()
            pool_message(SIB_UP + d - 1, layer_at(z - d, c), sib).start()

        @pl.when(from_above(d))
        def _():
            pool_message(DOWN + d - 1, layer_at(z + d, c), up).wait_recv()
            pool_message(SIB_DOWN + d - 1, layer_at(z + d, c), sib).start()

        if d < PLANES - 1:
            pool_start(d + 1)

    py_out.start()
    table_out.start()

    @for_pieces
    def _(j):
        for kind, k in ((KZ, 1), (KX, 0), (KY, 0), (KSZ, 0)):
            start(kind, k, j)

    plane_rows = PLANE_BLOCKS * rows

    @pl.when(z < 2)
    def _():
        window[:, :PLANE_BLOCKS] = jnp.zeros((heads, PLANE_BLOCKS, rows, width), window.dtype)

    @pl.when(z < 1)
    def _():
        window[:, PLANE_BLOCKS:2 * PLANE_BLOCKS] = jnp.zeros((heads, PLANE_BLOCKS, rows, width), window.dtype)

    span = bias.shape[1]
    column = lax.broadcasted_iota(jnp.int32, (rows, span), 1)
    row = lax.broadcasted_iota(jnp.int32, (rows, span), 0)
    base = (z * PLANE_BLOCKS + place) * rows - 2 * plane_rows
    seen = (column >= start_ref[...] - base) & (column <= row + 2 * plane_rows)
    bias[...] = jnp.where(seen, 0.0, -1e30)

    py_in.wait_recv()
    px_out.start()

    @for_pieces
    def _(j):
        arrived(KZ, 1, j)
        for kind, k in ((KZ, 2), (KX, 1), (KY, 1), (KSZ, 1)):
            start(kind, k, j)

    px_in.wait_recv()
    pool_start(1)
    pool_message(SIB_OWN, layer_at(z, c), sib).start()

    def cross(k, j):
        arrived(KX, k, j)
        corner_start(k, j, True)
        start(KSX, k, j)
        arrived(KY, k, j)
        corner_start(k, j, False)
        start(KSY, k, j)

    def corner(k, j):
        arrived(KD, k, j)
        start(KSD, k, j)

    @for_pieces
    def _(j):
        cross(0, j)

    @for_pieces
    def _(j):
        arrived(KZ, 2, j)
        for kind, k in ((KX, 2), (KY, 2), (KSZ, 2)):
            start(kind, k, j)

    pool_arrived(1)

    @for_pieces
    def _(j):
        cross(1, j)
        corner(0, j)

    pool_arrived(2)

    @for_pieces
    def _(j):
        corner(1, j)

    pool_arrived(3)

    table_in.wait_recv()
    pages = PLANES * 4
    keys = pages * page_rows
    slot = lax.broadcasted_iota(jnp.int32, (8, keys), 1) // page_rows
    page = (slot % (pages // 2)) * 2 + slot // (pages // 2)
    for side in range(2):
        table = tables[side]
        chosen = table[:, 0:1] == page
        for i in range(1, listed):
            chosen = chosen | (table[:, i:i + 1] == page)
        mask = jnp.where(chosen, 0.0, -1e30)
        for i in range(half):
            pool_bias[side * half + i] = mask[i:i + 1]

    for d in range(1, PLANES):
        @pl.when(from_below(d))
        def _():
            pool_message(SIB_UP + d - 1, layer_at(z - d, 1 - c), sib).wait_recv()

        @pl.when(from_above(d))
        def _():
            pool_message(SIB_DOWN + d - 1, layer_at(z + d, 1 - c), sib).wait_recv()
    pool_message(SIB_OWN, layer_at(z, 1 - c), sib).wait_recv()

    factor = HEAD_DIM ** (-0.5) * 1.4426950408889634
    group = query_ref.shape[2] // HEAD_DIM
    far_span = PLANE_BLOCKS * rows
    near_span = span - far_span
    contract = (((1,), (1,)), ((), ()))

    def stacked_queries(h):
        queries = query_ref[h]
        return jnp.concatenate(
            [queries[:, g * HEAD_DIM:(g + 1) * HEAD_DIM] for g in range(group)], axis=0
        )

    def scores_of(query, pairs, mask):
        scores = lax.dot_general(
            query, pairs[:, :HEAD_DIM], contract, preferred_element_type=jnp.float32
        )
        count = pairs.shape[0]
        return (scores.reshape(group, rows, count) + mask[None]).reshape(group * rows, count)

    def weighted(scores, top, pairs):
        weights = jnp.exp2((scores - top) * factor).astype(jnp.bfloat16)
        values = jnp.concatenate(
            [pairs[:, HEAD_DIM:], jnp.ones((pairs.shape[0], HEAD_DIM), jnp.bfloat16)], axis=1
        )
        return jnp.dot(weights, values, preferred_element_type=jnp.float32)

    def early(h):
        query = stacked_queries(h)
        near = window[h, pl.ds(place + PLANE_BLOCKS, PLANE_BLOCKS + 1)].reshape(near_span, width)
        pool_pairs = prefix[h]
        near_scores = scores_of(query, near, bias[:, far_span:])
        pool_scores = scores_of(query, pool_pairs, pool_bias[h])
        top = jnp.maximum(
            jnp.max(near_scores, axis=1, keepdims=True), jnp.max(pool_scores, axis=1, keepdims=True)
        )
        mixed[h] = weighted(near_scores, top, near) + weighted(pool_scores, top, pool_pairs)
        tops[h] = jnp.broadcast_to(top, tops.shape[1:])

    def late(h):
        query = stacked_queries(h)
        far = window[h, pl.ds(place, PLANE_BLOCKS)].reshape(far_span, width)
        scores = scores_of(query, far, bias[:, :far_span])
        before = tops[h][:, :1]
        top = jnp.maximum(before, jnp.max(scores, axis=1, keepdims=True))
        total = mixed[h] * jnp.exp2((before - top) * factor) + weighted(scores, top, far)
        result = (total[:, :HEAD_DIM] / total[:, HEAD_DIM:]).astype(out_ref.dtype)
        for g in range(group):
            out_ref[h, :, g * HEAD_DIM:(g + 1) * HEAD_DIM] = result[g * rows:(g + 1) * rows]

    def for_heads(j, body):
        lax.fori_loop(0, piece, lambda i, carry: (body(j * piece + i), carry)[1], 0)

    def from_sibling(k, j):
        for kind in (KSZ, KSX, KSY, KSD):
            arrived(kind, k, j)

    @for_pieces
    def _(j):
        cross(2, j)
        from_sibling(0, j)
        from_sibling(1, j)
        for_heads(j, early)

    @for_pieces
    def _(j):
        corner(2, j)

    @for_pieces
    def _(j):
        from_sibling(2, j)
        for_heads(j, late)

    @for_pieces
    def _(j):
        for kind, k in started:
            @pl.when(sends(kind, k))
            def _():
                outgoing(kind, k, j).wait_send()

        for k in range(3):
            for by_y in (True, False):
                @pl.when(corner_sends(k, j, by_y))
                def _():
                    corner_out(k, j, by_y).wait_send()

    table_out.wait_send()
    py_out.wait_send()
    px_out.wait_send()
    pool_message(SIB_OWN, layer_at(z, c), sib).wait_send()
    for d in range(1, PLANES):
        @pl.when(up_sends(d))
        def _():
            up_out(d).wait_send()

        @pl.when(down_sends(d))
        def _():
            down_out(d).wait_send()

        @pl.when(from_below(d))
        def _():
            pool_message(SIB_UP + d - 1, layer_at(z - d, c), sib).wait_send()

        @pl.when(from_above(d))
        def _():
            pool_message(SIB_DOWN + d - 1, layer_at(z + d, c), sib).wait_send()


def relayed(queries, branch_key_value, branch_ids, pool, page_table):
    rows, heads, width = branch_key_value.shape
    wide = queries.shape[2]
    page_rows = pool.shape[1]
    block = lax.axis_index("seq") * 2 + lax.axis_index("head")
    own_ids = lax.dynamic_slice_in_dim(branch_ids, block * rows, rows, 0)
    starts = jnp.sum((branch_ids[None, :] < own_ids[:, None]).astype(jnp.int32), axis=1, keepdims=True)
    table = jnp.pad(page_table, ((0, 8 - page_table.shape[0]), (0, 128 - page_table.shape[1])))
    span = 2 * PLANE_BLOCKS * rows + rows
    pool_keys = PLANES * 4 * page_rows
    vmem = pl.BlockSpec(memory_space=pltpu.VMEM)
    attended = pl.pallas_call(
        functools.partial(relay_kernel, page_table.shape[1]),
        out_shape=jax.ShapeDtypeStruct((heads, rows, wide), jnp.bfloat16),
        in_specs=[vmem] * 5,
        out_specs=vmem,
        scratch_shapes=[
            pltpu.VMEM((heads, 3 * PLANE_BLOCKS, rows, width), jnp.bfloat16),
            pltpu.VMEM((heads, pool_keys, width), jnp.bfloat16),
            pltpu.VMEM((2, 8, 128), jnp.int32),
            pltpu.VMEM((rows, span), jnp.float32),
            pltpu.VMEM((heads, 1, pool_keys), jnp.float32),
            pltpu.VMEM((heads, rows * (wide // HEAD_DIM), 2 * HEAD_DIM), jnp.float32),
            pltpu.VMEM((heads, rows * (wide // HEAD_DIM), HEAD_DIM), jnp.float32),
            pltpu.SemaphoreType.DMA((8, 3, PIECES)),
            pltpu.SemaphoreType.DMA((8, 3, PIECES)),
            pltpu.SemaphoreType.DMA((16,)),
            pltpu.SemaphoreType.DMA((16,)),
        ],
        compiler_params=pltpu.CompilerParams(
            collective_id=0, has_side_effects=True, vmem_limit_bytes=48 * 2**20
        ),
        cost_estimate=pl.CostEstimate(
            flops=4 * rows * wide * (span + pool_keys) * heads,
            bytes_accessed=2 * 2 * heads * rows * wide,
            transcendentals=rows * heads * (wide // HEAD_DIM) * (span + pool_keys),
        ),
    )(
        jnp.swapaxes(queries, 0, 1),
        jnp.swapaxes(branch_key_value, 0, 1),
        starts,
        jnp.swapaxes(pool[0], 0, 1),
        table,
    )
    return jnp.swapaxes(attended, 0, 1)


def solution(mesh):
    small = mesh.shape["seq"] == PLANES * 4 and mesh.shape["head"] == 2
    return jax.shard_map(
        relayed if small else per_device,
        mesh=mesh,
        in_specs=(
            P(("seq", "head"), None, None),
            P(("seq", "head"), None, None),
            P(),
            P("seq", None, "head", None),
            P("head", None),
        ),
        out_specs=P(("seq", "head"), None, None),
        check_vma=False,
    )
```

```python
import functools

import jax
import jax.numpy as jnp
from jax import lax
from jax.experimental import pallas as pl
from jax.experimental.pallas import tpu as pltpu
from jax.sharding import PartitionSpec as P

HEAD_DIM = 128
MESH = pl.DeviceIdType.MESH

def passed_along(value, axis, by):
    count = lax.axis_size(axis)
    pairs = [(i, i + by) for i in range(count) if 0 <= i + by < count]
    return lax.ppermute(value, axis, pairs)


def blend_keys(state, query, pairs, allowed, scale):
    top, total, summed = state
    width = query.shape[-1]
    keys = pairs[..., :width]
    value_rows = pairs[..., width:]
    scores = jnp.einsum("rhgd,khd->rhgk", query, keys, preferred_element_type=jnp.float32) * scale
    scores = jnp.where(allowed, scores, -jnp.inf)
    new_top = jnp.maximum(top, jnp.max(scores, axis=-1))
    factor = jnp.exp(top - new_top)
    weights = jnp.exp(scores - new_top[..., None])
    total = total * factor + jnp.sum(weights, axis=-1)
    rounded = weights.astype(jnp.bfloat16)
    summed = summed * factor[..., None] + jnp.einsum(
        "rhgk,khd->rhgd", rounded, value_rows, preferred_element_type=jnp.float32
    )
    return (new_top, total, summed)


def per_device(queries, branch_key_value, branch_ids, pool, page_table):
    reach_count = min(32, lax.axis_size("seq") // 2)
    query, pairs = (
        lax.all_to_all(queries, "head", split_axis=1, concat_axis=0, tiled=True),
        lax.all_to_all(branch_key_value, "head", split_axis=1, concat_axis=0, tiled=True),
    )
    rows = query.shape[0]
    local_heads = query.shape[1]
    group = query.shape[2] // HEAD_DIM
    query = query.reshape(rows, local_heads, group, HEAD_DIM)
    scale = HEAD_DIM ** (-0.5)
    row_start = lax.axis_index("seq") * rows
    row_ids = jnp.arange(rows, dtype=jnp.int32)
    own_ids = lax.dynamic_slice_in_dim(branch_ids, row_start, rows, 0)
    own_rows = row_start + row_ids
    state = (
        jnp.full((rows, local_heads, group), -1e30, jnp.float32),
        jnp.zeros((rows, local_heads, group), jnp.float32),
        jnp.zeros((rows, local_heads, group, HEAD_DIM), jnp.float32),
    )
    page_rows = pool.shape[1]
    pair_width = pool.shape[3]
    piece = lax.all_gather(pool, "seq", axis=0, tiled=True)
    count = piece.shape[0]
    page_ids = jnp.arange(count, dtype=jnp.int32)
    chosen = jnp.any(page_table[:, :, None] == page_ids[None, None, :], axis=1)
    allowed = jnp.broadcast_to(chosen[:, :, None], (local_heads, count, page_rows))
    allowed = allowed.reshape(local_heads, count * page_rows)
    flat = piece.reshape(count * page_rows, local_heads, pair_width)

    def fold_in_piece(inner):
        return blend_keys(inner, query, flat, allowed[None, :, None, :], scale)

    def keep_state(inner):
        return inner

    state = lax.cond(jnp.any(chosen), fold_in_piece, keep_state, state)

    def causal_step(carry, block, back):
        key_start = row_start - back * rows
        key_ids = lax.dynamic_slice_in_dim(branch_ids, jnp.maximum(key_start, 0), rows, 0)
        key_rows = key_start + row_ids
        allowed = (
            (key_ids[None, :] == own_ids[:, None])
            & (key_rows[None, :] <= own_rows[:, None])
            & (key_start >= 0)
        )
        return blend_keys(carry, query, block, allowed[:, None, None, :], scale)

    state = causal_step(state, pairs, 0)
    for back in range(1, reach_count + 1):
        earlier = passed_along(pairs, "seq", back)
        state = causal_step(state, earlier, back)
    top, total, summed = state
    mixed = (
        (summed / total[..., None])
        .astype(jnp.bfloat16)
        .reshape(rows, local_heads, group * HEAD_DIM)
    )
    return lax.all_to_all(mixed, "head", split_axis=0, concat_axis=1, tiled=True)


PLANES = 4
PLANE_BLOCKS = 8
CHUNK = 16
PIECES = 4
KZ, KX, KY, KD, KSZ, KSX, KSY, KSD = range(8)


def relay_kernel(
    listed,
    query_ref, pairs_ref, start_ref, pool_ref, table_ref, out_ref,
    window, prefix, tables, bias, pool_bias, scores, weights, mixed, tops,
    send_sem, recv_sem, pool_send, pool_recv,
):
    heads, rows, width = pairs_ref.shape
    page_rows = pool_ref.shape[1]
    piece = heads // PIECES
    seq = lax.axis_index("seq")
    y = lax.axis_index("head")
    z, x, c = seq // 4, (seq // 2) % 2, seq % 2
    place = x * 4 + c * 2 + y

    def device(dz=0, dx=0, dc=0, dy=0):
        nx = 1 - x if dx else x
        nc = 1 - c if dc else c
        ny = 1 - y if dy else y
        return (((z + dz) * 2 + nx) * 2 + nc, ny)

    up, down = device(dz=1), device(dz=-1)
    xn, yn, sib = device(dx=1), device(dy=1), device(dc=1)

    barrier = pltpu.get_barrier_semaphore()
    for other in (xn, yn, sib):
        pl.semaphore_signal(barrier, inc=1, device_id=other, device_id_type=MESH)

    @pl.when(z < PLANES - 1)
    def _():
        pl.semaphore_signal(barrier, inc=1, device_id=up, device_id_type=MESH)

    @pl.when(z > 0)
    def _():
        pl.semaphore_signal(barrier, inc=1, device_id=down, device_id_type=MESH)

    def block_at(k, bx, bc, by):
        return (2 - k) * PLANE_BLOCKS + bx * 4 + bc * 2 + by

    window[:, pl.ds(block_at(0, x, c, y), 1)] = pairs_ref[...][:, None]
    half = heads // 2
    own_page = pl.ds(pl.multiple_of(((c * PLANES + z) * 2 + x) * page_rows, page_rows), page_rows)
    prefix[pl.ds(y * half, half), own_page, :] = pool_ref[...]
    tables[pl.ds(y, 1)] = table_ref[...][None]

    pl.semaphore_wait(
        barrier, 3 + jnp.where(z < PLANES - 1, 1, 0) + jnp.where(z > 0, 1, 0)
    )

    def message(kind, k, j, k_from, bx, bc, by, target):
        part = pl.ds(j * piece, piece)
        return pltpu.make_async_remote_copy(
            src_ref=window.at[part, block_at(k_from, bx, bc, by)],
            dst_ref=window.at[part, block_at(k, bx, bc, by)],
            send_sem=send_sem.at[kind, k, j],
            recv_sem=recv_sem.at[kind, k, j],
            device_id=target,
            device_id_type=MESH,
        )

    source = {
        KZ: (x, c, y), KX: (x, c, y), KY: (x, c, y),
        KSZ: (x, c, y), KSX: (1 - x, c, y), KSY: (x, c, 1 - y), KSD: (1 - x, c, 1 - y),
    }
    landing = {
        KZ: (x, c, y), KX: (1 - x, c, y), KY: (x, c, 1 - y), KD: (1 - x, c, 1 - y),
        KSZ: (x, 1 - c, y), KSX: (1 - x, 1 - c, y),
        KSY: (x, 1 - c, 1 - y), KSD: (1 - x, 1 - c, 1 - y),
    }
    targets = {KZ: up, KX: xn, KY: yn, KSZ: sib, KSX: sib, KSY: sib, KSD: sib}

    def x_first(j):
        return j < PIECES // 2

    def outgoing(kind, k, j):
        return message(kind, k, j, k - 1 if kind == KZ else k, *source[kind], targets[kind])

    def corner_out(k, j, by_y):
        where, target = ((1 - x, c, y), yn) if by_y else ((x, c, 1 - y), xn)
        return message(KD, k, j, k, *where, target)

    def present(k):
        return z >= k

    def takes_x(k):
        if k == 0:
            return x == 1
        return present(k) if k == 1 else present(k) & (x == 0)

    def gives_x(k):
        if k == 0:
            return x == 0
        return present(k) if k == 1 else present(k) & (x == 1)

    def sends(kind, k):
        if kind == KZ:
            return (z < PLANES - 1) & (z >= k - 1)
        if kind == KX:
            return gives_x(k)
        if kind in (KY, KSZ, KSY):
            return present(k)
        return takes_x(k)

    def receives(kind, k):
        if kind in (KX, KD, KSX, KSD):
            return takes_x(k)
        return present(k)

    def corner_sends(k, j, by_y):
        return takes_x(k) & x_first(j) if by_y else gives_x(k) & jnp.logical_not(x_first(j))

    started = []

    def start(kind, k, j):
        started.append((kind, k))

        @pl.when(sends(kind, k))
        def _():
            outgoing(kind, k, j).start()

    def corner_start(k, j, by_y):
        @pl.when(corner_sends(k, j, by_y))
        def _():
            corner_out(k, j, by_y).start()

    def for_pieces(body):
        lax.fori_loop(0, PIECES, lambda j, carry: (body(j), carry)[1], 0)

    def arrived(kind, k, j):
        @pl.when(receives(kind, k))
        def _():
            message(kind, k, j, k, *landing[kind], sib).wait_recv()

    def pool_message(index, src, target):
        return pltpu.make_async_remote_copy(
            src_ref=src, dst_ref=src,
            send_sem=pool_send.at[index], recv_sem=pool_recv.at[index],
            device_id=target, device_id_type=MESH,
        )

    def layer_at(plane, layer):
        return prefix.at[
            :, pl.ds(pl.multiple_of((layer * PLANES + plane) * 2 * page_rows, 2 * page_rows), 2 * page_rows), :
        ]

    table_out = pool_message(0, tables.at[pl.ds(y, 1)], yn)
    table_in = pool_message(0, tables.at[pl.ds(1 - y, 1)], yn)
    py_out = pool_message(1, prefix.at[pl.ds(y * half, half), own_page, :], yn)
    py_in = pool_message(1, prefix.at[pl.ds((1 - y) * half, half), own_page, :], yn)
    x_page = pl.ds(pl.multiple_of(((c * PLANES + z) * 2 + 1 - x) * page_rows, page_rows), page_rows)
    px_out = pool_message(2, prefix.at[:, own_page, :], xn)
    px_in = pool_message(2, prefix.at[:, x_page, :], xn)
    UP, DOWN, SIB_UP, SIB_DOWN, SIB_OWN = 3, 6, 9, 12, 15

    def from_below(d):
        return z >= d

    def from_above(d):
        return z + d < PLANES

    def up_out(d):
        return pool_message(UP + d - 1, layer_at(z - d + 1, c), up)

    def down_out(d):
        return pool_message(DOWN + d - 1, layer_at(z + d - 1, c), down)

    def up_sends(d):
        return (z < PLANES - 1) & (z >= d - 1)

    def down_sends(d):
        return (z > 0) & (z + d - 1 < PLANES)

    def pool_start(d):
        @pl.when(up_sends(d))
        def _():
            up_out(d).start()

        @pl.when(down_sends(d))
        def _():
            down_out(d).start()

    def pool_arrived(d):
        @pl.when(from_below(d))
        def _():
            pool_message(UP + d - 1, layer_at(z - d, c), up).wait_recv()
            pool_message(SIB_UP + d - 1, layer_at(z - d, c), sib).start()

        @pl.when(from_above(d))
        def _():
            pool_message(DOWN + d - 1, layer_at(z + d, c), up).wait_recv()
            pool_message(SIB_DOWN + d - 1, layer_at(z + d, c), sib).start()

        if d < PLANES - 1:
            pool_start(d + 1)

    py_out.start()
    table_out.start()

    @for_pieces
    def _(j):
        for kind, k in ((KZ, 1), (KX, 0), (KY, 0), (KSZ, 0)):
            start(kind, k, j)

    plane_rows = PLANE_BLOCKS * rows

    @pl.when(z < 2)
    def _():
        window[:, :PLANE_BLOCKS] = jnp.zeros((heads, PLANE_BLOCKS, rows, width), window.dtype)

    @pl.when(z < 1)
    def _():
        window[:, PLANE_BLOCKS:2 * PLANE_BLOCKS] = jnp.zeros((heads, PLANE_BLOCKS, rows, width), window.dtype)

    span = bias.shape[1]
    column = lax.broadcasted_iota(jnp.int32, (rows, span), 1)
    row = lax.broadcasted_iota(jnp.int32, (rows, span), 0)
    base = (z * PLANE_BLOCKS + place) * rows - 2 * plane_rows
    seen = (column >= start_ref[...] - base) & (column <= row + 2 * plane_rows)
    bias[...] = jnp.where(seen, 0.0, -1e30)

    py_in.wait_recv()
    px_out.start()

    @for_pieces
    def _(j):
        arrived(KZ, 1, j)
        for kind, k in ((KZ, 2), (KX, 1), (KY, 1), (KSZ, 1)):
            start(kind, k, j)

    px_in.wait_recv()
    pool_start(1)
    pool_message(SIB_OWN, layer_at(z, c), sib).start()

    def cross(k, j):
        arrived(KX, k, j)
        corner_start(k, j, True)
        start(KSX, k, j)
        arrived(KY, k, j)
        corner_start(k, j, False)
        start(KSY, k, j)

    def corner(k, j):
        arrived(KD, k, j)
        start(KSD, k, j)

    @for_pieces
    def _(j):
        cross(0, j)

    @for_pieces
    def _(j):
        arrived(KZ, 2, j)
        for kind, k in ((KX, 2), (KY, 2), (KSZ, 2)):
            start(kind, k, j)

    pool_arrived(1)

    @for_pieces
    def _(j):
        cross(1, j)
        corner(0, j)

    pool_arrived(2)

    @for_pieces
    def _(j):
        corner(1, j)

    pool_arrived(3)

    table_in.wait_recv()
    pages = PLANES * 4
    keys = pages * page_rows
    slot = lax.broadcasted_iota(jnp.int32, (8, keys), 1) // page_rows
    page = (slot % (pages // 2)) * 2 + slot // (pages // 2)
    for side in range(2):
        table = tables[side]
        chosen = table[:, 0:1] == page
        for i in range(1, listed):
            chosen = chosen | (table[:, i:i + 1] == page)
        mask = jnp.where(chosen, 0.0, -1e30)
        for i in range(half):
            pool_bias[side * half + i] = mask[i:i + 1]

    for d in range(1, PLANES):
        @pl.when(from_below(d))
        def _():
            pool_message(SIB_UP + d - 1, layer_at(z - d, 1 - c), sib).wait_recv()

        @pl.when(from_above(d))
        def _():
            pool_message(SIB_DOWN + d - 1, layer_at(z + d, 1 - c), sib).wait_recv()
    pool_message(SIB_OWN, layer_at(z, 1 - c), sib).wait_recv()

    factor = HEAD_DIM ** (-0.5) * 1.4426950408889634
    group = query_ref.shape[2] // HEAD_DIM
    far_span = PLANE_BLOCKS * rows
    near_span = span - far_span
    contract = (((1,), (1,)), ((), ()))

    def stacked_queries(h):
        queries = query_ref[h]
        return jnp.concatenate(
            [queries[:, g * HEAD_DIM:(g + 1) * HEAD_DIM] for g in range(group)], axis=0
        )

    def score(query, pairs):
        scores[:, :pairs.shape[0]] = lax.dot_general(
            query, pairs[:, :HEAD_DIM], contract, preferred_element_type=jnp.float32
        )

    def weighted(pairs):
        count = pairs.shape[0]
        values = jnp.concatenate(
            [pairs[:, HEAD_DIM:], jnp.ones((count, HEAD_DIM), jnp.bfloat16)], axis=1
        )
        return jnp.dot(weights[:, :count], values, preferred_element_type=jnp.float32)

    def chunks():
        for r in range(0, rows, CHUNK):
            for g in range(group):
                yield pl.ds(r, CHUNK), pl.ds(g * rows + r, CHUNK)

    def early(h):
        near = window[h, pl.ds(place + PLANE_BLOCKS, PLANE_BLOCKS + 1)].reshape(near_span, width)
        pairs = jnp.concatenate([prefix[h], near], axis=0)
        score(stacked_queries(h), pairs)
        count = keys + near_span
        for mask_rows, own in chunks():
            pool_scores = scores[own, :keys] + pool_bias[h]
            near_scores = scores[own, keys:count] + bias[mask_rows, far_span:]
            top = factor * jnp.maximum(
                jnp.max(pool_scores, axis=1, keepdims=True), jnp.max(near_scores, axis=1, keepdims=True)
            )
            weights[own, :keys] = jnp.exp2(pool_scores * factor - top).astype(jnp.bfloat16)
            weights[own, keys:count] = jnp.exp2(near_scores * factor - top).astype(jnp.bfloat16)
            tops[h, own] = jnp.broadcast_to(top, (CHUNK, HEAD_DIM))
        mixed[h] = weighted(pairs)

    def late(h):
        far = window[h, pl.ds(place, PLANE_BLOCKS)].reshape(far_span, width)
        score(stacked_queries(h), far)
        for mask_rows, own in chunks():
            far_scores = scores[own, :far_span] + bias[mask_rows, :far_span]
            before = tops[h, own]
            top = jnp.maximum(before, factor * jnp.max(far_scores, axis=1, keepdims=True))
            weights[own, :far_span] = jnp.exp2(far_scores * factor - top[:, :1]).astype(jnp.bfloat16)
            tops[h, own] = jnp.exp2(before - top)
        part = weighted(far)
        shrink = tops[h]
        value_sum = mixed[h, :, :HEAD_DIM] * shrink + part[:, :HEAD_DIM]
        total = mixed[h, :, HEAD_DIM:] * shrink + part[:, HEAD_DIM:]
        result = (value_sum / total).astype(out_ref.dtype)
        for g in range(group):
            out_ref[h, :, g * HEAD_DIM:(g + 1) * HEAD_DIM] = result[g * rows:(g + 1) * rows]

    def for_heads(j, body):
        lax.fori_loop(0, piece, lambda i, carry: (body(j * piece + i), carry)[1], 0)

    def from_sibling(k, j):
        for kind in (KSZ, KSX, KSY, KSD):
            arrived(kind, k, j)

    @for_pieces
    def _(j):
        cross(2, j)
        from_sibling(0, j)
        from_sibling(1, j)
        for_heads(j, early)

    @for_pieces
    def _(j):
        corner(2, j)

    @for_pieces
    def _(j):
        from_sibling(2, j)
        for_heads(j, late)

    @for_pieces
    def _(j):
        for kind, k in started:
            @pl.when(sends(kind, k))
            def _():
                outgoing(kind, k, j).wait_send()

        for k in range(3):
            for by_y in (True, False):
                @pl.when(corner_sends(k, j, by_y))
                def _():
                    corner_out(k, j, by_y).wait_send()

    table_out.wait_send()
    py_out.wait_send()
    px_out.wait_send()
    pool_message(SIB_OWN, layer_at(z, c), sib).wait_send()
    for d in range(1, PLANES):
        @pl.when(up_sends(d))
        def _():
            up_out(d).wait_send()

        @pl.when(down_sends(d))
        def _():
            down_out(d).wait_send()

        @pl.when(from_below(d))
        def _():
            pool_message(SIB_UP + d - 1, layer_at(z - d, c), sib).wait_send()

        @pl.when(from_above(d))
        def _():
            pool_message(SIB_DOWN + d - 1, layer_at(z + d, c), sib).wait_send()


def relayed(queries, branch_key_value, branch_ids, pool, page_table):
    rows, heads, width = branch_key_value.shape
    wide = queries.shape[2]
    page_rows = pool.shape[1]
    block = lax.axis_index("seq") * 2 + lax.axis_index("head")
    own_ids = lax.dynamic_slice_in_dim(branch_ids, block * rows, rows, 0)
    starts = jnp.sum((branch_ids[None, :] < own_ids[:, None]).astype(jnp.int32), axis=1, keepdims=True)
    table = jnp.pad(page_table, ((0, 8 - page_table.shape[0]), (0, 128 - page_table.shape[1])))
    span = 2 * PLANE_BLOCKS * rows + rows
    pool_keys = PLANES * 4 * page_rows
    vmem = pl.BlockSpec(memory_space=pltpu.VMEM)
    attended = pl.pallas_call(
        functools.partial(relay_kernel, page_table.shape[1]),
        out_shape=jax.ShapeDtypeStruct((heads, rows, wide), jnp.bfloat16),
        in_specs=[vmem] * 5,
        out_specs=vmem,
        scratch_shapes=[
            pltpu.VMEM((heads, 3 * PLANE_BLOCKS, rows, width), jnp.bfloat16),
            pltpu.VMEM((heads, pool_keys, width), jnp.bfloat16),
            pltpu.VMEM((2, 8, 128), jnp.int32),
            pltpu.VMEM((rows, span), jnp.float32),
            pltpu.VMEM((heads, 1, pool_keys), jnp.float32),
            pltpu.VMEM((rows * (wide // HEAD_DIM), pool_keys + (PLANE_BLOCKS + 1) * rows), jnp.float32),
            pltpu.VMEM((rows * (wide // HEAD_DIM), pool_keys + (PLANE_BLOCKS + 1) * rows), jnp.bfloat16),
            pltpu.VMEM((heads, rows * (wide // HEAD_DIM), 2 * HEAD_DIM), jnp.float32),
            pltpu.VMEM((heads, rows * (wide // HEAD_DIM), HEAD_DIM), jnp.float32),
            pltpu.SemaphoreType.DMA((8, 3, PIECES)),
            pltpu.SemaphoreType.DMA((8, 3, PIECES)),
            pltpu.SemaphoreType.DMA((16,)),
            pltpu.SemaphoreType.DMA((16,)),
        ],
        compiler_params=pltpu.CompilerParams(
            collective_id=0, has_side_effects=True, vmem_limit_bytes=48 * 2**20
        ),
        cost_estimate=pl.CostEstimate(
            flops=4 * rows * wide * (span + pool_keys) * heads,
            bytes_accessed=2 * 2 * heads * rows * wide,
            transcendentals=rows * heads * (wide // HEAD_DIM) * (span + pool_keys),
        ),
    )(
        jnp.swapaxes(queries, 0, 1),
        jnp.swapaxes(branch_key_value, 0, 1),
        starts,
        jnp.swapaxes(pool[0], 0, 1),
        table,
    )
    return jnp.swapaxes(attended, 0, 1)


def solution(mesh):
    small = mesh.shape["seq"] == PLANES * 4 and mesh.shape["head"] == 2
    return jax.shard_map(
        relayed if small else per_device,
        mesh=mesh,
        in_specs=(
            P(("seq", "head"), None, None),
            P(("seq", "head"), None, None),
            P(),
            P("seq", None, "head", None),
            P("head", None),
        ),
        out_specs=P(("seq", "head"), None, None),
        check_vma=False,
    )
```

```python
import functools

import jax
import jax.numpy as jnp
from jax import lax
from jax.experimental import pallas as pl
from jax.experimental.pallas import tpu as pltpu
from jax.sharding import PartitionSpec as P

HEAD_DIM = 128
MESH = pl.DeviceIdType.MESH

def passed_along(value, axis, by):
    count = lax.axis_size(axis)
    pairs = [(i, i + by) for i in range(count) if 0 <= i + by < count]
    return lax.ppermute(value, axis, pairs)


def blend_keys(state, query, pairs, allowed, scale):
    top, total, summed = state
    width = query.shape[-1]
    keys = pairs[..., :width]
    value_rows = pairs[..., width:]
    scores = jnp.einsum("rhgd,khd->rhgk", query, keys, preferred_element_type=jnp.float32) * scale
    scores = jnp.where(allowed, scores, -jnp.inf)
    new_top = jnp.maximum(top, jnp.max(scores, axis=-1))
    factor = jnp.exp(top - new_top)
    weights = jnp.exp(scores - new_top[..., None])
    total = total * factor + jnp.sum(weights, axis=-1)
    rounded = weights.astype(jnp.bfloat16)
    summed = summed * factor[..., None] + jnp.einsum(
        "rhgk,khd->rhgd", rounded, value_rows, preferred_element_type=jnp.float32
    )
    return (new_top, total, summed)


def per_device(queries, branch_key_value, branch_ids, pool, page_table):
    reach_count = min(32, lax.axis_size("seq") // 2)
    query, pairs = (
        lax.all_to_all(queries, "head", split_axis=1, concat_axis=0, tiled=True),
        lax.all_to_all(branch_key_value, "head", split_axis=1, concat_axis=0, tiled=True),
    )
    rows = query.shape[0]
    local_heads = query.shape[1]
    group = query.shape[2] // HEAD_DIM
    query = query.reshape(rows, local_heads, group, HEAD_DIM)
    scale = HEAD_DIM ** (-0.5)
    row_start = lax.axis_index("seq") * rows
    row_ids = jnp.arange(rows, dtype=jnp.int32)
    own_ids = lax.dynamic_slice_in_dim(branch_ids, row_start, rows, 0)
    own_rows = row_start + row_ids
    state = (
        jnp.full((rows, local_heads, group), -1e30, jnp.float32),
        jnp.zeros((rows, local_heads, group), jnp.float32),
        jnp.zeros((rows, local_heads, group, HEAD_DIM), jnp.float32),
    )
    page_rows = pool.shape[1]
    pair_width = pool.shape[3]
    piece = lax.all_gather(pool, "seq", axis=0, tiled=True)
    count = piece.shape[0]
    page_ids = jnp.arange(count, dtype=jnp.int32)
    chosen = jnp.any(page_table[:, :, None] == page_ids[None, None, :], axis=1)
    allowed = jnp.broadcast_to(chosen[:, :, None], (local_heads, count, page_rows))
    allowed = allowed.reshape(local_heads, count * page_rows)
    flat = piece.reshape(count * page_rows, local_heads, pair_width)

    def fold_in_piece(inner):
        return blend_keys(inner, query, flat, allowed[None, :, None, :], scale)

    def keep_state(inner):
        return inner

    state = lax.cond(jnp.any(chosen), fold_in_piece, keep_state, state)

    def causal_step(carry, block, back):
        key_start = row_start - back * rows
        key_ids = lax.dynamic_slice_in_dim(branch_ids, jnp.maximum(key_start, 0), rows, 0)
        key_rows = key_start + row_ids
        allowed = (
            (key_ids[None, :] == own_ids[:, None])
            & (key_rows[None, :] <= own_rows[:, None])
            & (key_start >= 0)
        )
        return blend_keys(carry, query, block, allowed[:, None, None, :], scale)

    state = causal_step(state, pairs, 0)
    for back in range(1, reach_count + 1):
        earlier = passed_along(pairs, "seq", back)
        state = causal_step(state, earlier, back)
    top, total, summed = state
    mixed = (
        (summed / total[..., None])
        .astype(jnp.bfloat16)
        .reshape(rows, local_heads, group * HEAD_DIM)
    )
    return lax.all_to_all(mixed, "head", split_axis=0, concat_axis=1, tiled=True)


PLANES = 4
PLANE_BLOCKS = 8
CHUNK = 16
PIECES = 2
KZ, KX, KY, KD, KSZ, KSX, KSY, KSD = range(8)


def relay_kernel(
    listed,
    query_ref, pairs_ref, start_ref, pool_ref, table_ref, out_ref,
    window, prefix, tables, bias, pool_bias, scores, weights, mixed, tops,
    send_sem, recv_sem, pool_send, pool_recv,
):
    heads, rows, width = pairs_ref.shape
    page_rows = pool_ref.shape[1]
    piece = heads // PIECES
    seq = lax.axis_index("seq")
    y = lax.axis_index("head")
    z, x, c = seq // 4, (seq // 2) % 2, seq % 2
    place = x * 4 + c * 2 + y

    def device(dz=0, dx=0, dc=0, dy=0):
        nx = 1 - x if dx else x
        nc = 1 - c if dc else c
        ny = 1 - y if dy else y
        return (((z + dz) * 2 + nx) * 2 + nc, ny)

    up, down = device(dz=1), device(dz=-1)
    xn, yn, sib = device(dx=1), device(dy=1), device(dc=1)

    barrier = pltpu.get_barrier_semaphore()
    for other in (xn, yn, sib):
        pl.semaphore_signal(barrier, inc=1, device_id=other, device_id_type=MESH)

    @pl.when(z < PLANES - 1)
    def _():
        pl.semaphore_signal(barrier, inc=1, device_id=up, device_id_type=MESH)

    @pl.when(z > 0)
    def _():
        pl.semaphore_signal(barrier, inc=1, device_id=down, device_id_type=MESH)

    def block_at(k, bx, bc, by):
        return (2 - k) * PLANE_BLOCKS + bx * 4 + bc * 2 + by

    window[:, pl.ds(block_at(0, x, c, y), 1)] = pairs_ref[...][:, None]
    half = heads // 2
    own_page = pl.ds(pl.multiple_of(((c * PLANES + z) * 2 + x) * page_rows, page_rows), page_rows)
    prefix[pl.ds(y * half, half), own_page, :] = pool_ref[...]
    tables[pl.ds(y, 1)] = table_ref[...][None]

    pl.semaphore_wait(
        barrier, 3 + jnp.where(z < PLANES - 1, 1, 0) + jnp.where(z > 0, 1, 0)
    )

    def message(kind, k, j, k_from, bx, bc, by, target):
        part = pl.ds(j * piece, piece)
        return pltpu.make_async_remote_copy(
            src_ref=window.at[part, block_at(k_from, bx, bc, by)],
            dst_ref=window.at[part, block_at(k, bx, bc, by)],
            send_sem=send_sem.at[kind, k, j],
            recv_sem=recv_sem.at[kind, k, j],
            device_id=target,
            device_id_type=MESH,
        )

    source = {
        KZ: (x, c, y), KX: (x, c, y), KY: (x, c, y),
        KSZ: (x, c, y), KSX: (1 - x, c, y), KSY: (x, c, 1 - y), KSD: (1 - x, c, 1 - y),
    }
    landing = {
        KZ: (x, c, y), KX: (1 - x, c, y), KY: (x, c, 1 - y), KD: (1 - x, c, 1 - y),
        KSZ: (x, 1 - c, y), KSX: (1 - x, 1 - c, y),
        KSY: (x, 1 - c, 1 - y), KSD: (1 - x, 1 - c, 1 - y),
    }
    targets = {KZ: up, KX: xn, KY: yn, KSZ: sib, KSX: sib, KSY: sib, KSD: sib}

    def x_first(j):
        return j < PIECES // 2

    def outgoing(kind, k, j):
        return message(kind, k, j, k - 1 if kind == KZ else k, *source[kind], targets[kind])

    def corner_out(k, j, by_y):
        where, target = ((1 - x, c, y), yn) if by_y else ((x, c, 1 - y), xn)
        return message(KD, k, j, k, *where, target)

    def present(k):
        return z >= k

    def takes_x(k):
        if k == 0:
            return x == 1
        return present(k) if k == 1 else present(k) & (x == 0)

    def gives_x(k):
        if k == 0:
            return x == 0
        return present(k) if k == 1 else present(k) & (x == 1)

    def sends(kind, k):
        if kind == KZ:
            return (z < PLANES - 1) & (z >= k - 1)
        if kind == KX:
            return gives_x(k)
        if kind in (KY, KSZ, KSY):
            return present(k)
        return takes_x(k)

    def receives(kind, k):
        if kind in (KX, KD, KSX, KSD):
            return takes_x(k)
        return present(k)

    def corner_sends(k, j, by_y):
        return takes_x(k) & x_first(j) if by_y else gives_x(k) & jnp.logical_not(x_first(j))

    started = []

    def start(kind, k, j):
        started.append((kind, k))

        @pl.when(sends(kind, k))
        def _():
            outgoing(kind, k, j).start()

    def corner_start(k, j, by_y):
        @pl.when(corner_sends(k, j, by_y))
        def _():
            corner_out(k, j, by_y).start()

    def for_pieces(body):
        lax.fori_loop(0, PIECES, lambda j, carry: (body(j), carry)[1], 0)

    def arrived(kind, k, j):
        @pl.when(receives(kind, k))
        def _():
            message(kind, k, j, k, *landing[kind], sib).wait_recv()

    def pool_message(index, src, target):
        return pltpu.make_async_remote_copy(
            src_ref=src, dst_ref=src,
            send_sem=pool_send.at[index], recv_sem=pool_recv.at[index],
            device_id=target, device_id_type=MESH,
        )

    def layer_at(plane, layer):
        return prefix.at[
            :, pl.ds(pl.multiple_of((layer * PLANES + plane) * 2 * page_rows, 2 * page_rows), 2 * page_rows), :
        ]

    table_out = pool_message(0, tables.at[pl.ds(y, 1)], yn)
    table_in = pool_message(0, tables.at[pl.ds(1 - y, 1)], yn)
    py_out = pool_message(1, prefix.at[pl.ds(y * half, half), own_page, :], yn)
    py_in = pool_message(1, prefix.at[pl.ds((1 - y) * half, half), own_page, :], yn)
    x_page = pl.ds(pl.multiple_of(((c * PLANES + z) * 2 + 1 - x) * page_rows, page_rows), page_rows)
    px_out = pool_message(2, prefix.at[:, own_page, :], xn)
    px_in = pool_message(2, prefix.at[:, x_page, :], xn)
    UP, DOWN, SIB_UP, SIB_DOWN, SIB_OWN = 3, 6, 9, 12, 15

    def from_below(d):
        return z >= d

    def from_above(d):
        return z + d < PLANES

    def up_out(d):
        return pool_message(UP + d - 1, layer_at(z - d + 1, c), up)

    def down_out(d):
        return pool_message(DOWN + d - 1, layer_at(z + d - 1, c), down)

    def up_sends(d):
        return (z < PLANES - 1) & (z >= d - 1)

    def down_sends(d):
        return (z > 0) & (z + d - 1 < PLANES)

    def pool_start(d):
        @pl.when(up_sends(d))
        def _():
            up_out(d).start()

        @pl.when(down_sends(d))
        def _():
            down_out(d).start()

    def pool_arrived(d):
        @pl.when(from_below(d))
        def _():
            pool_message(UP + d - 1, layer_at(z - d, c), up).wait_recv()
            pool_message(SIB_UP + d - 1, layer_at(z - d, c), sib).start()

        @pl.when(from_above(d))
        def _():
            pool_message(DOWN + d - 1, layer_at(z + d, c), up).wait_recv()
            pool_message(SIB_DOWN + d - 1, layer_at(z + d, c), sib).start()

        if d < PLANES - 1:
            pool_start(d + 1)

    py_out.start()
    table_out.start()

    @for_pieces
    def _(j):
        for kind, k in ((KZ, 1), (KX, 0), (KY, 0), (KSZ, 0)):
            start(kind, k, j)

    plane_rows = PLANE_BLOCKS * rows

    @pl.when(z < 2)
    def _():
        window[:, :PLANE_BLOCKS] = jnp.zeros((heads, PLANE_BLOCKS, rows, width), window.dtype)

    @pl.when(z < 1)
    def _():
        window[:, PLANE_BLOCKS:2 * PLANE_BLOCKS] = jnp.zeros((heads, PLANE_BLOCKS, rows, width), window.dtype)

    span = bias.shape[1]
    column = lax.broadcasted_iota(jnp.int32, (rows, span), 1)
    row = lax.broadcasted_iota(jnp.int32, (rows, span), 0)
    base = (z * PLANE_BLOCKS + place) * rows - 2 * plane_rows
    seen = (column >= start_ref[...] - base) & (column <= row + 2 * plane_rows)
    bias[...] = jnp.where(seen, 0.0, -1e30)

    py_in.wait_recv()
    px_out.start()

    @for_pieces
    def _(j):
        arrived(KZ, 1, j)
        for kind, k in ((KZ, 2), (KX, 1), (KY, 1), (KSZ, 1)):
            start(kind, k, j)

    px_in.wait_recv()
    pool_start(1)
    pool_message(SIB_OWN, layer_at(z, c), sib).start()

    def cross(k, j):
        arrived(KX, k, j)
        corner_start(k, j, True)
        start(KSX, k, j)
        arrived(KY, k, j)
        corner_start(k, j, False)
        start(KSY, k, j)

    def corner(k, j):
        arrived(KD, k, j)
        start(KSD, k, j)

    @for_pieces
    def _(j):
        cross(0, j)

    pool_arrived(1)

    @for_pieces
    def _(j):
        arrived(KZ, 2, j)
        for kind, k in ((KX, 2), (KY, 2), (KSZ, 2)):
            start(kind, k, j)

    @for_pieces
    def _(j):
        cross(1, j)
        corner(0, j)

    pool_arrived(2)

    @for_pieces
    def _(j):
        corner(1, j)

    pool_arrived(3)

    factor = HEAD_DIM ** (-0.5) * 1.4426950408889634
    group = query_ref.shape[2] // HEAD_DIM
    keys = PLANES * 4 * page_rows
    far_span = PLANE_BLOCKS * rows
    near_span = span - far_span
    contract = (((1,), (1,)), ((), ()))

    def stacked_queries(h):
        queries = query_ref[h]
        return jnp.concatenate(
            [queries[:, g * HEAD_DIM:(g + 1) * HEAD_DIM] for g in range(group)], axis=0
        )

    def score(query, pairs):
        scores[:, :pairs.shape[0]] = lax.dot_general(
            query, pairs[:, :HEAD_DIM], contract, preferred_element_type=jnp.float32
        )

    def weighted(pairs):
        count = pairs.shape[0]
        values = jnp.concatenate(
            [pairs[:, HEAD_DIM:], jnp.ones((count, HEAD_DIM), jnp.bfloat16)], axis=1
        )
        return jnp.dot(weights[:, :count], values, preferred_element_type=jnp.float32)

    def chunks():
        for r in range(0, rows, CHUNK):
            for g in range(group):
                yield pl.ds(r, CHUNK), pl.ds(g * rows + r, CHUNK)

    def early(h):
        near = window[h, pl.ds(place + PLANE_BLOCKS, PLANE_BLOCKS + 1)].reshape(near_span, width)
        score(stacked_queries(h), near)
        for mask_rows, own in chunks():
            near_scores = scores[own, :near_span] + bias[mask_rows, far_span:]
            top = factor * jnp.max(near_scores, axis=1, keepdims=True)
            weights[own, :near_span] = jnp.exp2(near_scores * factor - top).astype(jnp.bfloat16)
            tops[h, own] = jnp.broadcast_to(top, (CHUNK, HEAD_DIM))
        mixed[h] = weighted(near)

    def late(h):
        far = window[h, pl.ds(place, PLANE_BLOCKS)].reshape(far_span, width)
        far = jnp.concatenate([prefix[h], far], axis=0)
        score(stacked_queries(h), far)
        count = keys + far_span
        for mask_rows, own in chunks():
            pool_scores = scores[own, :keys] + pool_bias[h]
            far_scores = scores[own, keys:count] + bias[mask_rows, :far_span]
            before = tops[h, own]
            top = jnp.maximum(
                jnp.max(pool_scores, axis=1, keepdims=True), jnp.max(far_scores, axis=1, keepdims=True)
            )
            top = jnp.maximum(before, factor * top)
            weights[own, :keys] = jnp.exp2(pool_scores * factor - top[:, :1]).astype(jnp.bfloat16)
            weights[own, keys:count] = jnp.exp2(far_scores * factor - top[:, :1]).astype(jnp.bfloat16)
            tops[h, own] = jnp.exp2(before - top)
        part = weighted(far)
        shrink = tops[h]
        value_sum = mixed[h, :, :HEAD_DIM] * shrink + part[:, :HEAD_DIM]
        total = mixed[h, :, HEAD_DIM:] * shrink + part[:, HEAD_DIM:]
        result = (value_sum / total).astype(out_ref.dtype)
        for g in range(group):
            out_ref[h, :, g * HEAD_DIM:(g + 1) * HEAD_DIM] = result[g * rows:(g + 1) * rows]

    def for_heads(j, body):
        lax.fori_loop(0, piece, lambda i, carry: (body(j * piece + i), carry)[1], 0)

    def from_sibling(k, j):
        for kind in (KSZ, KSX, KSY, KSD):
            arrived(kind, k, j)

    @for_pieces
    def _(j):
        cross(2, j)
        from_sibling(0, j)
        from_sibling(1, j)
        for_heads(j, early)

    table_in.wait_recv()
    pages = PLANES * 4
    slot = lax.broadcasted_iota(jnp.int32, (8, keys), 1) // page_rows
    page = (slot % (pages // 2)) * 2 + slot // (pages // 2)
    for side in range(2):
        table = tables[side]
        chosen = table[:, 0:1] == page
        for i in range(1, listed):
            chosen = chosen | (table[:, i:i + 1] == page)
        mask = jnp.where(chosen, 0.0, -1e30)
        for i in range(half):
            pool_bias[side * half + i] = mask[i:i + 1]

    @for_pieces
    def _(j):
        corner(2, j)

    for d in range(1, PLANES):
        @pl.when(from_below(d))
        def _():
            pool_message(SIB_UP + d - 1, layer_at(z - d, 1 - c), sib).wait_recv()

        @pl.when(from_above(d))
        def _():
            pool_message(SIB_DOWN + d - 1, layer_at(z + d, 1 - c), sib).wait_recv()
    pool_message(SIB_OWN, layer_at(z, 1 - c), sib).wait_recv()

    @for_pieces
    def _(j):
        from_sibling(2, j)
        for_heads(j, late)

    @for_pieces
    def _(j):
        for kind, k in started:
            @pl.when(sends(kind, k))
            def _():
                outgoing(kind, k, j).wait_send()

        for k in range(3):
            for by_y in (True, False):
                @pl.when(corner_sends(k, j, by_y))
                def _():
                    corner_out(k, j, by_y).wait_send()

    table_out.wait_send()
    py_out.wait_send()
    px_out.wait_send()
    pool_message(SIB_OWN, layer_at(z, c), sib).wait_send()
    for d in range(1, PLANES):
        @pl.when(up_sends(d))
        def _():
            up_out(d).wait_send()

        @pl.when(down_sends(d))
        def _():
            down_out(d).wait_send()

        @pl.when(from_below(d))
        def _():
            pool_message(SIB_UP + d - 1, layer_at(z - d, c), sib).wait_send()

        @pl.when(from_above(d))
        def _():
            pool_message(SIB_DOWN + d - 1, layer_at(z + d, c), sib).wait_send()


def relayed(queries, branch_key_value, branch_ids, pool, page_table):
    rows, heads, width = branch_key_value.shape
    wide = queries.shape[2]
    page_rows = pool.shape[1]
    block = lax.axis_index("seq") * 2 + lax.axis_index("head")
    own_ids = lax.dynamic_slice_in_dim(branch_ids, block * rows, rows, 0)
    starts = jnp.sum((branch_ids[None, :] < own_ids[:, None]).astype(jnp.int32), axis=1, keepdims=True)
    table = jnp.pad(page_table, ((0, 8 - page_table.shape[0]), (0, 128 - page_table.shape[1])))
    span = 2 * PLANE_BLOCKS * rows + rows
    pool_keys = PLANES * 4 * page_rows
    vmem = pl.BlockSpec(memory_space=pltpu.VMEM)
    attended = pl.pallas_call(
        functools.partial(relay_kernel, page_table.shape[1]),
        out_shape=jax.ShapeDtypeStruct((heads, rows, wide), jnp.bfloat16),
        in_specs=[vmem] * 5,
        out_specs=vmem,
        scratch_shapes=[
            pltpu.VMEM((heads, 3 * PLANE_BLOCKS, rows, width), jnp.bfloat16),
            pltpu.VMEM((heads, pool_keys, width), jnp.bfloat16),
            pltpu.VMEM((2, 8, 128), jnp.int32),
            pltpu.VMEM((rows, span), jnp.float32),
            pltpu.VMEM((heads, 1, pool_keys), jnp.float32),
            pltpu.VMEM((rows * (wide // HEAD_DIM), pool_keys + (PLANE_BLOCKS + 1) * rows), jnp.float32),
            pltpu.VMEM((rows * (wide // HEAD_DIM), pool_keys + (PLANE_BLOCKS + 1) * rows), jnp.bfloat16),
            pltpu.VMEM((heads, rows * (wide // HEAD_DIM), 2 * HEAD_DIM), jnp.float32),
            pltpu.VMEM((heads, rows * (wide // HEAD_DIM), HEAD_DIM), jnp.float32),
            pltpu.SemaphoreType.DMA((8, 3, PIECES)),
            pltpu.SemaphoreType.DMA((8, 3, PIECES)),
            pltpu.SemaphoreType.DMA((16,)),
            pltpu.SemaphoreType.DMA((16,)),
        ],
        compiler_params=pltpu.CompilerParams(
            collective_id=0, has_side_effects=True, vmem_limit_bytes=48 * 2**20
        ),
        cost_estimate=pl.CostEstimate(
            flops=4 * rows * wide * (span + pool_keys) * heads,
            bytes_accessed=2 * 2 * heads * rows * wide,
            transcendentals=rows * heads * (wide // HEAD_DIM) * (span + pool_keys),
        ),
    )(
        jnp.swapaxes(queries, 0, 1),
        jnp.swapaxes(branch_key_value, 0, 1),
        starts,
        jnp.swapaxes(pool[0], 0, 1),
        table,
    )
    return jnp.swapaxes(attended, 0, 1)


def solution(mesh):
    small = mesh.shape["seq"] == PLANES * 4 and mesh.shape["head"] == 2
    return jax.shard_map(
        relayed if small else per_device,
        mesh=mesh,
        in_specs=(
            P(("seq", "head"), None, None),
            P(("seq", "head"), None, None),
            P(),
            P("seq", None, "head", None),
            P("head", None),
        ),
        out_specs=P(("seq", "head"), None, None),
        check_vma=False,
    )
```

```python
import functools

import jax
import jax.numpy as jnp
from jax import lax
from jax.experimental import pallas as pl
from jax.experimental.pallas import tpu as pltpu
from jax.sharding import PartitionSpec as P

HEAD_DIM = 128
MESH = pl.DeviceIdType.MESH

def passed_along(value, axis, by):
    count = lax.axis_size(axis)
    pairs = [(i, i + by) for i in range(count) if 0 <= i + by < count]
    return lax.ppermute(value, axis, pairs)


def blend_keys(state, query, pairs, allowed, scale):
    top, total, summed = state
    width = query.shape[-1]
    keys = pairs[..., :width]
    value_rows = pairs[..., width:]
    scores = jnp.einsum("rhgd,khd->rhgk", query, keys, preferred_element_type=jnp.float32) * scale
    scores = jnp.where(allowed, scores, -jnp.inf)
    new_top = jnp.maximum(top, jnp.max(scores, axis=-1))
    factor = jnp.exp(top - new_top)
    weights = jnp.exp(scores - new_top[..., None])
    total = total * factor + jnp.sum(weights, axis=-1)
    rounded = weights.astype(jnp.bfloat16)
    summed = summed * factor[..., None] + jnp.einsum(
        "rhgk,khd->rhgd", rounded, value_rows, preferred_element_type=jnp.float32
    )
    return (new_top, total, summed)


def per_device(queries, branch_key_value, branch_ids, pool, page_table):
    reach_count = min(32, lax.axis_size("seq") // 2)
    query, pairs = (
        lax.all_to_all(queries, "head", split_axis=1, concat_axis=0, tiled=True),
        lax.all_to_all(branch_key_value, "head", split_axis=1, concat_axis=0, tiled=True),
    )
    rows = query.shape[0]
    local_heads = query.shape[1]
    group = query.shape[2] // HEAD_DIM
    query = query.reshape(rows, local_heads, group, HEAD_DIM)
    scale = HEAD_DIM ** (-0.5)
    row_start = lax.axis_index("seq") * rows
    row_ids = jnp.arange(rows, dtype=jnp.int32)
    own_ids = lax.dynamic_slice_in_dim(branch_ids, row_start, rows, 0)
    own_rows = row_start + row_ids
    state = (
        jnp.full((rows, local_heads, group), -1e30, jnp.float32),
        jnp.zeros((rows, local_heads, group), jnp.float32),
        jnp.zeros((rows, local_heads, group, HEAD_DIM), jnp.float32),
    )
    page_rows = pool.shape[1]
    pair_width = pool.shape[3]
    piece = lax.all_gather(pool, "seq", axis=0, tiled=True)
    count = piece.shape[0]
    page_ids = jnp.arange(count, dtype=jnp.int32)
    chosen = jnp.any(page_table[:, :, None] == page_ids[None, None, :], axis=1)
    allowed = jnp.broadcast_to(chosen[:, :, None], (local_heads, count, page_rows))
    allowed = allowed.reshape(local_heads, count * page_rows)
    flat = piece.reshape(count * page_rows, local_heads, pair_width)

    def fold_in_piece(inner):
        return blend_keys(inner, query, flat, allowed[None, :, None, :], scale)

    def keep_state(inner):
        return inner

    state = lax.cond(jnp.any(chosen), fold_in_piece, keep_state, state)

    def causal_step(carry, block, back):
        key_start = row_start - back * rows
        key_ids = lax.dynamic_slice_in_dim(branch_ids, jnp.maximum(key_start, 0), rows, 0)
        key_rows = key_start + row_ids
        allowed = (
            (key_ids[None, :] == own_ids[:, None])
            & (key_rows[None, :] <= own_rows[:, None])
            & (key_start >= 0)
        )
        return blend_keys(carry, query, block, allowed[:, None, None, :], scale)

    state = causal_step(state, pairs, 0)
    for back in range(1, reach_count + 1):
        earlier = passed_along(pairs, "seq", back)
        state = causal_step(state, earlier, back)
    top, total, summed = state
    mixed = (
        (summed / total[..., None])
        .astype(jnp.bfloat16)
        .reshape(rows, local_heads, group * HEAD_DIM)
    )
    return lax.all_to_all(mixed, "head", split_axis=0, concat_axis=1, tiled=True)


PLANES = 4
PLANE_BLOCKS = 8
CHUNK = 16
PIECES = 2
KZ, KX, KY, KD, KSZ, KSX, KSY, KSD = range(8)


def relay_kernel(
    listed,
    query_ref, pairs_ref, start_ref, pool_ref, table_ref, out_ref,
    window, prefix, tables, bias, pool_bias, scores, weights, mixed, tops,
    send_sem, recv_sem, pool_send, pool_recv,
):
    heads, rows, width = pairs_ref.shape
    page_rows = pool_ref.shape[1]
    piece = heads // PIECES
    seq = lax.axis_index("seq")
    y = lax.axis_index("head")
    z, x, c = seq // 4, (seq // 2) % 2, seq % 2
    place = x * 4 + c * 2 + y

    def device(dz=0, dx=0, dc=0, dy=0):
        nx = 1 - x if dx else x
        nc = 1 - c if dc else c
        ny = 1 - y if dy else y
        return (((z + dz) * 2 + nx) * 2 + nc, ny)

    up, down = device(dz=1), device(dz=-1)
    xn, yn, sib = device(dx=1), device(dy=1), device(dc=1)

    barrier = pltpu.get_barrier_semaphore()
    for other in (xn, yn, sib):
        pl.semaphore_signal(barrier, inc=1, device_id=other, device_id_type=MESH)

    @pl.when(z < PLANES - 1)
    def _():
        pl.semaphore_signal(barrier, inc=1, device_id=up, device_id_type=MESH)

    @pl.when(z > 0)
    def _():
        pl.semaphore_signal(barrier, inc=1, device_id=down, device_id_type=MESH)

    def block_at(k, bx, bc, by):
        return (2 - k) * PLANE_BLOCKS + bx * 4 + bc * 2 + by

    window[:, pl.ds(block_at(0, x, c, y), 1)] = pairs_ref[...][:, None]
    half = heads // 2
    own_page = pl.ds(pl.multiple_of(((c * PLANES + z) * 2 + x) * page_rows, page_rows), page_rows)
    prefix[pl.ds(y * half, half), own_page, :] = pool_ref[...]
    tables[pl.ds(y, 1)] = table_ref[...][None]

    pl.semaphore_wait(
        barrier, 3 + jnp.where(z < PLANES - 1, 1, 0) + jnp.where(z > 0, 1, 0)
    )

    def message(kind, k, j, k_from, bx, bc, by, target):
        part = pl.ds(j * piece, piece)
        return pltpu.make_async_remote_copy(
            src_ref=window.at[part, block_at(k_from, bx, bc, by)],
            dst_ref=window.at[part, block_at(k, bx, bc, by)],
            send_sem=send_sem.at[kind, k, j],
            recv_sem=recv_sem.at[kind, k, j],
            device_id=target,
            device_id_type=MESH,
        )

    source = {
        KZ: (x, c, y), KX: (x, c, y), KY: (x, c, y),
        KSZ: (x, c, y), KSX: (1 - x, c, y), KSY: (x, c, 1 - y), KSD: (1 - x, c, 1 - y),
    }
    landing = {
        KZ: (x, c, y), KX: (1 - x, c, y), KY: (x, c, 1 - y), KD: (1 - x, c, 1 - y),
        KSZ: (x, 1 - c, y), KSX: (1 - x, 1 - c, y),
        KSY: (x, 1 - c, 1 - y), KSD: (1 - x, 1 - c, 1 - y),
    }
    targets = {KZ: up, KX: xn, KY: yn, KSZ: sib, KSX: sib, KSY: sib, KSD: sib}

    def x_first(j):
        return j < PIECES // 2

    def outgoing(kind, k, j):
        return message(kind, k, j, k - 1 if kind == KZ else k, *source[kind], targets[kind])

    def corner_out(k, j, by_y):
        where, target = ((1 - x, c, y), yn) if by_y else ((x, c, 1 - y), xn)
        return message(KD, k, j, k, *where, target)

    def present(k):
        return z >= k

    def takes_x(k):
        if k == 0:
            return x == 1
        return present(k) if k == 1 else present(k) & (x == 0)

    def gives_x(k):
        if k == 0:
            return x == 0
        return present(k) if k == 1 else present(k) & (x == 1)

    def sends(kind, k):
        if kind == KZ:
            return (z < PLANES - 1) & (z >= k - 1)
        if kind == KX:
            return gives_x(k)
        if kind in (KY, KSZ, KSY):
            return present(k)
        return takes_x(k)

    def receives(kind, k):
        if kind in (KX, KD, KSX, KSD):
            return takes_x(k)
        return present(k)

    def corner_sends(k, j, by_y):
        return takes_x(k) & x_first(j) if by_y else gives_x(k) & jnp.logical_not(x_first(j))

    started = []

    def start(kind, k, j):
        started.append((kind, k))

        @pl.when(sends(kind, k))
        def _():
            outgoing(kind, k, j).start()

    def corner_start(k, j, by_y):
        @pl.when(corner_sends(k, j, by_y))
        def _():
            corner_out(k, j, by_y).start()

    def for_pieces(body):
        lax.fori_loop(0, PIECES, lambda j, carry: (body(j), carry)[1], 0)

    def arrived(kind, k, j):
        @pl.when(receives(kind, k))
        def _():
            message(kind, k, j, k, *landing[kind], sib).wait_recv()

    def pool_message(index, src, target):
        return pltpu.make_async_remote_copy(
            src_ref=src, dst_ref=src,
            send_sem=pool_send.at[index], recv_sem=pool_recv.at[index],
            device_id=target, device_id_type=MESH,
        )

    def layer_at(plane, layer):
        return prefix.at[
            :, pl.ds(pl.multiple_of((layer * PLANES + plane) * 2 * page_rows, 2 * page_rows), 2 * page_rows), :
        ]

    table_out = pool_message(0, tables.at[pl.ds(y, 1)], yn)
    table_in = pool_message(0, tables.at[pl.ds(1 - y, 1)], yn)
    py_out = pool_message(1, prefix.at[pl.ds(y * half, half), own_page, :], yn)
    py_in = pool_message(1, prefix.at[pl.ds((1 - y) * half, half), own_page, :], yn)
    x_page = pl.ds(pl.multiple_of(((c * PLANES + z) * 2 + 1 - x) * page_rows, page_rows), page_rows)
    px_out = pool_message(2, prefix.at[:, own_page, :], xn)
    px_in = pool_message(2, prefix.at[:, x_page, :], xn)
    UP, DOWN, SIB_UP, SIB_DOWN, SIB_OWN = 3, 6, 9, 12, 15

    def from_below(d):
        return z >= d

    def from_above(d):
        return z + d < PLANES

    def up_out(d):
        return pool_message(UP + d - 1, layer_at(z - d + 1, c), up)

    def down_out(d):
        return pool_message(DOWN + d - 1, layer_at(z + d - 1, c), down)

    def up_sends(d):
        return (z < PLANES - 1) & (z >= d - 1)

    def down_sends(d):
        return (z > 0) & (z + d - 1 < PLANES)

    def pool_start(d):
        @pl.when(up_sends(d))
        def _():
            up_out(d).start()

        @pl.when(down_sends(d))
        def _():
            down_out(d).start()

    def pool_arrived(d):
        @pl.when(from_below(d))
        def _():
            pool_message(UP + d - 1, layer_at(z - d, c), up).wait_recv()
            pool_message(SIB_UP + d - 1, layer_at(z - d, c), sib).start()

        @pl.when(from_above(d))
        def _():
            pool_message(DOWN + d - 1, layer_at(z + d, c), up).wait_recv()
            pool_message(SIB_DOWN + d - 1, layer_at(z + d, c), sib).start()

        if d < PLANES - 1:
            pool_start(d + 1)

    py_out.start()
    table_out.start()

    @for_pieces
    def _(j):
        for kind, k in ((KZ, 1), (KX, 0), (KY, 0), (KSZ, 0)):
            start(kind, k, j)

    plane_rows = PLANE_BLOCKS * rows

    @pl.when(z < 2)
    def _():
        window[:, :PLANE_BLOCKS] = jnp.zeros((heads, PLANE_BLOCKS, rows, width), window.dtype)

    @pl.when(z < 1)
    def _():
        window[:, PLANE_BLOCKS:2 * PLANE_BLOCKS] = jnp.zeros((heads, PLANE_BLOCKS, rows, width), window.dtype)

    span = bias.shape[1]
    column = lax.broadcasted_iota(jnp.int32, (rows, span), 1)
    row = lax.broadcasted_iota(jnp.int32, (rows, span), 0)
    base = (z * PLANE_BLOCKS + place) * rows - 2 * plane_rows
    seen = (column >= start_ref[...] - base) & (column <= row + 2 * plane_rows)
    bias[...] = jnp.where(seen, 0.0, -1e30)

    py_in.wait_recv()
    px_out.start()

    @for_pieces
    def _(j):
        arrived(KZ, 1, j)
        for kind, k in ((KZ, 2), (KX, 1), (KY, 1), (KSZ, 1)):
            start(kind, k, j)

    px_in.wait_recv()
    pool_start(1)
    pool_message(SIB_OWN, layer_at(z, c), sib).start()

    def cross(k, j):
        arrived(KX, k, j)
        corner_start(k, j, True)
        start(KSX, k, j)
        arrived(KY, k, j)
        corner_start(k, j, False)
        start(KSY, k, j)

    def corner(k, j):
        arrived(KD, k, j)
        start(KSD, k, j)

    @for_pieces
    def _(j):
        cross(0, j)

    pool_arrived(1)

    @for_pieces
    def _(j):
        arrived(KZ, 2, j)
        for kind, k in ((KX, 2), (KY, 2), (KSZ, 2)):
            start(kind, k, j)

    @for_pieces
    def _(j):
        cross(1, j)
        corner(0, j)

    pool_arrived(2)

    @for_pieces
    def _(j):
        corner(1, j)

    pool_arrived(3)

    factor = HEAD_DIM ** (-0.5) * 1.4426950408889634
    group = query_ref.shape[2] // HEAD_DIM
    keys = PLANES * 4 * page_rows
    far_span = PLANE_BLOCKS * rows
    near_span = span - far_span
    contract = (((1,), (1,)), ((), ()))

    def stacked_queries(h):
        queries = query_ref[h]
        return jnp.concatenate(
            [queries[:, g * HEAD_DIM:(g + 1) * HEAD_DIM] for g in range(group)], axis=0
        )

    def score(query, pairs):
        count = pairs.shape[0]
        scores[:, :, :count] = lax.dot_general(
            query, pairs[:, :HEAD_DIM], contract, preferred_element_type=jnp.float32
        ).reshape(group, rows, count)

    def weighted(pairs):
        count = pairs.shape[0]
        values = jnp.concatenate(
            [pairs[:, HEAD_DIM:], jnp.ones((count, HEAD_DIM), jnp.bfloat16)], axis=1
        )
        return jnp.dot(
            weights[:, :, :count].reshape(group * rows, count), values, preferred_element_type=jnp.float32
        )

    chunks = [pl.ds(r, CHUNK) for r in range(0, rows, CHUNK)]

    def early(h):
        near = window[h, pl.ds(place + PLANE_BLOCKS, PLANE_BLOCKS + 1)].reshape(near_span, width)
        score(stacked_queries(h), near)
        for own in chunks:
            near_scores = scores[:, own, :near_span] + bias[own, far_span:][None]
            top = factor * jnp.max(near_scores, axis=2, keepdims=True)
            weights[:, own, :near_span] = jnp.exp2(near_scores * factor - top).astype(jnp.bfloat16)
            tops[h, :, own] = jnp.broadcast_to(top, (group, CHUNK, HEAD_DIM))
        mixed[h] = weighted(near)

    def late(h):
        far = window[h, pl.ds(place, PLANE_BLOCKS)].reshape(far_span, width)
        far = jnp.concatenate([prefix[h], far], axis=0)
        score(stacked_queries(h), far)
        count = keys + far_span
        pool_mask = pool_bias[h][None]
        for own in chunks:
            pool_scores = scores[:, own, :keys] + pool_mask
            far_scores = scores[:, own, keys:count] + bias[own, :far_span][None]
            before = tops[h, :, own]
            top = jnp.maximum(
                jnp.max(pool_scores, axis=2, keepdims=True), jnp.max(far_scores, axis=2, keepdims=True)
            )
            top = jnp.maximum(before, factor * top)
            weights[:, own, :keys] = jnp.exp2(pool_scores * factor - top[..., :1]).astype(jnp.bfloat16)
            weights[:, own, keys:count] = jnp.exp2(far_scores * factor - top[..., :1]).astype(jnp.bfloat16)
            tops[h, :, own] = jnp.exp2(before - top)
        part = weighted(far)
        shrink = tops[h].reshape(group * rows, HEAD_DIM)
        value_sum = mixed[h, :, :HEAD_DIM] * shrink + part[:, :HEAD_DIM]
        total = mixed[h, :, HEAD_DIM:] * shrink + part[:, HEAD_DIM:]
        result = (value_sum / total).astype(out_ref.dtype)
        for g in range(group):
            out_ref[h, :, g * HEAD_DIM:(g + 1) * HEAD_DIM] = result[g * rows:(g + 1) * rows]

    def for_heads(j, body):
        lax.fori_loop(0, piece, lambda i, carry: (body(j * piece + i), carry)[1], 0)

    def from_sibling(k, j):
        for kind in (KSZ, KSX, KSY, KSD):
            arrived(kind, k, j)

    @for_pieces
    def _(j):
        cross(2, j)
        from_sibling(0, j)
        from_sibling(1, j)
        for_heads(j, early)

    table_in.wait_recv()
    pages = PLANES * 4
    slot = lax.broadcasted_iota(jnp.int32, (8, keys), 1) // page_rows
    page = (slot % (pages // 2)) * 2 + slot // (pages // 2)
    for side in range(2):
        table = tables[side]
        chosen = table[:, 0:1] == page
        for i in range(1, listed):
            chosen = chosen | (table[:, i:i + 1] == page)
        mask = jnp.where(chosen, 0.0, -1e30)
        for i in range(half):
            pool_bias[side * half + i] = mask[i:i + 1]

    @for_pieces
    def _(j):
        corner(2, j)

    for d in range(1, PLANES):
        @pl.when(from_below(d))
        def _():
            pool_message(SIB_UP + d - 1, layer_at(z - d, 1 - c), sib).wait_recv()

        @pl.when(from_above(d))
        def _():
            pool_message(SIB_DOWN + d - 1, layer_at(z + d, 1 - c), sib).wait_recv()
    pool_message(SIB_OWN, layer_at(z, 1 - c), sib).wait_recv()

    @for_pieces
    def _(j):
        from_sibling(2, j)
        for_heads(j, late)

    @for_pieces
    def _(j):
        for kind, k in started:
            @pl.when(sends(kind, k))
            def _():
                outgoing(kind, k, j).wait_send()

        for k in range(3):
            for by_y in (True, False):
                @pl.when(corner_sends(k, j, by_y))
                def _():
                    corner_out(k, j, by_y).wait_send()

    table_out.wait_send()
    py_out.wait_send()
    px_out.wait_send()
    pool_message(SIB_OWN, layer_at(z, c), sib).wait_send()
    for d in range(1, PLANES):
        @pl.when(up_sends(d))
        def _():
            up_out(d).wait_send()

        @pl.when(down_sends(d))
        def _():
            down_out(d).wait_send()

        @pl.when(from_below(d))
        def _():
            pool_message(SIB_UP + d - 1, layer_at(z - d, c), sib).wait_send()

        @pl.when(from_above(d))
        def _():
            pool_message(SIB_DOWN + d - 1, layer_at(z + d, c), sib).wait_send()


def relayed(queries, branch_key_value, branch_ids, pool, page_table):
    rows, heads, width = branch_key_value.shape
    wide = queries.shape[2]
    page_rows = pool.shape[1]
    block = lax.axis_index("seq") * 2 + lax.axis_index("head")
    own_ids = lax.dynamic_slice_in_dim(branch_ids, block * rows, rows, 0)
    starts = jnp.sum((branch_ids[None, :] < own_ids[:, None]).astype(jnp.int32), axis=1, keepdims=True)
    table = jnp.pad(page_table, ((0, 8 - page_table.shape[0]), (0, 128 - page_table.shape[1])))
    span = 2 * PLANE_BLOCKS * rows + rows
    pool_keys = PLANES * 4 * page_rows
    vmem = pl.BlockSpec(memory_space=pltpu.VMEM)
    attended = pl.pallas_call(
        functools.partial(relay_kernel, page_table.shape[1]),
        out_shape=jax.ShapeDtypeStruct((heads, rows, wide), jnp.bfloat16),
        in_specs=[vmem] * 5,
        out_specs=vmem,
        scratch_shapes=[
            pltpu.VMEM((heads, 3 * PLANE_BLOCKS, rows, width), jnp.bfloat16),
            pltpu.VMEM((heads, pool_keys, width), jnp.bfloat16),
            pltpu.VMEM((2, 8, 128), jnp.int32),
            pltpu.VMEM((rows, span), jnp.float32),
            pltpu.VMEM((heads, 1, pool_keys), jnp.float32),
            pltpu.VMEM((wide // HEAD_DIM, rows, pool_keys + PLANE_BLOCKS * rows), jnp.float32),
            pltpu.VMEM((wide // HEAD_DIM, rows, pool_keys + PLANE_BLOCKS * rows), jnp.bfloat16),
            pltpu.VMEM((heads, rows * (wide // HEAD_DIM), 2 * HEAD_DIM), jnp.float32),
            pltpu.VMEM((heads, wide // HEAD_DIM, rows, HEAD_DIM), jnp.float32),
            pltpu.SemaphoreType.DMA((8, 3, PIECES)),
            pltpu.SemaphoreType.DMA((8, 3, PIECES)),
            pltpu.SemaphoreType.DMA((16,)),
            pltpu.SemaphoreType.DMA((16,)),
        ],
        compiler_params=pltpu.CompilerParams(
            collective_id=0, has_side_effects=True, vmem_limit_bytes=48 * 2**20
        ),
        cost_estimate=pl.CostEstimate(
            flops=4 * rows * wide * (span + pool_keys) * heads,
            bytes_accessed=2 * 2 * heads * rows * wide,
            transcendentals=rows * heads * (wide // HEAD_DIM) * (span + pool_keys),
        ),
    )(
        jnp.swapaxes(queries, 0, 1),
        jnp.swapaxes(branch_key_value, 0, 1),
        starts,
        jnp.swapaxes(pool[0], 0, 1),
        table,
    )
    return jnp.swapaxes(attended, 0, 1)


def solution(mesh):
    small = mesh.shape["seq"] == PLANES * 4 and mesh.shape["head"] == 2
    return jax.shard_map(
        relayed if small else per_device,
        mesh=mesh,
        in_specs=(
            P(("seq", "head"), None, None),
            P(("seq", "head"), None, None),
            P(),
            P("seq", None, "head", None),
            P("head", None),
        ),
        out_specs=P(("seq", "head"), None, None),
        check_vma=False,
    )
```

```python
import functools

import jax
import jax.numpy as jnp
from jax import lax
from jax.experimental import pallas as pl
from jax.experimental.pallas import tpu as pltpu
from jax.sharding import PartitionSpec as P

HEAD_DIM = 128
MESH = pl.DeviceIdType.MESH

def passed_along(value, axis, by):
    count = lax.axis_size(axis)
    pairs = [(i, i + by) for i in range(count) if 0 <= i + by < count]
    return lax.ppermute(value, axis, pairs)


def blend_keys(state, query, pairs, allowed, scale):
    top, total, summed = state
    width = query.shape[-1]
    keys = pairs[..., :width]
    value_rows = pairs[..., width:]
    scores = jnp.einsum("rhgd,khd->rhgk", query, keys, preferred_element_type=jnp.float32) * scale
    scores = jnp.where(allowed, scores, -jnp.inf)
    new_top = jnp.maximum(top, jnp.max(scores, axis=-1))
    factor = jnp.exp(top - new_top)
    weights = jnp.exp(scores - new_top[..., None])
    total = total * factor + jnp.sum(weights, axis=-1)
    rounded = weights.astype(jnp.bfloat16)
    summed = summed * factor[..., None] + jnp.einsum(
        "rhgk,khd->rhgd", rounded, value_rows, preferred_element_type=jnp.float32
    )
    return (new_top, total, summed)


def per_device(queries, branch_key_value, branch_ids, pool, page_table):
    reach_count = min(32, lax.axis_size("seq") // 2)
    query, pairs = (
        lax.all_to_all(queries, "head", split_axis=1, concat_axis=0, tiled=True),
        lax.all_to_all(branch_key_value, "head", split_axis=1, concat_axis=0, tiled=True),
    )
    rows = query.shape[0]
    local_heads = query.shape[1]
    group = query.shape[2] // HEAD_DIM
    query = query.reshape(rows, local_heads, group, HEAD_DIM)
    scale = HEAD_DIM ** (-0.5)
    row_start = lax.axis_index("seq") * rows
    row_ids = jnp.arange(rows, dtype=jnp.int32)
    own_ids = lax.dynamic_slice_in_dim(branch_ids, row_start, rows, 0)
    own_rows = row_start + row_ids
    state = (
        jnp.full((rows, local_heads, group), -1e30, jnp.float32),
        jnp.zeros((rows, local_heads, group), jnp.float32),
        jnp.zeros((rows, local_heads, group, HEAD_DIM), jnp.float32),
    )
    page_rows = pool.shape[1]
    pair_width = pool.shape[3]
    piece = lax.all_gather(pool, "seq", axis=0, tiled=True)
    count = piece.shape[0]
    page_ids = jnp.arange(count, dtype=jnp.int32)
    chosen = jnp.any(page_table[:, :, None] == page_ids[None, None, :], axis=1)
    allowed = jnp.broadcast_to(chosen[:, :, None], (local_heads, count, page_rows))
    allowed = allowed.reshape(local_heads, count * page_rows)
    flat = piece.reshape(count * page_rows, local_heads, pair_width)

    def fold_in_piece(inner):
        return blend_keys(inner, query, flat, allowed[None, :, None, :], scale)

    def keep_state(inner):
        return inner

    state = lax.cond(jnp.any(chosen), fold_in_piece, keep_state, state)

    def causal_step(carry, block, back):
        key_start = row_start - back * rows
        key_ids = lax.dynamic_slice_in_dim(branch_ids, jnp.maximum(key_start, 0), rows, 0)
        key_rows = key_start + row_ids
        allowed = (
            (key_ids[None, :] == own_ids[:, None])
            & (key_rows[None, :] <= own_rows[:, None])
            & (key_start >= 0)
        )
        return blend_keys(carry, query, block, allowed[:, None, None, :], scale)

    state = causal_step(state, pairs, 0)
    for back in range(1, reach_count + 1):
        earlier = passed_along(pairs, "seq", back)
        state = causal_step(state, earlier, back)
    top, total, summed = state
    mixed = (
        (summed / total[..., None])
        .astype(jnp.bfloat16)
        .reshape(rows, local_heads, group * HEAD_DIM)
    )
    return lax.all_to_all(mixed, "head", split_axis=0, concat_axis=1, tiled=True)


PLANES = 4
PLANE_BLOCKS = 8
CHUNK = 16
PIECES = 2
KZ, KX, KY, KD, KSZ, KSX, KSY, KSD = range(8)


def relay_kernel(
    listed,
    query_ref, pairs_ref, start_ref, pool_ref, table_ref, out_ref,
    window, prefix, tables, bias, pool_bias, scores, weights, mixed, tops, shrinks,
    send_sem, recv_sem, pool_send, pool_recv,
):
    heads, rows, width = pairs_ref.shape
    page_rows = pool_ref.shape[1]
    piece = heads // PIECES
    seq = lax.axis_index("seq")
    y = lax.axis_index("head")
    z, x, c = seq // 4, (seq // 2) % 2, seq % 2
    place = x * 4 + c * 2 + y

    def device(dz=0, dx=0, dc=0, dy=0):
        nx = 1 - x if dx else x
        nc = 1 - c if dc else c
        ny = 1 - y if dy else y
        return (((z + dz) * 2 + nx) * 2 + nc, ny)

    up, down = device(dz=1), device(dz=-1)
    xn, yn, sib = device(dx=1), device(dy=1), device(dc=1)

    barrier = pltpu.get_barrier_semaphore()
    for other in (xn, yn, sib):
        pl.semaphore_signal(barrier, inc=1, device_id=other, device_id_type=MESH)

    @pl.when(z < PLANES - 1)
    def _():
        pl.semaphore_signal(barrier, inc=1, device_id=up, device_id_type=MESH)

    @pl.when(z > 0)
    def _():
        pl.semaphore_signal(barrier, inc=1, device_id=down, device_id_type=MESH)

    def block_at(k, bx, bc, by):
        return (2 - k) * PLANE_BLOCKS + bx * 4 + bc * 2 + by

    window[:, pl.ds(block_at(0, x, c, y), 1)] = pairs_ref[...][:, None]
    half = heads // 2
    own_page = pl.ds(pl.multiple_of(((c * PLANES + z) * 2 + x) * page_rows, page_rows), page_rows)
    prefix[pl.ds(y * half, half), own_page, :] = pool_ref[...]
    tables[pl.ds(y, 1)] = table_ref[...][None]

    pl.semaphore_wait(
        barrier, 3 + jnp.where(z < PLANES - 1, 1, 0) + jnp.where(z > 0, 1, 0)
    )

    def message(kind, k, j, k_from, bx, bc, by, target):
        part = pl.ds(j * piece, piece)
        return pltpu.make_async_remote_copy(
            src_ref=window.at[part, block_at(k_from, bx, bc, by)],
            dst_ref=window.at[part, block_at(k, bx, bc, by)],
            send_sem=send_sem.at[kind, k, j],
            recv_sem=recv_sem.at[kind, k, j],
            device_id=target,
            device_id_type=MESH,
        )

    source = {
        KZ: (x, c, y), KX: (x, c, y), KY: (x, c, y),
        KSZ: (x, c, y), KSX: (1 - x, c, y), KSY: (x, c, 1 - y), KSD: (1 - x, c, 1 - y),
    }
    landing = {
        KZ: (x, c, y), KX: (1 - x, c, y), KY: (x, c, 1 - y), KD: (1 - x, c, 1 - y),
        KSZ: (x, 1 - c, y), KSX: (1 - x, 1 - c, y),
        KSY: (x, 1 - c, 1 - y), KSD: (1 - x, 1 - c, 1 - y),
    }
    targets = {KZ: up, KX: xn, KY: yn, KSZ: sib, KSX: sib, KSY: sib, KSD: sib}

    def x_half(j):
        return j // (PIECES // 2)

    def outgoing(kind, k, j):
        return message(kind, k, j, k - 1 if kind == KZ else k, *source[kind], targets[kind])

    def corner_out(k, j, by_y):
        where, target = ((1 - x, c, y), yn) if by_y else ((x, c, 1 - y), xn)
        return message(KD, k, j, k, *where, target)

    def present(k):
        return z >= k

    def takes_x(k):
        if k == 0:
            return x == 1
        return present(k) if k == 1 else present(k) & (x == 0)

    def gives_x(k):
        if k == 0:
            return x == 0
        return present(k) if k == 1 else present(k) & (x == 1)

    def sends(kind, k):
        if kind == KZ:
            return (z < PLANES - 1) & (z >= k - 1)
        if kind == KX:
            return gives_x(k)
        if kind in (KY, KSZ, KSY):
            return present(k)
        return takes_x(k)

    def receives(kind, k):
        if kind in (KX, KD, KSX, KSD):
            return takes_x(k)
        return present(k)

    def corner_sends(k, j, by_y):
        return takes_x(k) & (x_half(j) == 0) if by_y else gives_x(k) & (x_half(j) == 1)

    started = []

    def start(kind, k, j):
        if (kind, k) not in started:
            started.append((kind, k))

        @pl.when(sends(kind, k))
        def _():
            outgoing(kind, k, j).start()

    def corner_start(k, j, by_y):
        @pl.when(corner_sends(k, j, by_y))
        def _():
            corner_out(k, j, by_y).start()

    def for_pieces(body):
        lax.fori_loop(0, PIECES, lambda j, carry: (body(j), carry)[1], 0)

    def arrived(kind, k, j):
        @pl.when(receives(kind, k))
        def _():
            message(kind, k, j, k, *landing[kind], sib).wait_recv()

    def pool_message(index, src, target):
        return pltpu.make_async_remote_copy(
            src_ref=src, dst_ref=src,
            send_sem=pool_send.at[index], recv_sem=pool_recv.at[index],
            device_id=target, device_id_type=MESH,
        )

    def layer_at(plane, layer):
        return prefix.at[
            :, pl.ds(pl.multiple_of((layer * PLANES + plane) * 2 * page_rows, 2 * page_rows), 2 * page_rows), :
        ]

    table_out = pool_message(0, tables.at[pl.ds(y, 1)], yn)
    table_in = pool_message(0, tables.at[pl.ds(1 - y, 1)], yn)
    py_out = pool_message(1, prefix.at[pl.ds(y * half, half), own_page, :], yn)
    py_in = pool_message(1, prefix.at[pl.ds((1 - y) * half, half), own_page, :], yn)
    x_page = pl.ds(pl.multiple_of(((c * PLANES + z) * 2 + 1 - x) * page_rows, page_rows), page_rows)
    px_out = pool_message(2, prefix.at[:, own_page, :], xn)
    px_in = pool_message(2, prefix.at[:, x_page, :], xn)
    UP, DOWN, SIB_UP, SIB_DOWN, SIB_OWN = 3, 6, 9, 12, 15

    def from_below(d):
        return z >= d

    def from_above(d):
        return z + d < PLANES

    def up_out(d):
        return pool_message(UP + d - 1, layer_at(z - d + 1, c), up)

    def down_out(d):
        return pool_message(DOWN + d - 1, layer_at(z + d - 1, c), down)

    def up_sends(d):
        return (z < PLANES - 1) & (z >= d - 1)

    def down_sends(d):
        return (z > 0) & (z + d - 1 < PLANES)

    def pool_start(d):
        @pl.when(up_sends(d))
        def _():
            up_out(d).start()

        @pl.when(down_sends(d))
        def _():
            down_out(d).start()

    def pool_arrived(d):
        @pl.when(from_below(d))
        def _():
            pool_message(UP + d - 1, layer_at(z - d, c), up).wait_recv()
            pool_message(SIB_UP + d - 1, layer_at(z - d, c), sib).start()

        @pl.when(from_above(d))
        def _():
            pool_message(DOWN + d - 1, layer_at(z + d, c), up).wait_recv()
            pool_message(SIB_DOWN + d - 1, layer_at(z + d, c), sib).start()

        if d < PLANES - 1:
            pool_start(d + 1)

    py_out.start()
    table_out.start()

    @for_pieces
    def _(j):
        for kind, k in ((KZ, 1), (KX, 0), (KY, 0), (KSZ, 0)):
            start(kind, k, j)

    plane_rows = PLANE_BLOCKS * rows

    @pl.when(z < 1)
    def _():
        window[:, PLANE_BLOCKS:2 * PLANE_BLOCKS] = jnp.zeros((heads, PLANE_BLOCKS, rows, width), window.dtype)

    span = bias.shape[1]
    column = lax.broadcasted_iota(jnp.int32, (rows, span), 1)
    row = lax.broadcasted_iota(jnp.int32, (rows, span), 0)
    base = z * plane_rows - 2 * plane_rows
    seen = (column >= start_ref[...] - base) & (column <= row + place * rows + 2 * plane_rows)
    bias[...] = jnp.where(seen, 0.0, -1e30)

    py_in.wait_recv()
    px_out.start()

    @for_pieces
    def _(j):
        arrived(KZ, 1, j)
        for kind, k in ((KZ, 2), (KX, 1), (KY, 1), (KSZ, 1)):
            start(kind, k, j)

    px_in.wait_recv()
    pool_start(1)
    pool_message(SIB_OWN, layer_at(z, c), sib).start()

    def cross(k, j):
        arrived(KX, k, j)
        corner_start(k, j, True)
        start(KSX, k, j)
        arrived(KY, k, j)
        corner_start(k, j, False)
        start(KSY, k, j)

    def corner(k, j):
        arrived(KD, k, j)
        start(KSD, k, j)

    @for_pieces
    def _(j):
        cross(0, j)

    table_in.wait_recv()
    pages = PLANES * 4
    keys = pages * page_rows
    slot = lax.broadcasted_iota(jnp.int32, (8, keys), 1) // page_rows
    page = (slot % (pages // 2)) * 2 + slot // (pages // 2)
    for side in range(2):
        table = tables[side]
        chosen = table[:, 0:1] == page
        for i in range(1, listed):
            chosen = chosen | (table[:, i:i + 1] == page)
        mask = jnp.where(chosen, 0.0, -1e30)
        for i in range(half):
            pool_bias[side * half + i] = mask[i:i + 1]

    factor = HEAD_DIM ** (-0.5) * 1.4426950408889634
    group = query_ref.shape[2] // HEAD_DIM
    contract = (((1,), (1,)), ((), ()))

    def stacked_queries(h):
        queries = query_ref[h]
        return jnp.concatenate(
            [queries[:, g * HEAD_DIM:(g + 1) * HEAD_DIM] for g in range(group)], axis=0
        )

    def score(query, pairs):
        count = pairs.shape[0]
        scores[:, :, :count] = lax.dot_general(
            query, pairs[:, :HEAD_DIM], contract, preferred_element_type=jnp.float32
        ).reshape(group, rows, count)

    def weighted(pairs):
        count = pairs.shape[0]
        values = jnp.concatenate(
            [pairs[:, HEAD_DIM:], jnp.ones((count, HEAD_DIM), jnp.bfloat16)], axis=1
        )
        return jnp.dot(
            weights[:, :, :count].reshape(group * rows, count), values, preferred_element_type=jnp.float32
        )

    chunks = [pl.ds(r, CHUNK) for r in range(0, rows, CHUNK)]

    def attend(h, first_slot, slots, with_pool, begins):
        pairs = window[h, first_slot:first_slot + slots].reshape(slots * rows, width)
        columns = slice(first_slot * rows, (first_slot + slots) * rows)
        at = keys if with_pool else 0
        if with_pool:
            pairs = jnp.concatenate([prefix[h], pairs], axis=0)
        score(stacked_queries(h), pairs)
        count = pairs.shape[0]
        for own in chunks:
            near_scores = scores[:, own, at:count] + bias[own, columns][None]
            top = jnp.max(near_scores, axis=2, keepdims=True)
            if with_pool:
                pool_scores = scores[:, own, :at] + pool_bias[h][None]
                top = jnp.maximum(top, jnp.max(pool_scores, axis=2, keepdims=True))
            top = jnp.broadcast_to(factor * top, (group, CHUNK, HEAD_DIM))
            if not begins:
                before = tops[h, :, own]
                top = jnp.maximum(before, top)
                shrinks[:, own] = jnp.exp2(before - top)
            tops[h, :, own] = top
            if with_pool:
                weights[:, own, :at] = jnp.exp2(pool_scores * factor - top[..., :1]).astype(jnp.bfloat16)
            weights[:, own, at:count] = jnp.exp2(near_scores * factor - top[..., :1]).astype(jnp.bfloat16)
        part = weighted(pairs)
        if begins:
            mixed[h] = part
        else:
            shrink = shrinks[...].reshape(group * rows, HEAD_DIM)
            mixed[h, :, :HEAD_DIM] = mixed[h, :, :HEAD_DIM] * shrink + part[:, :HEAD_DIM]
            mixed[h, :, HEAD_DIM:] = mixed[h, :, HEAD_DIM:] * shrink + part[:, HEAD_DIM:]

    def finish(h):
        result = (mixed[h, :, :HEAD_DIM] / mixed[h, :, HEAD_DIM:]).astype(out_ref.dtype)
        for g in range(group):
            out_ref[h, :, g * HEAD_DIM:(g + 1) * HEAD_DIM] = result[g * rows:(g + 1) * rows]

    half_plane = PLANE_BLOCKS // 2

    def own_part(h):
        @pl.when(x == 0)
        def _():
            attend(h, 2 * PLANE_BLOCKS, half_plane, False, True)

        @pl.when(x == 1)
        def _():
            attend(h, 2 * PLANE_BLOCKS, PLANE_BLOCKS, False, True)

    def next_part(h):
        attend(h, PLANE_BLOCKS, PLANE_BLOCKS, True, False)

    def last_part(h):
        @pl.when((z >= 2) & (x == 0))
        def _():
            attend(h, 0, PLANE_BLOCKS, False, False)

        @pl.when((z >= 2) & (x == 1))
        def _():
            attend(h, half_plane, half_plane, False, False)

        finish(h)

    def for_heads(body):
        lax.fori_loop(0, heads, lambda h, carry: (body(h), carry)[1], 0)

    def from_sibling(k):
        @for_pieces
        def _(j):
            for kind in (KSZ, KSX, KSY, KSD):
                arrived(kind, k, j)

    @for_pieces
    def _(j):
        corner(0, j)

    from_sibling(0)

    @for_heads
    def _(h):
        own_part(h)

        @pl.when(h == 1)
        def _():
            @for_pieces
            def _(j):
                arrived(KZ, 2, j)
                for kind, k in ((KX, 2), (KY, 2), (KSZ, 2)):
                    start(kind, k, j)

            pool_arrived(1)

        @pl.when(h == 3)
        def _():
            cross(1, 0)

        @pl.when(h == 5)
        def _():
            for j in range(1, PIECES):
                cross(1, j)
            pool_arrived(2)

    @for_pieces
    def _(j):
        corner(1, j)

    pool_arrived(3)
    for d in range(1, PLANES):
        @pl.when(from_below(d))
        def _():
            pool_message(SIB_UP + d - 1, layer_at(z - d, 1 - c), sib).wait_recv()

        @pl.when(from_above(d))
        def _():
            pool_message(SIB_DOWN + d - 1, layer_at(z + d, 1 - c), sib).wait_recv()
    pool_message(SIB_OWN, layer_at(z, 1 - c), sib).wait_recv()

    from_sibling(1)

    @for_heads
    def _(h):
        next_part(h)

        @pl.when(h == 1)
        def _():
            cross(2, 0)

        @pl.when(h == 3)
        def _():
            for j in range(1, PIECES):
                cross(2, j)

        @pl.when(h == 5)
        def _():
            @for_pieces
            def _(j):
                corner(2, j)

    from_sibling(2)

    for_heads(last_part)

    @for_pieces
    def _(j):
        for kind, k in started:
            @pl.when(sends(kind, k))
            def _():
                outgoing(kind, k, j).wait_send()

        for k in range(3):
            for by_y in (True, False):
                @pl.when(corner_sends(k, j, by_y))
                def _():
                    corner_out(k, j, by_y).wait_send()

    table_out.wait_send()
    py_out.wait_send()
    px_out.wait_send()
    pool_message(SIB_OWN, layer_at(z, c), sib).wait_send()
    for d in range(1, PLANES):
        @pl.when(up_sends(d))
        def _():
            up_out(d).wait_send()

        @pl.when(down_sends(d))
        def _():
            down_out(d).wait_send()

        @pl.when(from_below(d))
        def _():
            pool_message(SIB_UP + d - 1, layer_at(z - d, c), sib).wait_send()

        @pl.when(from_above(d))
        def _():
            pool_message(SIB_DOWN + d - 1, layer_at(z + d, c), sib).wait_send()


def relayed(queries, branch_key_value, branch_ids, pool, page_table):
    rows, heads, width = branch_key_value.shape
    wide = queries.shape[2]
    page_rows = pool.shape[1]
    block = lax.axis_index("seq") * 2 + lax.axis_index("head")
    own_ids = lax.dynamic_slice_in_dim(branch_ids, block * rows, rows, 0)
    starts = jnp.sum((branch_ids[None, :] < own_ids[:, None]).astype(jnp.int32), axis=1, keepdims=True)
    table = jnp.pad(page_table, ((0, 8 - page_table.shape[0]), (0, 128 - page_table.shape[1])))
    span = 3 * PLANE_BLOCKS * rows
    pool_keys = PLANES * 4 * page_rows
    vmem = pl.BlockSpec(memory_space=pltpu.VMEM)
    attended = pl.pallas_call(
        functools.partial(relay_kernel, page_table.shape[1]),
        out_shape=jax.ShapeDtypeStruct((heads, rows, wide), jnp.bfloat16),
        in_specs=[vmem] * 5,
        out_specs=vmem,
        scratch_shapes=[
            pltpu.VMEM((heads, 3 * PLANE_BLOCKS, rows, width), jnp.bfloat16),
            pltpu.VMEM((heads, pool_keys, width), jnp.bfloat16),
            pltpu.VMEM((2, 8, 128), jnp.int32),
            pltpu.VMEM((rows, span), jnp.float32),
            pltpu.VMEM((heads, 1, pool_keys), jnp.float32),
            pltpu.VMEM((wide // HEAD_DIM, rows, pool_keys + PLANE_BLOCKS * rows), jnp.float32),
            pltpu.VMEM((wide // HEAD_DIM, rows, pool_keys + PLANE_BLOCKS * rows), jnp.bfloat16),
            pltpu.VMEM((heads, rows * (wide // HEAD_DIM), 2 * HEAD_DIM), jnp.float32),
            pltpu.VMEM((heads, wide // HEAD_DIM, rows, HEAD_DIM), jnp.float32),
            pltpu.VMEM((wide // HEAD_DIM, rows, HEAD_DIM), jnp.float32),
            pltpu.SemaphoreType.DMA((8, 3, PIECES)),
            pltpu.SemaphoreType.DMA((8, 3, PIECES)),
            pltpu.SemaphoreType.DMA((16,)),
            pltpu.SemaphoreType.DMA((16,)),
        ],
        compiler_params=pltpu.CompilerParams(
            collective_id=0, has_side_effects=True, vmem_limit_bytes=48 * 2**20
        ),
        cost_estimate=pl.CostEstimate(
            flops=4 * rows * wide * (span + pool_keys) * heads,
            bytes_accessed=2 * 2 * heads * rows * wide,
            transcendentals=rows * heads * (wide // HEAD_DIM) * (span + pool_keys),
        ),
    )(
        jnp.swapaxes(queries, 0, 1),
        jnp.swapaxes(branch_key_value, 0, 1),
        starts,
        jnp.swapaxes(pool[0], 0, 1),
        table,
    )
    return jnp.swapaxes(attended, 0, 1)


def solution(mesh):
    small = mesh.shape["seq"] == PLANES * 4 and mesh.shape["head"] == 2
    return jax.shard_map(
        relayed if small else per_device,
        mesh=mesh,
        in_specs=(
            P(("seq", "head"), None, None),
            P(("seq", "head"), None, None),
            P(),
            P("seq", None, "head", None),
            P("head", None),
        ),
        out_specs=P(("seq", "head"), None, None),
        check_vma=False,
    )
```

```python
import functools

import jax
import jax.numpy as jnp
from jax import lax
from jax.experimental import pallas as pl
from jax.experimental.pallas import tpu as pltpu
from jax.sharding import PartitionSpec as P

HEAD_DIM = 128
MESH = pl.DeviceIdType.MESH

def passed_along(value, axis, by):
    count = lax.axis_size(axis)
    pairs = [(i, i + by) for i in range(count) if 0 <= i + by < count]
    return lax.ppermute(value, axis, pairs)


def blend_keys(state, query, pairs, allowed, scale):
    top, total, summed = state
    width = query.shape[-1]
    keys = pairs[..., :width]
    value_rows = pairs[..., width:]
    scores = jnp.einsum("rhgd,khd->rhgk", query, keys, preferred_element_type=jnp.float32) * scale
    scores = jnp.where(allowed, scores, -jnp.inf)
    new_top = jnp.maximum(top, jnp.max(scores, axis=-1))
    factor = jnp.exp(top - new_top)
    weights = jnp.exp(scores - new_top[..., None])
    total = total * factor + jnp.sum(weights, axis=-1)
    rounded = weights.astype(jnp.bfloat16)
    summed = summed * factor[..., None] + jnp.einsum(
        "rhgk,khd->rhgd", rounded, value_rows, preferred_element_type=jnp.float32
    )
    return (new_top, total, summed)


def per_device(queries, branch_key_value, branch_ids, pool, page_table):
    reach_count = min(32, lax.axis_size("seq") // 2)
    query, pairs = (
        lax.all_to_all(queries, "head", split_axis=1, concat_axis=0, tiled=True),
        lax.all_to_all(branch_key_value, "head", split_axis=1, concat_axis=0, tiled=True),
    )
    rows = query.shape[0]
    local_heads = query.shape[1]
    group = query.shape[2] // HEAD_DIM
    query = query.reshape(rows, local_heads, group, HEAD_DIM)
    scale = HEAD_DIM ** (-0.5)
    row_start = lax.axis_index("seq") * rows
    row_ids = jnp.arange(rows, dtype=jnp.int32)
    own_ids = lax.dynamic_slice_in_dim(branch_ids, row_start, rows, 0)
    own_rows = row_start + row_ids
    state = (
        jnp.full((rows, local_heads, group), -1e30, jnp.float32),
        jnp.zeros((rows, local_heads, group), jnp.float32),
        jnp.zeros((rows, local_heads, group, HEAD_DIM), jnp.float32),
    )
    page_rows = pool.shape[1]
    pair_width = pool.shape[3]
    piece = lax.all_gather(pool, "seq", axis=0, tiled=True)
    count = piece.shape[0]
    page_ids = jnp.arange(count, dtype=jnp.int32)
    chosen = jnp.any(page_table[:, :, None] == page_ids[None, None, :], axis=1)
    allowed = jnp.broadcast_to(chosen[:, :, None], (local_heads, count, page_rows))
    allowed = allowed.reshape(local_heads, count * page_rows)
    flat = piece.reshape(count * page_rows, local_heads, pair_width)

    def fold_in_piece(inner):
        return blend_keys(inner, query, flat, allowed[None, :, None, :], scale)

    def keep_state(inner):
        return inner

    state = lax.cond(jnp.any(chosen), fold_in_piece, keep_state, state)

    def causal_step(carry, block, back):
        key_start = row_start - back * rows
        key_ids = lax.dynamic_slice_in_dim(branch_ids, jnp.maximum(key_start, 0), rows, 0)
        key_rows = key_start + row_ids
        allowed = (
            (key_ids[None, :] == own_ids[:, None])
            & (key_rows[None, :] <= own_rows[:, None])
            & (key_start >= 0)
        )
        return blend_keys(carry, query, block, allowed[:, None, None, :], scale)

    state = causal_step(state, pairs, 0)
    for back in range(1, reach_count + 1):
        earlier = passed_along(pairs, "seq", back)
        state = causal_step(state, earlier, back)
    top, total, summed = state
    mixed = (
        (summed / total[..., None])
        .astype(jnp.bfloat16)
        .reshape(rows, local_heads, group * HEAD_DIM)
    )
    return lax.all_to_all(mixed, "head", split_axis=0, concat_axis=1, tiled=True)


PLANES = 4
PLANE_BLOCKS = 8
CHUNK = 16
PIECES = 4
KZ, KX, KY, KD, KSZ, KSX, KSY, KSD = range(8)


def relay_kernel(
    listed,
    query_ref, pairs_ref, start_ref, pool_ref, table_ref, out_ref,
    window, prefix, tables, bias, pool_bias, scores, weights,
    send_sem, recv_sem, pool_send, pool_recv,
):
    heads, rows, width = pairs_ref.shape
    page_rows = pool_ref.shape[1]
    piece = heads // PIECES
    seq = lax.axis_index("seq")
    y = lax.axis_index("head")
    z, x, c = seq // 4, (seq // 2) % 2, seq % 2
    place = x * 4 + c * 2 + y

    def device(dz=0, dx=0, dc=0, dy=0):
        nx = 1 - x if dx else x
        nc = 1 - c if dc else c
        ny = 1 - y if dy else y
        return (((z + dz) * 2 + nx) * 2 + nc, ny)

    up, down = device(dz=1), device(dz=-1)
    xn, yn, sib = device(dx=1), device(dy=1), device(dc=1)

    barrier = pltpu.get_barrier_semaphore()
    for other in (xn, yn, sib):
        pl.semaphore_signal(barrier, inc=1, device_id=other, device_id_type=MESH)

    @pl.when(z < PLANES - 1)
    def _():
        pl.semaphore_signal(barrier, inc=1, device_id=up, device_id_type=MESH)

    @pl.when(z > 0)
    def _():
        pl.semaphore_signal(barrier, inc=1, device_id=down, device_id_type=MESH)

    def block_at(k, bx, bc, by):
        return (2 - k) * PLANE_BLOCKS + bx * 4 + bc * 2 + by

    window[:, pl.ds(block_at(0, x, c, y), 1)] = pairs_ref[...][:, None]
    half = heads // 2
    own_page = pl.ds(pl.multiple_of(((c * PLANES + z) * 2 + x) * page_rows, page_rows), page_rows)
    prefix[pl.ds(y * half, half), own_page, :] = pool_ref[...]
    tables[pl.ds(y, 1)] = table_ref[...][None]

    pl.semaphore_wait(
        barrier, 3 + jnp.where(z < PLANES - 1, 1, 0) + jnp.where(z > 0, 1, 0)
    )

    def message(kind, k, j, k_from, bx, bc, by, target):
        part = pl.ds(j * piece, piece)
        return pltpu.make_async_remote_copy(
            src_ref=window.at[part, block_at(k_from, bx, bc, by)],
            dst_ref=window.at[part, block_at(k, bx, bc, by)],
            send_sem=send_sem.at[kind, k, j],
            recv_sem=recv_sem.at[kind, k, j],
            device_id=target,
            device_id_type=MESH,
        )

    source = {
        KZ: (x, c, y), KX: (x, c, y), KY: (x, c, y),
        KSZ: (x, c, y), KSX: (1 - x, c, y), KSY: (x, c, 1 - y), KSD: (1 - x, c, 1 - y),
    }
    landing = {
        KZ: (x, c, y), KX: (1 - x, c, y), KY: (x, c, 1 - y), KD: (1 - x, c, 1 - y),
        KSZ: (x, 1 - c, y), KSX: (1 - x, 1 - c, y),
        KSY: (x, 1 - c, 1 - y), KSD: (1 - x, 1 - c, 1 - y),
    }
    targets = {KZ: up, KX: xn, KY: yn, KSZ: sib, KSX: sib, KSY: sib, KSD: sib}

    def x_first(j):
        return j < PIECES // 2

    def outgoing(kind, k, j):
        return message(kind, k, j, k - 1 if kind == KZ else k, *source[kind], targets[kind])

    def corner_out(k, j, by_y):
        where, target = ((1 - x, c, y), yn) if by_y else ((x, c, 1 - y), xn)
        return message(KD, k, j, k, *where, target)

    def present(k):
        return z >= k

    def takes_x(k):
        if k == 0:
            return x == 1
        return present(k) if k == 1 else present(k) & (x == 0)

    def gives_x(k):
        if k == 0:
            return x == 0
        return present(k) if k == 1 else present(k) & (x == 1)

    def sends(kind, k):
        if kind == KZ:
            return (z < PLANES - 1) & (z >= k - 1)
        if kind == KX:
            return gives_x(k)
        if kind in (KY, KSZ, KSY):
            return present(k)
        return takes_x(k)

    def receives(kind, k):
        if kind in (KX, KD, KSX, KSD):
            return takes_x(k)
        return present(k)

    def corner_sends(k, j, by_y):
        return takes_x(k) & x_first(j) if by_y else gives_x(k) & jnp.logical_not(x_first(j))

    started = []

    def start(kind, k, j):
        started.append((kind, k))

        @pl.when(sends(kind, k))
        def _():
            outgoing(kind, k, j).start()

    def corner_start(k, j, by_y):
        @pl.when(corner_sends(k, j, by_y))
        def _():
            corner_out(k, j, by_y).start()

    def for_pieces(body):
        lax.fori_loop(0, PIECES, lambda j, carry: (body(j), carry)[1], 0)

    def arrived(kind, k, j):
        @pl.when(receives(kind, k))
        def _():
            message(kind, k, j, k, *landing[kind], sib).wait_recv()

    def pool_message(index, src, target):
        return pltpu.make_async_remote_copy(
            src_ref=src, dst_ref=src,
            send_sem=pool_send.at[index], recv_sem=pool_recv.at[index],
            device_id=target, device_id_type=MESH,
        )

    def layer_at(plane, layer):
        return prefix.at[
            :, pl.ds(pl.multiple_of((layer * PLANES + plane) * 2 * page_rows, 2 * page_rows), 2 * page_rows), :
        ]

    table_out = pool_message(0, tables.at[pl.ds(y, 1)], yn)
    table_in = pool_message(0, tables.at[pl.ds(1 - y, 1)], yn)
    py_out = pool_message(1, prefix.at[pl.ds(y * half, half), own_page, :], yn)
    py_in = pool_message(1, prefix.at[pl.ds((1 - y) * half, half), own_page, :], yn)
    x_page = pl.ds(pl.multiple_of(((c * PLANES + z) * 2 + 1 - x) * page_rows, page_rows), page_rows)
    px_out = pool_message(2, prefix.at[:, own_page, :], xn)
    px_in = pool_message(2, prefix.at[:, x_page, :], xn)
    UP, DOWN, SIB_UP, SIB_DOWN, SIB_OWN = 3, 6, 9, 12, 15

    def from_below(d):
        return z >= d

    def from_above(d):
        return z + d < PLANES

    def up_out(d):
        return pool_message(UP + d - 1, layer_at(z - d + 1, c), up)

    def down_out(d):
        return pool_message(DOWN + d - 1, layer_at(z + d - 1, c), down)

    def up_sends(d):
        return (z < PLANES - 1) & (z >= d - 1)

    def down_sends(d):
        return (z > 0) & (z + d - 1 < PLANES)

    def pool_start(d):
        @pl.when(up_sends(d))
        def _():
            up_out(d).start()

        @pl.when(down_sends(d))
        def _():
            down_out(d).start()

    def pool_arrived(d):
        @pl.when(from_below(d))
        def _():
            pool_message(UP + d - 1, layer_at(z - d, c), up).wait_recv()
            pool_message(SIB_UP + d - 1, layer_at(z - d, c), sib).start()

        @pl.when(from_above(d))
        def _():
            pool_message(DOWN + d - 1, layer_at(z + d, c), up).wait_recv()
            pool_message(SIB_DOWN + d - 1, layer_at(z + d, c), sib).start()

        if d < PLANES - 1:
            pool_start(d + 1)

    py_out.start()
    table_out.start()

    @for_pieces
    def _(j):
        for kind, k in ((KZ, 1), (KX, 0), (KY, 0), (KSZ, 0)):
            start(kind, k, j)

    plane_rows = PLANE_BLOCKS * rows

    @pl.when(z < 2)
    def _():
        window[:, :PLANE_BLOCKS] = jnp.zeros((heads, PLANE_BLOCKS, rows, width), window.dtype)

    @pl.when(z < 1)
    def _():
        window[:, PLANE_BLOCKS:2 * PLANE_BLOCKS] = jnp.zeros((heads, PLANE_BLOCKS, rows, width), window.dtype)

    span = bias.shape[1]
    column = lax.broadcasted_iota(jnp.int32, (rows, span), 1)
    row = lax.broadcasted_iota(jnp.int32, (rows, span), 0)
    base = (z * PLANE_BLOCKS + place) * rows - 2 * plane_rows
    seen = (column >= start_ref[...] - base) & (column <= row + 2 * plane_rows)
    bias[...] = jnp.where(seen, 0.0, -1e30)

    py_in.wait_recv()
    px_out.start()

    @for_pieces
    def _(j):
        arrived(KZ, 1, j)
        for kind, k in ((KZ, 2), (KX, 1), (KY, 1), (KSZ, 1)):
            start(kind, k, j)

    px_in.wait_recv()
    pool_start(1)
    pool_message(SIB_OWN, layer_at(z, c), sib).start()

    def cross(k, j):
        arrived(KX, k, j)
        corner_start(k, j, True)
        start(KSX, k, j)
        arrived(KY, k, j)
        corner_start(k, j, False)
        start(KSY, k, j)

    def corner(k, j):
        arrived(KD, k, j)
        start(KSD, k, j)

    @for_pieces
    def _(j):
        cross(0, j)

    @for_pieces
    def _(j):
        arrived(KZ, 2, j)
        for kind, k in ((KX, 2), (KY, 2), (KSZ, 2)):
            start(kind, k, j)

    pool_arrived(1)

    @for_pieces
    def _(j):
        cross(1, j)
        corner(0, j)

    pool_arrived(2)

    @for_pieces
    def _(j):
        cross(2, j)
        corner(1, j)

    pool_arrived(3)

    @for_pieces
    def _(j):
        corner(2, j)

    table_in.wait_recv()
    pages = PLANES * 4
    keys = pages * page_rows
    slot = lax.broadcasted_iota(jnp.int32, (8, keys), 1) // page_rows
    page = (slot % (pages // 2)) * 2 + slot // (pages // 2)
    for side in range(2):
        table = tables[side]
        chosen = table[:, 0:1] == page
        for i in range(1, listed):
            chosen = chosen | (table[:, i:i + 1] == page)
        mask = jnp.where(chosen, 0.0, -1e30)
        for i in range(half):
            pool_bias[side * half + i] = mask[i:i + 1]

    for d in range(1, PLANES):
        @pl.when(from_below(d))
        def _():
            pool_message(SIB_UP + d - 1, layer_at(z - d, 1 - c), sib).wait_recv()

        @pl.when(from_above(d))
        def _():
            pool_message(SIB_DOWN + d - 1, layer_at(z + d, 1 - c), sib).wait_recv()
    pool_message(SIB_OWN, layer_at(z, 1 - c), sib).wait_recv()

    @for_pieces
    def _(j):
        for k in range(3):
            for kind in (KSZ, KSX, KSY, KSD):
                arrived(kind, k, j)

    factor = HEAD_DIM ** (-0.5) * 1.4426950408889634
    group = query_ref.shape[2] // HEAD_DIM
    contract = (((1,), (1,)), ((), ()))
    count = keys + span

    def pairs_of(h):
        near = window[h, pl.ds(place, 2 * PLANE_BLOCKS + 1)].reshape(span, width)
        return jnp.concatenate([prefix[h], near], axis=0)

    def score(h, lane):
        queries = query_ref[h]
        query = jnp.concatenate(
            [queries[:, g * HEAD_DIM:(g + 1) * HEAD_DIM] for g in range(group)], axis=0
        )
        scores[lane] = lax.dot_general(
            query, pairs_of(h)[:, :HEAD_DIM], contract, preferred_element_type=jnp.float32
        )

    def soften(h, lane):
        for r in range(0, rows, CHUNK):
            mask = bias[r:r + CHUNK, :]
            for g in range(group):
                own = slice(g * rows + r, g * rows + r + CHUNK)
                pool_scores = scores[lane, own, :keys] + pool_bias[h]
                near_scores = scores[lane, own, keys:] + mask
                top = factor * jnp.maximum(
                    jnp.max(pool_scores, axis=1, keepdims=True), jnp.max(near_scores, axis=1, keepdims=True)
                )
                weights[lane, own, :keys] = jnp.exp2(pool_scores * factor - top).astype(jnp.bfloat16)
                weights[lane, own, keys:] = jnp.exp2(near_scores * factor - top).astype(jnp.bfloat16)

    def mix(h, lane):
        values = jnp.concatenate(
            [pairs_of(h)[:, HEAD_DIM:], jnp.ones((count, HEAD_DIM), jnp.bfloat16)], axis=1
        )
        mixed = jnp.dot(weights[lane], values, preferred_element_type=jnp.float32)
        result = (mixed[:, :HEAD_DIM] / mixed[:, HEAD_DIM:]).astype(out_ref.dtype)
        for g in range(group):
            out_ref[h, :, g * HEAD_DIM:(g + 1) * HEAD_DIM] = result[g * rows:(g + 1) * rows]

    score(0, 0)

    def two_heads(i, carry):
        h = 2 * i
        score(h + 1, 1)
        soften(h, 0)
        mix(h, 0)
        score(jnp.minimum(h + 2, heads - 1), 0)
        soften(h + 1, 1)
        mix(h + 1, 1)
        return carry

    lax.fori_loop(0, heads // 2, two_heads, 0)

    @for_pieces
    def _(j):
        for kind, k in started:
            @pl.when(sends(kind, k))
            def _():
                outgoing(kind, k, j).wait_send()

        for k in range(3):
            for by_y in (True, False):
                @pl.when(corner_sends(k, j, by_y))
                def _():
                    corner_out(k, j, by_y).wait_send()

    table_out.wait_send()
    py_out.wait_send()
    px_out.wait_send()
    pool_message(SIB_OWN, layer_at(z, c), sib).wait_send()
    for d in range(1, PLANES):
        @pl.when(up_sends(d))
        def _():
            up_out(d).wait_send()

        @pl.when(down_sends(d))
        def _():
            down_out(d).wait_send()

        @pl.when(from_below(d))
        def _():
            pool_message(SIB_UP + d - 1, layer_at(z - d, c), sib).wait_send()

        @pl.when(from_above(d))
        def _():
            pool_message(SIB_DOWN + d - 1, layer_at(z + d, c), sib).wait_send()


def relayed(queries, branch_key_value, branch_ids, pool, page_table):
    rows, heads, width = branch_key_value.shape
    wide = queries.shape[2]
    page_rows = pool.shape[1]
    block = lax.axis_index("seq") * 2 + lax.axis_index("head")
    own_ids = lax.dynamic_slice_in_dim(branch_ids, block * rows, rows, 0)
    starts = jnp.sum((branch_ids[None, :] < own_ids[:, None]).astype(jnp.int32), axis=1, keepdims=True)
    table = jnp.pad(page_table, ((0, 8 - page_table.shape[0]), (0, 128 - page_table.shape[1])))
    span = 2 * PLANE_BLOCKS * rows + rows
    pool_keys = PLANES * 4 * page_rows
    vmem = pl.BlockSpec(memory_space=pltpu.VMEM)
    attended = pl.pallas_call(
        functools.partial(relay_kernel, page_table.shape[1]),
        out_shape=jax.ShapeDtypeStruct((heads, rows, wide), jnp.bfloat16),
        in_specs=[vmem] * 5,
        out_specs=vmem,
        scratch_shapes=[
            pltpu.VMEM((heads, 3 * PLANE_BLOCKS, rows, width), jnp.bfloat16),
            pltpu.VMEM((heads, pool_keys, width), jnp.bfloat16),
            pltpu.VMEM((2, 8, 128), jnp.int32),
            pltpu.VMEM((rows, span), jnp.float32),
            pltpu.VMEM((heads, 1, pool_keys), jnp.float32),
            pltpu.VMEM((2, rows * (wide // HEAD_DIM), pool_keys + span), jnp.float32),
            pltpu.VMEM((2, rows * (wide // HEAD_DIM), pool_keys + span), jnp.bfloat16),
            pltpu.SemaphoreType.DMA((8, 3, PIECES)),
            pltpu.SemaphoreType.DMA((8, 3, PIECES)),
            pltpu.SemaphoreType.DMA((16,)),
            pltpu.SemaphoreType.DMA((16,)),
        ],
        compiler_params=pltpu.CompilerParams(
            collective_id=0, has_side_effects=True, vmem_limit_bytes=48 * 2**20
        ),
        cost_estimate=pl.CostEstimate(
            flops=4 * rows * wide * (span + pool_keys) * heads,
            bytes_accessed=2 * 2 * heads * rows * wide,
            transcendentals=rows * heads * (wide // HEAD_DIM) * (span + pool_keys),
        ),
    )(
        jnp.swapaxes(queries, 0, 1),
        jnp.swapaxes(branch_key_value, 0, 1),
        starts,
        jnp.swapaxes(pool[0], 0, 1),
        table,
    )
    return jnp.swapaxes(attended, 0, 1)


def solution(mesh):
    small = mesh.shape["seq"] == PLANES * 4 and mesh.shape["head"] == 2
    return jax.shard_map(
        relayed if small else per_device,
        mesh=mesh,
        in_specs=(
            P(("seq", "head"), None, None),
            P(("seq", "head"), None, None),
            P(),
            P("seq", None, "head", None),
            P("head", None),
        ),
        out_specs=P(("seq", "head"), None, None),
        check_vma=False,
    )
```

```python
import functools

import jax
import jax.numpy as jnp
from jax import lax
from jax.experimental import pallas as pl
from jax.experimental.pallas import tpu as pltpu
from jax.sharding import PartitionSpec as P

HEAD_DIM = 128
MESH = pl.DeviceIdType.MESH

def passed_along(value, axis, by):
    count = lax.axis_size(axis)
    pairs = [(i, i + by) for i in range(count) if 0 <= i + by < count]
    return lax.ppermute(value, axis, pairs)


def blend_keys(state, query, pairs, allowed, scale):
    top, total, summed = state
    width = query.shape[-1]
    keys = pairs[..., :width]
    value_rows = pairs[..., width:]
    scores = jnp.einsum("rhgd,khd->rhgk", query, keys, preferred_element_type=jnp.float32) * scale
    scores = jnp.where(allowed, scores, -jnp.inf)
    new_top = jnp.maximum(top, jnp.max(scores, axis=-1))
    factor = jnp.exp(top - new_top)
    weights = jnp.exp(scores - new_top[..., None])
    total = total * factor + jnp.sum(weights, axis=-1)
    rounded = weights.astype(jnp.bfloat16)
    summed = summed * factor[..., None] + jnp.einsum(
        "rhgk,khd->rhgd", rounded, value_rows, preferred_element_type=jnp.float32
    )
    return (new_top, total, summed)


def per_device(queries, branch_key_value, branch_ids, pool, page_table):
    reach_count = min(32, lax.axis_size("seq") // 2)
    query, pairs = (
        lax.all_to_all(queries, "head", split_axis=1, concat_axis=0, tiled=True),
        lax.all_to_all(branch_key_value, "head", split_axis=1, concat_axis=0, tiled=True),
    )
    rows = query.shape[0]
    local_heads = query.shape[1]
    group = query.shape[2] // HEAD_DIM
    query = query.reshape(rows, local_heads, group, HEAD_DIM)
    scale = HEAD_DIM ** (-0.5)
    row_start = lax.axis_index("seq") * rows
    row_ids = jnp.arange(rows, dtype=jnp.int32)
    own_ids = lax.dynamic_slice_in_dim(branch_ids, row_start, rows, 0)
    own_rows = row_start + row_ids
    state = (
        jnp.full((rows, local_heads, group), -1e30, jnp.float32),
        jnp.zeros((rows, local_heads, group), jnp.float32),
        jnp.zeros((rows, local_heads, group, HEAD_DIM), jnp.float32),
    )
    page_rows = pool.shape[1]
    pair_width = pool.shape[3]
    piece = lax.all_gather(pool, "seq", axis=0, tiled=True)
    count = piece.shape[0]
    page_ids = jnp.arange(count, dtype=jnp.int32)
    chosen = jnp.any(page_table[:, :, None] == page_ids[None, None, :], axis=1)
    allowed = jnp.broadcast_to(chosen[:, :, None], (local_heads, count, page_rows))
    allowed = allowed.reshape(local_heads, count * page_rows)
    flat = piece.reshape(count * page_rows, local_heads, pair_width)

    def fold_in_piece(inner):
        return blend_keys(inner, query, flat, allowed[None, :, None, :], scale)

    def keep_state(inner):
        return inner

    state = lax.cond(jnp.any(chosen), fold_in_piece, keep_state, state)

    def causal_step(carry, block, back):
        key_start = row_start - back * rows
        key_ids = lax.dynamic_slice_in_dim(branch_ids, jnp.maximum(key_start, 0), rows, 0)
        key_rows = key_start + row_ids
        allowed = (
            (key_ids[None, :] == own_ids[:, None])
            & (key_rows[None, :] <= own_rows[:, None])
            & (key_start >= 0)
        )
        return blend_keys(carry, query, block, allowed[:, None, None, :], scale)

    state = causal_step(state, pairs, 0)
    for back in range(1, reach_count + 1):
        earlier = passed_along(pairs, "seq", back)
        state = causal_step(state, earlier, back)
    top, total, summed = state
    mixed = (
        (summed / total[..., None])
        .astype(jnp.bfloat16)
        .reshape(rows, local_heads, group * HEAD_DIM)
    )
    return lax.all_to_all(mixed, "head", split_axis=0, concat_axis=1, tiled=True)


PLANES = 4
PLANE_BLOCKS = 8
CHUNK = 16
PIECES = 4
KZ, KX, KY, KD, KSZ, KSX, KSY, KSD = range(8)


def relay_kernel(
    listed,
    query_ref, pairs_ref, start_ref, pool_ref, table_ref, out_ref,
    window, prefix, tables, bias, pool_bias, scores, weights,
    send_sem, recv_sem, pool_send, pool_recv,
):
    heads, rows, width = pairs_ref.shape
    page_rows = pool_ref.shape[1]
    piece = heads // PIECES
    seq = lax.axis_index("seq")
    y = lax.axis_index("head")
    z, x, c = seq // 4, (seq // 2) % 2, seq % 2
    place = x * 4 + c * 2 + y

    def device(dz=0, dx=0, dc=0, dy=0):
        nx = 1 - x if dx else x
        nc = 1 - c if dc else c
        ny = 1 - y if dy else y
        return (((z + dz) * 2 + nx) * 2 + nc, ny)

    up, down = device(dz=1), device(dz=-1)
    xn, yn, sib = device(dx=1), device(dy=1), device(dc=1)

    barrier = pltpu.get_barrier_semaphore()
    for other in (xn, yn, sib):
        pl.semaphore_signal(barrier, inc=1, device_id=other, device_id_type=MESH)

    @pl.when(z < PLANES - 1)
    def _():
        pl.semaphore_signal(barrier, inc=1, device_id=up, device_id_type=MESH)

    @pl.when(z > 0)
    def _():
        pl.semaphore_signal(barrier, inc=1, device_id=down, device_id_type=MESH)

    def block_at(k, bx, bc, by):
        return (2 - k) * PLANE_BLOCKS + bx * 4 + bc * 2 + by

    window[:, pl.ds(block_at(0, x, c, y), 1)] = pairs_ref[...][:, None]
    half = heads // 2
    own_page = pl.ds(pl.multiple_of(((c * PLANES + z) * 2 + x) * page_rows, page_rows), page_rows)
    prefix[pl.ds(y * half, half), own_page, :] = pool_ref[...]
    tables[pl.ds(y, 1)] = table_ref[...][None]

    pl.semaphore_wait(
        barrier, 3 + jnp.where(z < PLANES - 1, 1, 0) + jnp.where(z > 0, 1, 0)
    )

    def message(kind, k, j, k_from, bx, bc, by, target):
        part = pl.ds(j * piece, piece)
        return pltpu.make_async_remote_copy(
            src_ref=window.at[part, block_at(k_from, bx, bc, by)],
            dst_ref=window.at[part, block_at(k, bx, bc, by)],
            send_sem=send_sem.at[kind, k, j],
            recv_sem=recv_sem.at[kind, k, j],
            device_id=target,
            device_id_type=MESH,
        )

    source = {
        KZ: (x, c, y), KX: (x, c, y), KY: (x, c, y),
        KSZ: (x, c, y), KSX: (1 - x, c, y), KSY: (x, c, 1 - y), KSD: (1 - x, c, 1 - y),
    }
    landing = {
        KZ: (x, c, y), KX: (1 - x, c, y), KY: (x, c, 1 - y), KD: (1 - x, c, 1 - y),
        KSZ: (x, 1 - c, y), KSX: (1 - x, 1 - c, y),
        KSY: (x, 1 - c, 1 - y), KSD: (1 - x, 1 - c, 1 - y),
    }
    targets = {KZ: up, KX: xn, KY: yn, KSZ: sib, KSX: sib, KSY: sib, KSD: sib}

    def x_first(j):
        return j < PIECES // 2

    def outgoing(kind, k, j):
        return message(kind, k, j, k - 1 if kind == KZ else k, *source[kind], targets[kind])

    def corner_out(k, j, by_y):
        where, target = ((1 - x, c, y), yn) if by_y else ((x, c, 1 - y), xn)
        return message(KD, k, j, k, *where, target)

    def present(k):
        return z >= k

    def takes_x(k):
        if k == 0:
            return x == 1
        return present(k) if k == 1 else present(k) & (x == 0)

    def gives_x(k):
        if k == 0:
            return x == 0
        return present(k) if k == 1 else present(k) & (x == 1)

    def sends(kind, k):
        if kind == KZ:
            return (z < PLANES - 1) & (z >= k - 1)
        if kind == KX:
            return gives_x(k)
        if kind in (KY, KSZ, KSY):
            return present(k)
        return takes_x(k)

    def receives(kind, k):
        if kind in (KX, KD, KSX, KSD):
            return takes_x(k)
        return present(k)

    def corner_sends(k, j, by_y):
        if k != 1:
            return gives_x(k)
        return takes_x(k) & x_first(j) if by_y else gives_x(k) & jnp.logical_not(x_first(j))

    started = []

    def start(kind, k, j):
        started.append((kind, k))

        @pl.when(sends(kind, k))
        def _():
            outgoing(kind, k, j).start()

    def corner_start(k, j, by_y):
        @pl.when(corner_sends(k, j, by_y))
        def _():
            corner_out(k, j, by_y).start()

    def for_pieces(body):
        lax.fori_loop(0, PIECES, lambda j, carry: (body(j), carry)[1], 0)

    def arrived(kind, k, j):
        @pl.when(receives(kind, k))
        def _():
            message(kind, k, j, k, *landing[kind], sib).wait_recv()

    def pool_message(index, src, target):
        return pltpu.make_async_remote_copy(
            src_ref=src, dst_ref=src,
            send_sem=pool_send.at[index], recv_sem=pool_recv.at[index],
            device_id=target, device_id_type=MESH,
        )

    def layer_at(plane, layer):
        return prefix.at[
            :, pl.ds(pl.multiple_of((layer * PLANES + plane) * 2 * page_rows, 2 * page_rows), 2 * page_rows), :
        ]

    table_out = pool_message(0, tables.at[pl.ds(y, 1)], yn)
    table_in = pool_message(0, tables.at[pl.ds(1 - y, 1)], yn)
    py_out = pool_message(1, prefix.at[pl.ds(y * half, half), own_page, :], yn)
    py_in = pool_message(1, prefix.at[pl.ds((1 - y) * half, half), own_page, :], yn)
    x_page = pl.ds(pl.multiple_of(((c * PLANES + z) * 2 + 1 - x) * page_rows, page_rows), page_rows)
    px_out = pool_message(2, prefix.at[:, own_page, :], xn)
    px_in = pool_message(2, prefix.at[:, x_page, :], xn)
    UP, DOWN, SIB_UP, SIB_DOWN, SIB_OWN = 3, 6, 9, 12, 15

    def from_below(d):
        return z >= d

    def from_above(d):
        return z + d < PLANES

    def up_out(d):
        return pool_message(UP + d - 1, layer_at(z - d + 1, c), up)

    def down_out(d):
        return pool_message(DOWN + d - 1, layer_at(z + d - 1, c), down)

    def up_sends(d):
        return (z < PLANES - 1) & (z >= d - 1)

    def down_sends(d):
        return (z > 0) & (z + d - 1 < PLANES)

    def pool_start(d):
        @pl.when(up_sends(d))
        def _():
            up_out(d).start()

        @pl.when(down_sends(d))
        def _():
            down_out(d).start()

    def pool_arrived(d):
        @pl.when(from_below(d))
        def _():
            pool_message(UP + d - 1, layer_at(z - d, c), up).wait_recv()
            pool_message(SIB_UP + d - 1, layer_at(z - d, c), sib).start()

        @pl.when(from_above(d))
        def _():
            pool_message(DOWN + d - 1, layer_at(z + d, c), up).wait_recv()
            pool_message(SIB_DOWN + d - 1, layer_at(z + d, c), sib).start()

        if d < PLANES - 1:
            pool_start(d + 1)

    py_out.start()
    table_out.start()

    @for_pieces
    def _(j):
        for kind, k in ((KZ, 1), (KX, 0), (KY, 0), (KSZ, 0)):
            start(kind, k, j)

    plane_rows = PLANE_BLOCKS * rows

    @pl.when(z < 2)
    def _():
        window[:, :PLANE_BLOCKS] = jnp.zeros((heads, PLANE_BLOCKS, rows, width), window.dtype)

    @pl.when(z < 1)
    def _():
        window[:, PLANE_BLOCKS:2 * PLANE_BLOCKS] = jnp.zeros((heads, PLANE_BLOCKS, rows, width), window.dtype)

    span = bias.shape[1]
    column = lax.broadcasted_iota(jnp.int32, (rows, span), 1)
    row = lax.broadcasted_iota(jnp.int32, (rows, span), 0)
    base = (z * PLANE_BLOCKS + place) * rows - 2 * plane_rows
    seen = (column >= start_ref[...] - base) & (column <= row + 2 * plane_rows)
    bias[...] = jnp.where(seen, 0.0, -1e30)

    py_in.wait_recv()
    px_out.start()

    @for_pieces
    def _(j):
        arrived(KZ, 1, j)
        for kind, k in ((KZ, 2), (KX, 1), (KY, 1), (KSZ, 1)):
            start(kind, k, j)

    px_in.wait_recv()
    pool_start(1)
    pool_message(SIB_OWN, layer_at(z, c), sib).start()

    def cross(k, j):
        if k == 1:
            arrived(KX, k, j)
            corner_start(k, j, True)
            start(KSX, k, j)
        arrived(KY, k, j)
        corner_start(k, j, False)
        start(KSY, k, j)
        if k != 1:
            arrived(KX, k, j)
            start(KSX, k, j)

    def corner(k, j):
        arrived(KD, k, j)
        start(KSD, k, j)

    @for_pieces
    def _(j):
        cross(0, j)

    @for_pieces
    def _(j):
        arrived(KZ, 2, j)
        for kind, k in ((KX, 2), (KY, 2), (KSZ, 2)):
            start(kind, k, j)

    pool_arrived(1)

    @for_pieces
    def _(j):
        cross(1, j)
        corner(0, j)

    pool_arrived(2)

    @for_pieces
    def _(j):
        cross(2, j)
        corner(1, j)

    pool_arrived(3)

    @for_pieces
    def _(j):
        corner(2, j)

    table_in.wait_recv()
    pages = PLANES * 4
    keys = pages * page_rows
    slot = lax.broadcasted_iota(jnp.int32, (8, keys), 1) // page_rows
    page = (slot % (pages // 2)) * 2 + slot // (pages // 2)
    for side in range(2):
        table = tables[side]
        chosen = table[:, 0:1] == page
        for i in range(1, listed):
            chosen = chosen | (table[:, i:i + 1] == page)
        mask = jnp.where(chosen, 0.0, -1e30)
        for i in range(half):
            pool_bias[side * half + i] = mask[i:i + 1]

    for d in range(1, PLANES):
        @pl.when(from_below(d))
        def _():
            pool_message(SIB_UP + d - 1, layer_at(z - d, 1 - c), sib).wait_recv()

        @pl.when(from_above(d))
        def _():
            pool_message(SIB_DOWN + d - 1, layer_at(z + d, 1 - c), sib).wait_recv()
    pool_message(SIB_OWN, layer_at(z, 1 - c), sib).wait_recv()

    @for_pieces
    def _(j):
        for k in range(3):
            for kind in (KSZ, KSX, KSY, KSD):
                arrived(kind, k, j)

    factor = HEAD_DIM ** (-0.5) * 1.4426950408889634
    group = query_ref.shape[2] // HEAD_DIM
    contract = (((1,), (1,)), ((), ()))
    count = keys + span

    def pairs_of(h):
        near = window[h, pl.ds(place, 2 * PLANE_BLOCKS + 1)].reshape(span, width)
        return jnp.concatenate([prefix[h], near], axis=0)

    def score(h, lane):
        queries = query_ref[h]
        query = jnp.concatenate(
            [queries[:, g * HEAD_DIM:(g + 1) * HEAD_DIM] for g in range(group)], axis=0
        )
        scores[lane] = lax.dot_general(
            query, pairs_of(h)[:, :HEAD_DIM], contract, preferred_element_type=jnp.float32
        )

    def soften(h, lane):
        for r in range(0, rows, CHUNK):
            mask = bias[r:r + CHUNK, :]
            for g in range(group):
                own = slice(g * rows + r, g * rows + r + CHUNK)
                pool_scores = scores[lane, own, :keys] + pool_bias[h]
                near_scores = scores[lane, own, keys:] + mask
                top = factor * jnp.maximum(
                    jnp.max(pool_scores, axis=1, keepdims=True), jnp.max(near_scores, axis=1, keepdims=True)
                )
                weights[lane, own, :keys] = jnp.exp2(pool_scores * factor - top).astype(jnp.bfloat16)
                weights[lane, own, keys:] = jnp.exp2(near_scores * factor - top).astype(jnp.bfloat16)

    def mix(h, lane):
        values = jnp.concatenate(
            [pairs_of(h)[:, HEAD_DIM:], jnp.ones((count, HEAD_DIM), jnp.bfloat16)], axis=1
        )
        mixed = jnp.dot(weights[lane], values, preferred_element_type=jnp.float32)
        result = (mixed[:, :HEAD_DIM] / mixed[:, HEAD_DIM:]).astype(out_ref.dtype)
        for g in range(group):
            out_ref[h, :, g * HEAD_DIM:(g + 1) * HEAD_DIM] = result[g * rows:(g + 1) * rows]

    score(0, 0)

    def two_heads(i, carry):
        h = 2 * i
        score(h + 1, 1)
        soften(h, 0)
        mix(h, 0)
        score(jnp.minimum(h + 2, heads - 1), 0)
        soften(h + 1, 1)
        mix(h + 1, 1)
        return carry

    lax.fori_loop(0, heads // 2, two_heads, 0)

    @for_pieces
    def _(j):
        for kind, k in started:
            @pl.when(sends(kind, k))
            def _():
                outgoing(kind, k, j).wait_send()

        for k in range(3):
            for by_y in (True, False) if k == 1 else (False,):
                @pl.when(corner_sends(k, j, by_y))
                def _():
                    corner_out(k, j, by_y).wait_send()

    table_out.wait_send()
    py_out.wait_send()
    px_out.wait_send()
    pool_message(SIB_OWN, layer_at(z, c), sib).wait_send()
    for d in range(1, PLANES):
        @pl.when(up_sends(d))
        def _():
            up_out(d).wait_send()

        @pl.when(down_sends(d))
        def _():
            down_out(d).wait_send()

        @pl.when(from_below(d))
        def _():
            pool_message(SIB_UP + d - 1, layer_at(z - d, c), sib).wait_send()

        @pl.when(from_above(d))
        def _():
            pool_message(SIB_DOWN + d - 1, layer_at(z + d, c), sib).wait_send()


def relayed(queries, branch_key_value, branch_ids, pool, page_table):
    rows, heads, width = branch_key_value.shape
    wide = queries.shape[2]
    page_rows = pool.shape[1]
    block = lax.axis_index("seq") * 2 + lax.axis_index("head")
    own_ids = lax.dynamic_slice_in_dim(branch_ids, block * rows, rows, 0)
    starts = jnp.sum((branch_ids[None, :] < own_ids[:, None]).astype(jnp.int32), axis=1, keepdims=True)
    table = jnp.pad(page_table, ((0, 8 - page_table.shape[0]), (0, 128 - page_table.shape[1])))
    span = 2 * PLANE_BLOCKS * rows + rows
    pool_keys = PLANES * 4 * page_rows
    vmem = pl.BlockSpec(memory_space=pltpu.VMEM)
    attended = pl.pallas_call(
        functools.partial(relay_kernel, page_table.shape[1]),
        out_shape=jax.ShapeDtypeStruct((heads, rows, wide), jnp.bfloat16),
        in_specs=[vmem] * 5,
        out_specs=vmem,
        scratch_shapes=[
            pltpu.VMEM((heads, 3 * PLANE_BLOCKS, rows, width), jnp.bfloat16),
            pltpu.VMEM((heads, pool_keys, width), jnp.bfloat16),
            pltpu.VMEM((2, 8, 128), jnp.int32),
            pltpu.VMEM((rows, span), jnp.float32),
            pltpu.VMEM((heads, 1, pool_keys), jnp.float32),
            pltpu.VMEM((2, rows * (wide // HEAD_DIM), pool_keys + span), jnp.float32),
            pltpu.VMEM((2, rows * (wide // HEAD_DIM), pool_keys + span), jnp.bfloat16),
            pltpu.SemaphoreType.DMA((8, 3, PIECES)),
            pltpu.SemaphoreType.DMA((8, 3, PIECES)),
            pltpu.SemaphoreType.DMA((16,)),
            pltpu.SemaphoreType.DMA((16,)),
        ],
        compiler_params=pltpu.CompilerParams(
            collective_id=0, has_side_effects=True, vmem_limit_bytes=48 * 2**20
        ),
        cost_estimate=pl.CostEstimate(
            flops=4 * rows * wide * (span + pool_keys) * heads,
            bytes_accessed=2 * 2 * heads * rows * wide,
            transcendentals=rows * heads * (wide // HEAD_DIM) * (span + pool_keys),
        ),
    )(
        jnp.swapaxes(queries, 0, 1),
        jnp.swapaxes(branch_key_value, 0, 1),
        starts,
        jnp.swapaxes(pool[0], 0, 1),
        table,
    )
    return jnp.swapaxes(attended, 0, 1)


def solution(mesh):
    small = mesh.shape["seq"] == PLANES * 4 and mesh.shape["head"] == 2
    return jax.shard_map(
        relayed if small else per_device,
        mesh=mesh,
        in_specs=(
            P(("seq", "head"), None, None),
            P(("seq", "head"), None, None),
            P(),
            P("seq", None, "head", None),
            P("head", None),
        ),
        out_specs=P(("seq", "head"), None, None),
        check_vma=False,
    )
```

```python
import functools

import jax
import jax.numpy as jnp
from jax import lax
from jax.experimental import pallas as pl
from jax.experimental.pallas import tpu as pltpu
from jax.sharding import PartitionSpec as P

HEAD_DIM = 128
MESH = pl.DeviceIdType.MESH

def passed_along(value, axis, by):
    count = lax.axis_size(axis)
    pairs = [(i, i + by) for i in range(count) if 0 <= i + by < count]
    return lax.ppermute(value, axis, pairs)


def blend_keys(state, query, pairs, allowed, scale):
    top, total, summed = state
    width = query.shape[-1]
    keys = pairs[..., :width]
    value_rows = pairs[..., width:]
    scores = jnp.einsum("rhgd,khd->rhgk", query, keys, preferred_element_type=jnp.float32) * scale
    scores = jnp.where(allowed, scores, -jnp.inf)
    new_top = jnp.maximum(top, jnp.max(scores, axis=-1))
    factor = jnp.exp(top - new_top)
    weights = jnp.exp(scores - new_top[..., None])
    total = total * factor + jnp.sum(weights, axis=-1)
    rounded = weights.astype(jnp.bfloat16)
    summed = summed * factor[..., None] + jnp.einsum(
        "rhgk,khd->rhgd", rounded, value_rows, preferred_element_type=jnp.float32
    )
    return (new_top, total, summed)


def per_device(queries, branch_key_value, branch_ids, pool, page_table):
    reach_count = min(32, lax.axis_size("seq") // 2)
    query, pairs = (
        lax.all_to_all(queries, "head", split_axis=1, concat_axis=0, tiled=True),
        lax.all_to_all(branch_key_value, "head", split_axis=1, concat_axis=0, tiled=True),
    )
    rows = query.shape[0]
    local_heads = query.shape[1]
    group = query.shape[2] // HEAD_DIM
    query = query.reshape(rows, local_heads, group, HEAD_DIM)
    scale = HEAD_DIM ** (-0.5)
    row_start = lax.axis_index("seq") * rows
    row_ids = jnp.arange(rows, dtype=jnp.int32)
    own_ids = lax.dynamic_slice_in_dim(branch_ids, row_start, rows, 0)
    own_rows = row_start + row_ids
    state = (
        jnp.full((rows, local_heads, group), -1e30, jnp.float32),
        jnp.zeros((rows, local_heads, group), jnp.float32),
        jnp.zeros((rows, local_heads, group, HEAD_DIM), jnp.float32),
    )
    page_rows = pool.shape[1]
    pair_width = pool.shape[3]
    piece = lax.all_gather(pool, "seq", axis=0, tiled=True)
    count = piece.shape[0]
    page_ids = jnp.arange(count, dtype=jnp.int32)
    chosen = jnp.any(page_table[:, :, None] == page_ids[None, None, :], axis=1)
    allowed = jnp.broadcast_to(chosen[:, :, None], (local_heads, count, page_rows))
    allowed = allowed.reshape(local_heads, count * page_rows)
    flat = piece.reshape(count * page_rows, local_heads, pair_width)

    def fold_in_piece(inner):
        return blend_keys(inner, query, flat, allowed[None, :, None, :], scale)

    def keep_state(inner):
        return inner

    state = lax.cond(jnp.any(chosen), fold_in_piece, keep_state, state)

    def causal_step(carry, block, back):
        key_start = row_start - back * rows
        key_ids = lax.dynamic_slice_in_dim(branch_ids, jnp.maximum(key_start, 0), rows, 0)
        key_rows = key_start + row_ids
        allowed = (
            (key_ids[None, :] == own_ids[:, None])
            & (key_rows[None, :] <= own_rows[:, None])
            & (key_start >= 0)
        )
        return blend_keys(carry, query, block, allowed[:, None, None, :], scale)

    state = causal_step(state, pairs, 0)
    for back in range(1, reach_count + 1):
        earlier = passed_along(pairs, "seq", back)
        state = causal_step(state, earlier, back)
    top, total, summed = state
    mixed = (
        (summed / total[..., None])
        .astype(jnp.bfloat16)
        .reshape(rows, local_heads, group * HEAD_DIM)
    )
    return lax.all_to_all(mixed, "head", split_axis=0, concat_axis=1, tiled=True)


PLANES = 4
PLANE_BLOCKS = 8
CHUNK = 16
PIECES = 4
KZ, KX, KY, KD, KSZ, KSX, KSY, KSD = range(8)


def relay_kernel(
    listed,
    query_ref, pairs_ref, start_ref, pool_ref, table_ref, out_ref,
    window, prefix, tables, bias, pool_bias, scores, weights,
    send_sem, recv_sem, pool_send, pool_recv,
):
    heads, rows, width = pairs_ref.shape
    page_rows = pool_ref.shape[1]
    piece = heads // PIECES
    seq = lax.axis_index("seq")
    y = lax.axis_index("head")
    z, x, c = seq // 4, (seq // 2) % 2, seq % 2
    place = x * 4 + c * 2 + y

    def device(dz=0, dx=0, dc=0, dy=0):
        nx = 1 - x if dx else x
        nc = 1 - c if dc else c
        ny = 1 - y if dy else y
        return (((z + dz) * 2 + nx) * 2 + nc, ny)

    up, down = device(dz=1), device(dz=-1)
    xn, yn, sib = device(dx=1), device(dy=1), device(dc=1)

    barrier = pltpu.get_barrier_semaphore()
    for other in (xn, yn, sib):
        pl.semaphore_signal(barrier, inc=1, device_id=other, device_id_type=MESH)

    @pl.when(z < PLANES - 1)
    def _():
        pl.semaphore_signal(barrier, inc=1, device_id=up, device_id_type=MESH)

    @pl.when(z > 0)
    def _():
        pl.semaphore_signal(barrier, inc=1, device_id=down, device_id_type=MESH)

    def block_at(k, bx, bc, by):
        return (2 - k) * PLANE_BLOCKS + bx * 4 + bc * 2 + by

    window[:, pl.ds(block_at(0, x, c, y), 1)] = pairs_ref[...][:, None]
    half = heads // 2
    own_page = pl.ds(pl.multiple_of(((c * PLANES + z) * 2 + x) * page_rows, page_rows), page_rows)
    prefix[pl.ds(y * half, half), own_page, :] = pool_ref[...]
    tables[pl.ds(y, 1)] = table_ref[...][None]

    pl.semaphore_wait(
        barrier, 3 + jnp.where(z < PLANES - 1, 1, 0) + jnp.where(z > 0, 1, 0)
    )

    def message(kind, k, j, k_from, bx, bc, by, target):
        part = pl.ds(j * piece, piece)
        return pltpu.make_async_remote_copy(
            src_ref=window.at[part, block_at(k_from, bx, bc, by)],
            dst_ref=window.at[part, block_at(k, bx, bc, by)],
            send_sem=send_sem.at[kind, k, j],
            recv_sem=recv_sem.at[kind, k, j],
            device_id=target,
            device_id_type=MESH,
        )

    source = {
        KZ: (x, c, y), KX: (x, c, y), KY: (x, c, y),
        KSZ: (x, c, y), KSX: (1 - x, c, y), KSY: (x, c, 1 - y), KSD: (1 - x, c, 1 - y),
    }
    landing = {
        KZ: (x, c, y), KX: (1 - x, c, y), KY: (x, c, 1 - y), KD: (1 - x, c, 1 - y),
        KSZ: (x, 1 - c, y), KSX: (1 - x, 1 - c, y),
        KSY: (x, 1 - c, 1 - y), KSD: (1 - x, 1 - c, 1 - y),
    }
    targets = {KZ: up, KX: xn, KY: yn, KSZ: sib, KSX: sib, KSY: sib, KSD: sib}

    def x_first(j):
        return j < PIECES // 2

    def outgoing(kind, k, j):
        return message(kind, k, j, k - 1 if kind == KZ else k, *source[kind], targets[kind])

    def corner_out(k, j, by_y):
        where, target = ((1 - x, c, y), yn) if by_y else ((x, c, 1 - y), xn)
        return message(KD, k, j, k, *where, target)

    def present(k):
        return z >= k

    def takes_x(k):
        if k == 0:
            return x == 1
        return present(k) if k == 1 else present(k) & (x == 0)

    def gives_x(k):
        if k == 0:
            return x == 0
        return present(k) if k == 1 else present(k) & (x == 1)

    def sends(kind, k):
        if kind == KZ:
            return (z < PLANES - 1) & (z >= k - 1)
        if kind == KX:
            return gives_x(k)
        if kind in (KY, KSZ, KSY):
            return present(k)
        return takes_x(k)

    def receives(kind, k):
        if kind in (KX, KD, KSX, KSD):
            return takes_x(k)
        return present(k)

    def corner_sends(k, j, by_y):
        if k != 1:
            return gives_x(k)
        return takes_x(k) & x_first(j) if by_y else gives_x(k) & jnp.logical_not(x_first(j))

    started = []

    def start(kind, k, j):
        if (kind, k) not in started:
            started.append((kind, k))

        @pl.when(sends(kind, k))
        def _():
            outgoing(kind, k, j).start()

    def corner_start(k, j, by_y):
        @pl.when(corner_sends(k, j, by_y))
        def _():
            corner_out(k, j, by_y).start()

    def for_pieces(body):
        lax.fori_loop(0, PIECES, lambda j, carry: (body(j), carry)[1], 0)

    def arrived(kind, k, j):
        @pl.when(receives(kind, k))
        def _():
            message(kind, k, j, k, *landing[kind], sib).wait_recv()

    def pool_message(index, src, target):
        return pltpu.make_async_remote_copy(
            src_ref=src, dst_ref=src,
            send_sem=pool_send.at[index], recv_sem=pool_recv.at[index],
            device_id=target, device_id_type=MESH,
        )

    def layer_at(plane, layer):
        return prefix.at[
            :, pl.ds(pl.multiple_of((layer * PLANES + plane) * 2 * page_rows, 2 * page_rows), 2 * page_rows), :
        ]

    table_out = pool_message(0, tables.at[pl.ds(y, 1)], yn)
    table_in = pool_message(0, tables.at[pl.ds(1 - y, 1)], yn)
    py_out = pool_message(1, prefix.at[pl.ds(y * half, half), own_page, :], yn)
    py_in = pool_message(1, prefix.at[pl.ds((1 - y) * half, half), own_page, :], yn)
    x_page = pl.ds(pl.multiple_of(((c * PLANES + z) * 2 + 1 - x) * page_rows, page_rows), page_rows)
    px_out = pool_message(2, prefix.at[:, own_page, :], xn)
    px_in = pool_message(2, prefix.at[:, x_page, :], xn)
    UP, DOWN, SIB_UP, SIB_DOWN, SIB_OWN = 3, 6, 9, 12, 15

    def from_below(d):
        return z >= d

    def from_above(d):
        return z + d < PLANES

    def up_out(d):
        return pool_message(UP + d - 1, layer_at(z - d + 1, c), up)

    def down_out(d):
        return pool_message(DOWN + d - 1, layer_at(z + d - 1, c), down)

    def up_sends(d):
        return (z < PLANES - 1) & (z >= d - 1)

    def down_sends(d):
        return (z > 0) & (z + d - 1 < PLANES)

    def pool_start(d):
        @pl.when(up_sends(d))
        def _():
            up_out(d).start()

        @pl.when(down_sends(d))
        def _():
            down_out(d).start()

    def pool_arrived(d):
        @pl.when(from_below(d))
        def _():
            pool_message(UP + d - 1, layer_at(z - d, c), up).wait_recv()
            pool_message(SIB_UP + d - 1, layer_at(z - d, c), sib).start()

        @pl.when(from_above(d))
        def _():
            pool_message(DOWN + d - 1, layer_at(z + d, c), up).wait_recv()
            pool_message(SIB_DOWN + d - 1, layer_at(z + d, c), sib).start()

        if d < PLANES - 1:
            pool_start(d + 1)

    py_out.start()
    table_out.start()

    @for_pieces
    def _(j):
        for kind, k in ((KZ, 1), (KX, 0), (KY, 0), (KSZ, 0)):
            start(kind, k, j)

    plane_rows = PLANE_BLOCKS * rows

    @pl.when(z < 2)
    def _():
        window[:, :PLANE_BLOCKS] = jnp.zeros((heads, PLANE_BLOCKS, rows, width), window.dtype)

    @pl.when(z < 1)
    def _():
        window[:, PLANE_BLOCKS:2 * PLANE_BLOCKS] = jnp.zeros((heads, PLANE_BLOCKS, rows, width), window.dtype)

    span = bias.shape[1]
    column = lax.broadcasted_iota(jnp.int32, (rows, span), 1)
    row = lax.broadcasted_iota(jnp.int32, (rows, span), 0)
    base = (z * PLANE_BLOCKS + place) * rows - 2 * plane_rows
    seen = (column >= start_ref[...] - base) & (column <= row + 2 * plane_rows)
    bias[...] = jnp.where(seen, 0.0, -1e30)

    py_in.wait_recv()
    px_out.start()

    @for_pieces
    def _(j):
        arrived(KZ, 1, j)
        for kind, k in ((KZ, 2), (KX, 1), (KY, 1), (KSZ, 1)):
            start(kind, k, j)

    px_in.wait_recv()
    pool_start(1)
    pool_message(SIB_OWN, layer_at(z, c), sib).start()

    def cross(k, j):
        if k == 1:
            arrived(KX, k, j)
            corner_start(k, j, True)
            start(KSX, k, j)
        arrived(KY, k, j)
        corner_start(k, j, False)
        start(KSY, k, j)
        if k != 1:
            arrived(KX, k, j)
            start(KSX, k, j)

    def corner(k, j):
        arrived(KD, k, j)
        start(KSD, k, j)

    @for_pieces
    def _(j):
        cross(0, j)

    @for_pieces
    def _(j):
        arrived(KZ, 2, j)
        for kind, k in ((KX, 2), (KY, 2), (KSZ, 2)):
            start(kind, k, j)

    pool_arrived(1)

    @for_pieces
    def _(j):
        cross(1, j)
        corner(0, j)

    pool_arrived(2)

    @for_pieces
    def _(j):
        cross(2, j)
        corner(1, j)

    pool_arrived(3)

    corner(2, 0)
    corner(2, 1)

    table_in.wait_recv()
    pages = PLANES * 4
    keys = pages * page_rows
    slot = lax.broadcasted_iota(jnp.int32, (8, keys), 1) // page_rows
    page = (slot % (pages // 2)) * 2 + slot // (pages // 2)
    for side in range(2):
        table = tables[side]
        chosen = table[:, 0:1] == page
        for i in range(1, listed):
            chosen = chosen | (table[:, i:i + 1] == page)
        mask = jnp.where(chosen, 0.0, -1e30)
        for i in range(half):
            pool_bias[side * half + i] = mask[i:i + 1]

    for d in range(1, PLANES):
        @pl.when(from_below(d))
        def _():
            pool_message(SIB_UP + d - 1, layer_at(z - d, 1 - c), sib).wait_recv()

        @pl.when(from_above(d))
        def _():
            pool_message(SIB_DOWN + d - 1, layer_at(z + d, 1 - c), sib).wait_recv()
    pool_message(SIB_OWN, layer_at(z, 1 - c), sib).wait_recv()

    def from_sibling(j):
        for k in range(3):
            for kind in (KSZ, KSX, KSY, KSD):
                arrived(kind, k, j)

    from_sibling(0)

    factor = HEAD_DIM ** (-0.5) * 1.4426950408889634
    group = query_ref.shape[2] // HEAD_DIM
    contract = (((1,), (1,)), ((), ()))
    count = keys + span

    def pairs_of(h):
        near = window[h, pl.ds(place, 2 * PLANE_BLOCKS + 1)].reshape(span, width)
        return jnp.concatenate([prefix[h], near], axis=0)

    def score(h, lane):
        queries = query_ref[h]
        query = jnp.concatenate(
            [queries[:, g * HEAD_DIM:(g + 1) * HEAD_DIM] for g in range(group)], axis=0
        )
        scores[lane] = lax.dot_general(
            query, pairs_of(h)[:, :HEAD_DIM], contract, preferred_element_type=jnp.float32
        )

    def soften(h, lane):
        for r in range(0, rows, CHUNK):
            mask = bias[r:r + CHUNK, :]
            for g in range(group):
                own = slice(g * rows + r, g * rows + r + CHUNK)
                pool_scores = scores[lane, own, :keys] + pool_bias[h]
                near_scores = scores[lane, own, keys:] + mask
                top = factor * jnp.maximum(
                    jnp.max(pool_scores, axis=1, keepdims=True), jnp.max(near_scores, axis=1, keepdims=True)
                )
                weights[lane, own, :keys] = jnp.exp2(pool_scores * factor - top).astype(jnp.bfloat16)
                weights[lane, own, keys:] = jnp.exp2(near_scores * factor - top).astype(jnp.bfloat16)

    def mix(h, lane):
        values = jnp.concatenate(
            [pairs_of(h)[:, HEAD_DIM:], jnp.ones((count, HEAD_DIM), jnp.bfloat16)], axis=1
        )
        mixed = jnp.dot(weights[lane], values, preferred_element_type=jnp.float32)
        result = (mixed[:, :HEAD_DIM] / mixed[:, HEAD_DIM:]).astype(out_ref.dtype)
        for g in range(group):
            out_ref[h, :, g * HEAD_DIM:(g + 1) * HEAD_DIM] = result[g * rows:(g + 1) * rows]

    score(0, 0)

    def two_heads(i, carry):
        @pl.when(i < PIECES - 2)
        def _():
            corner(2, i + 2)

        @pl.when(i < PIECES - 1)
        def _():
            from_sibling(i + 1)

        h = 2 * i
        score(h + 1, 1)
        soften(h, 0)
        mix(h, 0)
        score(jnp.minimum(h + 2, heads - 1), 0)
        soften(h + 1, 1)
        mix(h + 1, 1)
        return carry

    lax.fori_loop(0, heads // 2, two_heads, 0)

    @for_pieces
    def _(j):
        for kind, k in started:
            @pl.when(sends(kind, k))
            def _():
                outgoing(kind, k, j).wait_send()

        for k in range(3):
            for by_y in (True, False) if k == 1 else (False,):
                @pl.when(corner_sends(k, j, by_y))
                def _():
                    corner_out(k, j, by_y).wait_send()

    table_out.wait_send()
    py_out.wait_send()
    px_out.wait_send()
    pool_message(SIB_OWN, layer_at(z, c), sib).wait_send()
    for d in range(1, PLANES):
        @pl.when(up_sends(d))
        def _():
            up_out(d).wait_send()

        @pl.when(down_sends(d))
        def _():
            down_out(d).wait_send()

        @pl.when(from_below(d))
        def _():
            pool_message(SIB_UP + d - 1, layer_at(z - d, c), sib).wait_send()

        @pl.when(from_above(d))
        def _():
            pool_message(SIB_DOWN + d - 1, layer_at(z + d, c), sib).wait_send()


def relayed(queries, branch_key_value, branch_ids, pool, page_table):
    rows, heads, width = branch_key_value.shape
    wide = queries.shape[2]
    page_rows = pool.shape[1]
    block = lax.axis_index("seq") * 2 + lax.axis_index("head")
    own_ids = lax.dynamic_slice_in_dim(branch_ids, block * rows, rows, 0)
    starts = jnp.sum((branch_ids[None, :] < own_ids[:, None]).astype(jnp.int32), axis=1, keepdims=True)
    table = jnp.pad(page_table, ((0, 8 - page_table.shape[0]), (0, 128 - page_table.shape[1])))
    span = 2 * PLANE_BLOCKS * rows + rows
    pool_keys = PLANES * 4 * page_rows
    vmem = pl.BlockSpec(memory_space=pltpu.VMEM)
    attended = pl.pallas_call(
        functools.partial(relay_kernel, page_table.shape[1]),
        out_shape=jax.ShapeDtypeStruct((heads, rows, wide), jnp.bfloat16),
        in_specs=[vmem] * 5,
        out_specs=vmem,
        scratch_shapes=[
            pltpu.VMEM((heads, 3 * PLANE_BLOCKS, rows, width), jnp.bfloat16),
            pltpu.VMEM((heads, pool_keys, width), jnp.bfloat16),
            pltpu.VMEM((2, 8, 128), jnp.int32),
            pltpu.VMEM((rows, span), jnp.float32),
            pltpu.VMEM((heads, 1, pool_keys), jnp.float32),
            pltpu.VMEM((2, rows * (wide // HEAD_DIM), pool_keys + span), jnp.float32),
            pltpu.VMEM((2, rows * (wide // HEAD_DIM), pool_keys + span), jnp.bfloat16),
            pltpu.SemaphoreType.DMA((8, 3, PIECES)),
            pltpu.SemaphoreType.DMA((8, 3, PIECES)),
            pltpu.SemaphoreType.DMA((16,)),
            pltpu.SemaphoreType.DMA((16,)),
        ],
        compiler_params=pltpu.CompilerParams(
            collective_id=0, has_side_effects=True, vmem_limit_bytes=48 * 2**20
        ),
        cost_estimate=pl.CostEstimate(
            flops=4 * rows * wide * (span + pool_keys) * heads,
            bytes_accessed=2 * 2 * heads * rows * wide,
            transcendentals=rows * heads * (wide // HEAD_DIM) * (span + pool_keys),
        ),
    )(
        jnp.swapaxes(queries, 0, 1),
        jnp.swapaxes(branch_key_value, 0, 1),
        starts,
        jnp.swapaxes(pool[0], 0, 1),
        table,
    )
    return jnp.swapaxes(attended, 0, 1)


def solution(mesh):
    small = mesh.shape["seq"] == PLANES * 4 and mesh.shape["head"] == 2
    return jax.shard_map(
        relayed if small else per_device,
        mesh=mesh,
        in_specs=(
            P(("seq", "head"), None, None),
            P(("seq", "head"), None, None),
            P(),
            P("seq", None, "head", None),
            P("head", None),
        ),
        out_specs=P(("seq", "head"), None, None),
        check_vma=False,
    )
```
